128 devices in a mesh: section: 2 (over core), dp: 64 (over x, y, z).
Axes of the slice: x: 4, y: 4, z: 4, core: 2. Of those that a mesh axis runs over, the one named last changes fastest.
Arguments:
- inputs: bfloat16 [2, 4096, 1088], P(None, 'dp'), may hold values from -6 to 6
- cotangent: bfloat16 [2, 4096, 1088], P(None, 'dp'), may hold values from -6 to 6
- lengths: int32 [2, 64, 4], P(None, 'dp'), may hold values from 1 to 32, as said below
- vectors: bfloat16 [2, 1088, 8], P('section', 'dp'), may hold values from -1.5 to 1.5, as said below
- qkv_weight: bfloat16 [2, 1088, 3264], P('section', 'dp'), may hold values from -0.1875 to 0.1875
- out_weight: bfloat16 [2, 1088, 1088], P('section', 'dp'), may hold values from -0.75 to 0.75
- up_weight: bfloat16 [2, 1088, 4352], P('section', 'dp'), may hold values from -0.1875 to 0.1875
- up_bias: bfloat16 [2, 4352], P('section', 'dp'), may hold values from -1.5 to 1.5
- down_weight: bfloat16 [2, 4352, 1088], P('section', 'dp'), may hold values from -0.09375 to 0.09375
Outputs:
- acts_out: bfloat16 [2, 2, 4096, 1088], P('section', None, 'dp')
- grad_in: bfloat16 [2, 2, 4096, 1088], P('section', None, 'dp')
- grad_vectors: float32 [2, 1088, 8], P('section', 'dp')
- grad_qkv: float32 [2, 1088, 3264], P('section', 'dp')
- grad_out: float32 [2, 1088, 1088], P('section', 'dp')
- grad_up: float32 [2, 1088, 4352], P('section', 'dp')
- grad_up_bias: float32 [2, 4352], P('section', 'dp')
- grad_down: float32 [2, 4352, 1088], P('section', 'dp')
The draws below stay inside these ranges and needn't reach their ends.
Inputs may be any that keep to these rules, and one draw needn't show every extreme that they name: The 4 lengths of each block sum to 64, and exactly one of them is 32. `vectors`: columns 0 and 5 lie in 0.6 to 1.4.
All inputs are finite; a program needn't handle non-finite values.
Results may differ from the reference program's by a relative error of at most 0.017.
Values may be sent and summed in bfloat16 or wider, within the bound.
No kernel may reach another device: no remote copies, remote signals or barrier semaphores. Data moves between devices by JAX's collectives and lax.ppermute only.
A program may use at most 192 MiB of HBM per device.

```python
import jax
import jax.numpy as jnp
from jax import lax

D = 1088
FF = 4352
HEADS = 17
HDIM = 64
MB = 2
ROWS = 64
SEQS = 4
MOST = 32
TOKENS = 4096
N_DP = 64


def draw_lengths(key, part):
    key = jax.random.fold_in(key, 7)
    remaining = ROWS - MOST

    def one_block(block_key):
        cut_key, rotation_key = jax.random.split(block_key)
        cut_points = jnp.sort(jax.random.permutation(cut_key, remaining - 1)[:SEQS - 2] + 1).astype(jnp.int32)
        edges = jnp.concatenate([jnp.zeros((1,), jnp.int32), cut_points, jnp.full((1,), remaining, jnp.int32)])
        pieces = edges[1:] - edges[:-1]
        ordered = jnp.concatenate([jnp.full((1,), MOST, jnp.int32), pieces])
        rotation = jax.random.randint(rotation_key, (), 0, SEQS)
        return jnp.roll(ordered, rotation)
    block_keys = jax.random.split(key, MB * N_DP)
    return jax.vmap(one_block)(block_keys).reshape(MB, N_DP, SEQS).astype(jnp.int32)


def draw_vectors(key, part):
    key = jax.random.fold_in(key, 11)
    gain_key, shift_key = jax.random.split(key)
    gains = jax.random.uniform(gain_key, (2, D, 8), jnp.float32, 0.6, 1.4)
    shifts = jnp.clip(0.3 * jax.random.normal(shift_key, (2, D, 8), jnp.float32), -1.5, 1.5)
    columns = jnp.arange(8, dtype=jnp.int32)
    is_gain = (columns == 0) | (columns == 5)
    return jnp.where(is_gain[None, None, :], gains, shifts).astype(jnp.bfloat16)


def block_levels(key, dims, cuts, least, top_value):
    loudness, own = 1.0, jax.random.fold_in(key, 6)
    for axis_at, blocks in cuts:
        heights = jnp.exp(jax.random.uniform(jax.random.fold_in(own, axis_at), (blocks,), jnp.float32, least / len(cuts), top_value / len(cuts)))
        loudness = loudness * jnp.repeat(heights, dims[axis_at] // blocks).reshape([-1 if axis == axis_at else 1 for axis in range(len(dims))])
    return loudness


def scatter_about(stream_key, extent, deviation, limit, cuts=(), kind=jnp.bfloat16):
    loudness = block_levels(stream_key, extent, cuts, -0.22, 0.18) if cuts else 1.0
    array = jax.random.normal(stream_key, extent, jnp.float32) * deviation * loudness
    return jnp.minimum(jnp.maximum(array, -limit), limit).astype(kind)


def setup_inputs(seed: int = 0) -> dict:
    arg_keys = jax.random.split(jax.random.key(seed), 10)
    inputs = scatter_about(arg_keys[0], (MB, TOKENS, D), 1.0, 6.0, ((1, 64),))
    cotangent = scatter_about(arg_keys[1], (MB, TOKENS, D), 1.0, 6.0, ((1, 64),))
    lengths = draw_lengths(jax.random.fold_in(arg_keys[9], 71), 0)
    vectors = draw_vectors(jax.random.fold_in(arg_keys[9], 71), 0)
    qkv_weight = scatter_about(arg_keys[4], (2, D, 3 * D), D ** -0.5, 0.1875, ((0, 2), (1, 64)))
    out_weight = scatter_about(arg_keys[5], (2, D, D), (D // 16) ** -0.5, 0.75, ((0, 2), (1, 64)))
    up_weight = scatter_about(arg_keys[6], (2, D, FF), D ** -0.5, 0.1875, ((0, 2), (1, 64)))
    up_bias = scatter_about(arg_keys[7], (2, FF), 0.3, 1.5, ((0, 2), (1, 64)))
    down_weight = scatter_about(arg_keys[8], (2, FF, D), FF ** -0.5, 0.09375, ((0, 2), (1, 64)))
    return dict(inputs=inputs, cotangent=cotangent, lengths=lengths, vectors=vectors, qkv_weight=qkv_weight, out_weight=out_weight, up_weight=up_weight, up_bias=up_bias, down_weight=down_weight)


NORM_EPSILON = 1e-05
SCORE_SCALE = 0.125
PRECISE = lax.Precision.HIGHEST

@jax.custom_vjp
def low(v):
    return lax.optimization_barrier(v.astype(jnp.bfloat16)).astype(jnp.float32)

@jax.custom_vjp
def low_back(v):
    return v

def low_keep(v):
    return (low(v), None)

def low_pass(kept, grad):
    return (grad,)

def back_keep(v):
    return (v, None)

def back_low(kept, grad):
    return (low(grad),)
low.defvjp(low_keep, low_pass)
low_back.defvjp(back_keep, back_low)

def product(left_side, right_side):
    return jnp.dot(left_side, right_side, precision=PRECISE)

def layer_norm(features, gain_vec, bias_vec):
    row_mean = lax.optimization_barrier(jnp.mean(features, axis=-1, keepdims=True))
    centred = features - row_mean
    variance = lax.optimization_barrier(jnp.mean(centred * centred, axis=-1, keepdims=True))
    return centred * lax.rsqrt(variance + NORM_EPSILON) * gain_vec + bias_vec

def segment_ids(seq_lengths):
    boundaries = jnp.cumsum(seq_lengths)
    places = jnp.arange(ROWS, dtype=jnp.int32)
    return lax.optimization_barrier(jnp.sum((places[:, None] >= boundaries[None, :]).astype(jnp.int32), axis=1))

def attend_block(operands):
    queries, keys_heads, values_heads, seq_lengths = operands
    segment = segment_ids(seq_lengths)
    places = jnp.arange(ROWS, dtype=jnp.int32)
    allowed = (segment[:, None] == segment[None, :]) & (places[:, None] >= places[None, :])
    scores = low_back(jnp.einsum('qhd,khd->hqk', queries, keys_heads, precision=PRECISE) * SCORE_SCALE)
    scores = jnp.where(allowed[None], scores, -1e+30)
    soft_weights = low(jax.nn.softmax(scores, axis=-1))
    return jnp.einsum('hqk,khd->qhd', soft_weights, values_heads, precision=PRECISE)

def layer(features, block_lengths, vectors, qkv_weight, out_weight, up_weight, up_bias, down_weight):
    entry = low(layer_norm(features, vectors[:, 0], vectors[:, 1]))
    packed = product(entry, qkv_weight)
    queries = low(low_back(packed[:, :D] + vectors[:, 2]))
    keys_rows = low(low_back(packed[:, D:2 * D]))
    values_rows = low(low_back(packed[:, 2 * D:] + vectors[:, 3]))
    blocks = block_lengths.shape[0]
    shaped = [piece_rows.reshape(blocks, ROWS, HEADS, HDIM) for piece_rows in (queries, keys_rows, values_rows)]
    mixed_heads = lax.map(jax.checkpoint(attend_block), (shaped[0], shaped[1], shaped[2], block_lengths))
    mixed_rows = low(low_back(mixed_heads.reshape(blocks * ROWS, D)))
    middle = features + low_back(product(mixed_rows, out_weight) + vectors[:, 4])
    second = low(layer_norm(middle, vectors[:, 5], vectors[:, 6]))
    hidden = low_back(product(second, up_weight) + up_bias)
    active = low(jax.nn.gelu(hidden, approximate=True))
    return middle + low_back(product(active, down_weight) + vectors[:, 7])

def reference(inputs, cotangent, lengths, vectors, qkv_weight, out_weight, up_weight, up_bias, down_weight):
    block_lengths = lengths.reshape(MB * N_DP, SEQS)
    start_rows = inputs.astype(jnp.float32).reshape(MB * TOKENS, D)
    offsets = jnp.zeros((MB * TOKENS, D), jnp.float32)
    weights = tuple((source.astype(jnp.float32) for source in (vectors, qkv_weight, out_weight, up_weight, up_bias, down_weight)))

    def forward(first_in, second_shift, param_list):
        first_params = [stacked[0] for stacked in param_list]
        second_params = [stacked[1] for stacked in param_list]
        mid_out = low(layer(low_back(first_in), block_lengths, *first_params))
        top_out = layer(low_back(mid_out + second_shift), block_lengths, *second_params)
        return (mid_out, top_out)
    (mid_out, top_out), pull_back = jax.vjp(forward, start_rows, offsets, weights)
    top_grad = cotangent.astype(jnp.float32).reshape(MB * TOKENS, D)
    grad_first, grad_second, grad_weights = pull_back((jnp.zeros_like(mid_out), top_grad))
    acts_out = jnp.stack([mid_out, top_out]).reshape(2, MB, TOKENS, D).astype(jnp.bfloat16)
    grad_in = jnp.stack([grad_first, grad_second]).reshape(2, MB, TOKENS, D).astype(jnp.bfloat16)
    return (acts_out, grad_in, grad_weights[0], grad_weights[1], grad_weights[2], grad_weights[3], grad_weights[4], grad_weights[5])
```

```python
import jax
import jax.numpy as jnp
from jax import lax
from jax.sharding import Mesh, PartitionSpec as P

HEADS = 17
HDIM = 64
D = HEADS * HDIM
FF = 4 * D
SHARD = 17
NDP = 64
MAIN = 16 * NDP
PAD = 1152
QPAD = 3328

NORM_EPSILON = 1e-05
SCORE_SCALE = 0.125
BF = jnp.bfloat16
F32 = jnp.float32

UP0 = 0
DOWN0 = FF
QKV0 = DOWN0 + 4 * PAD
OUT0 = QKV0 + QPAD
TAIL0 = OUT0 + PAD
TAILW = 896
WIDTH = TAIL0 + TAILW


def matmul(a, b):
    return jnp.dot(a, b, preferred_element_type=F32)


def dot_t(a, b):
    return lax.dot_general(a, b, (((1,), (1,)), ((), ())), preferred_element_type=F32)


def t_dot(a, b):
    return lax.dot_general(a, b, (((0,), (0,)), ((), ())), preferred_element_type=F32)


def order_matrix():
    nat = lax.broadcasted_iota(jnp.int32, (D, D), 0)
    new = lax.broadcasted_iota(jnp.int32, (D, D), 1)
    source = jnp.where(new < MAIN, (new // 16) * SHARD + new % 16, (new - MAIN) * SHARD + 16)
    return (nat == source).astype(BF)


def rows_to_order(rows):
    return jnp.concatenate([rows[:, :16].reshape(MAIN, -1), rows[:, 16]], axis=0)


def hidden_to_order(cols):
    k = cols.shape[0]
    c = cols.reshape(k, NDP, 4, SHARD).transpose(0, 2, 1, 3)
    return jnp.concatenate([c[..., :16].reshape(k, 4, MAIN), c[..., 16]], axis=2).reshape(k, FF)


def hidden_to_natural(cols):
    k = cols.shape[0]
    c = cols.reshape(k, 4, D)
    main = c[..., :MAIN].reshape(k, 4, NDP, 16)
    return jnp.concatenate([main, c[..., MAIN:, None]], axis=3).transpose(0, 2, 1, 3).reshape(k, FF)


def gelu_tanh(v):
    return jax.nn.gelu(v, approximate=True)


def norm_parts(features):
    centred = features - jnp.mean(features, axis=-1, keepdims=True)
    inverse = lax.rsqrt(jnp.mean(centred * centred, axis=-1, keepdims=True) + NORM_EPSILON)
    return centred * inverse, inverse


def norm_back(gradient, normed, inverse, gain):
    gain_grad = jnp.sum(gradient * normed, axis=0)
    bias_grad = jnp.sum(gradient, axis=0)
    scaled = gradient * gain
    centred = scaled - jnp.mean(scaled, axis=-1, keepdims=True)
    centred = centred - normed * jnp.mean(scaled * normed, axis=-1, keepdims=True)
    return inverse * centred, gain_grad, bias_grad


def mm(x, w):
    return matmul(x[:, :MAIN], w[0]) + matmul(x[:, MAIN:], w[1])


def mm_t(g, w):
    return jnp.concatenate([dot_t(g, w[0]), dot_t(g, w[1])], axis=1)


def heads_of(rows):
    return rows.reshape(rows.shape[0], HEADS, HDIM)


def soft_weights_of(q, k, allowed):
    scores = jnp.einsum("qhd,khd->hqk", q, k, preferred_element_type=F32) * SCORE_SCALE
    scores = jnp.where(allowed[None], scores, -1e30)
    e = jnp.exp(scores - jnp.max(scores, axis=-1, keepdims=True))
    return e / jnp.sum(e, axis=-1, keepdims=True)


def forward(x, allowed, order, w, vecs, bias, up_bias):
    normed1, inv1 = norm_parts(x)
    entry = (normed1 * vecs[0] + vecs[1]).astype(BF)
    packed = (mm(entry, w["qkv"]) + bias).astype(BF)
    q, k, v = (heads_of(packed[:, i * D : (i + 1) * D]) for i in range(3))
    soft = soft_weights_of(q, k, allowed)
    mixed = jnp.einsum("hqk,khd->qhd", soft.astype(BF), v, preferred_element_type=F32)
    mixed = matmul(mixed.reshape(-1, D).astype(BF), order).astype(BF)
    middle = x + mm(mixed, w["out"]) + vecs[4]
    normed2, inv2 = norm_parts(middle)
    second = (normed2 * vecs[5] + vecs[6]).astype(BF)
    hidden = mm(second, w["up"]) + up_bias
    active = gelu_tanh(hidden).astype(BF)
    branch = sum(mm(active[:, a * D : (a + 1) * D], w["down"][a]) for a in range(4))
    result = (middle + branch + vecs[7]).astype(BF)
    return result, (normed1, inv1, entry, packed, mixed, normed2, inv2, second, hidden, active)


def backward(grad, allowed, order, w, vecs, kept):
    normed1, inv1, entry, packed, mixed, normed2, inv2, second, hidden, active = kept
    dres = grad.astype(F32)
    dactive = jnp.concatenate([mm_t(grad, w["down"][a]) for a in range(4)], axis=1)
    dhidden = jax.vjp(gelu_tanh, hidden)[1](dactive)[0].astype(BF)
    dsecond = mm_t(dhidden, w["up"])
    dnorm2, dgain2, dbias2 = norm_back(dsecond, normed2, inv2, vecs[5])
    dmiddle = dres + dnorm2
    dattn = dmiddle.astype(BF)
    dmixed = dot_t(mm_t(dattn, w["out"]).astype(BF), order).astype(BF)
    q, k, v = (heads_of(packed[:, i * D : (i + 1) * D]) for i in range(3))
    soft = soft_weights_of(q, k, allowed)
    dm = heads_of(dmixed)
    dsoft = jnp.einsum("qhd,khd->hqk", dm, v, preferred_element_type=F32)
    dscores = (soft * (dsoft - jnp.sum(dsoft * soft, axis=-1, keepdims=True))).astype(BF)
    dv = jnp.einsum("hqk,qhd->khd", soft.astype(BF), dm, preferred_element_type=F32)
    dq = jnp.einsum("hqk,khd->qhd", dscores, k, preferred_element_type=F32) * SCORE_SCALE
    dk = jnp.einsum("hqk,qhd->khd", dscores, q, preferred_element_type=F32) * SCORE_SCALE
    dpacked = jnp.concatenate([p.reshape(-1, D).astype(BF) for p in (dq, dk, dv)], axis=1)
    dentry = mm_t(dpacked, w["qkv"])
    dnorm1, dgain1, dbias1 = norm_back(dentry, normed1, inv1, vecs[0])
    dx = (dmiddle + dnorm1).astype(BF)

    def total(v):
        return jnp.sum(v.astype(F32), axis=0)

    dbias_qv = jnp.stack([total(dpacked[:, :D]), total(dpacked[:, 2 * D :])]).astype(BF)
    dbias_qv = matmul(dbias_qv, order)
    small = jnp.concatenate(
        [
            jnp.stack([dgain1, dbias1]),
            dbias_qv,
            jnp.stack([total(dattn), dgain2, dbias2, total(grad)]),
            total(dhidden).reshape(4, D),
        ],
        axis=0,
    )
    return dx, (dhidden, dattn, dpacked, grad, small)


def pad_cols(v, width):
    return jnp.pad(v, ((0, 0), (0, width - v.shape[1])))


def body(inputs, cotangent, lengths, vectors, qkv_w, out_w, up_w, up_b, down_w):
    section = lax.axis_index("section")
    zi = lax.axis_index("z")
    mb, rows, _ = inputs.shape
    n = mb * rows
    order = order_matrix()

    outdown = matmul(jnp.concatenate([out_w[0], down_w[0]], axis=0), order).astype(BF)
    shard = [hidden_to_order(up_w[0])]
    shard += [pad_cols(outdown[SHARD * (1 + a) : SHARD * (2 + a)], PAD) for a in range(4)]
    shard += [pad_cols(qkv_w[0], QPAD), pad_cols(outdown[:SHARD], PAD)]
    shard = jnp.concatenate(shard, axis=1)
    tail = jnp.concatenate([shard[16], vectors[0].reshape(-1), up_b[0]])
    tail = jnp.pad(tail, (0, 16 * TAILW - tail.shape[0])).reshape(16, TAILW)
    sent = jnp.concatenate([shard[:16], tail], axis=1)
    whole = lax.all_gather(sent, ("x", "y", "z"), axis=0, tiled=True)
    tails = whole[:, TAIL0:].reshape(NDP, 16 * TAILW)
    vec_all = tails[:, TAIL0 : TAIL0 + SHARD * 8].reshape(NDP, SHARD, 8).astype(F32)
    upb_all = tails[:, TAIL0 + SHARD * 8 : TAIL0 + SHARD * 12].reshape(NDP, 4, SHARD).astype(F32)

    def weight(start, width):
        return whole[:, start : start + width], tails[:, start : start + width]

    w = {
        "up": weight(UP0, FF),
        "down": [weight(DOWN0 + a * PAD, D) for a in range(4)],
        "qkv": weight(QKV0, 3 * D),
        "out": weight(OUT0, D),
    }
    vecs = rows_to_order(vec_all).T
    vec_nat = vec_all.reshape(D, 8)
    bias = jnp.concatenate([vec_nat[:, 2], jnp.zeros((D,), F32), vec_nat[:, 3]])
    up_bias = rows_to_order(upb_all.transpose(0, 2, 1)).T.reshape(FF)

    ends = jnp.cumsum(lengths[:, 0], axis=1)
    place = jnp.arange(rows, dtype=jnp.int32)
    seg = jnp.sum((place[None, :, None] >= ends[:, None, :]).astype(jnp.int32), axis=2)
    seg = (seg + 8 * jnp.arange(mb, dtype=jnp.int32)[:, None]).reshape(n)
    at = jnp.arange(n, dtype=jnp.int32)
    allowed = (seg[:, None] == seg[None, :]) & (at[:, None] >= at[None, :])

    x0 = matmul(inputs.reshape(n, D), order).astype(BF)
    cot = matmul(cotangent.reshape(n, D), order).astype(BF)

    def fwd(x):
        return forward(x.astype(F32), allowed, order, w, vecs, bias, up_bias)

    def bwd(grad, kept):
        return backward(grad, allowed, order, w, vecs, kept)

    def zeros_like_tree(t):
        return jax.tree.map(lambda s: jnp.zeros(s.shape, s.dtype), t)

    fwd_shape = jax.eval_shape(fwd, x0)
    bwd_shape = jax.eval_shape(bwd, cot, fwd_shape[1])
    first = lax.cond(section == 0, fwd, lambda x: zeros_like_tree(fwd_shape), x0)
    arrived = lax.ppermute(first[0], "section", [(0, 1)])

    def top(x, first):
        res, kept = fwd(x)
        dx, factors = bwd(cot, kept)
        return res, kept, dx, factors

    def keep(x, first):
        return first[0], first[1], *zeros_like_tree(bwd_shape)

    result, kept, dx, factors = lax.cond(section == 1, top, keep, arrived, first)
    coming = lax.ppermute(dx, "section", [(1, 0)])
    dx, factors = lax.cond(
        section == 0,
        lambda g, old: bwd(g, kept),
        lambda g, old: old,
        coming,
        (dx, factors),
    )

    entry, mixed, second, active = kept[2], kept[4], kept[7], kept[9]
    dhidden, dattn, dpacked, dbranch, small = factors
    blocks = jnp.stack(
        [
            jnp.stack([entry, entry, entry, mixed]),
            jnp.stack([dpacked[:, :D], dpacked[:, D : 2 * D], dpacked[:, 2 * D :], dattn]),
            active.reshape(n, 4, D).transpose(1, 0, 2),
            dhidden.reshape(n, 4, D).transpose(1, 0, 2),
        ]
    )

    def for_z(target):
        own = lax.dynamic_index_in_dim(blocks, target, 1, keepdims=False)
        return jnp.concatenate([own, second[None], dbranch[None]], axis=0)

    parts = [for_z(zi)]
    for d in (1, 2, 3):
        parts.append(
            lax.ppermute(for_z((zi + d) % 4), "z", [(i, (i + d) % 4) for i in range(4)])
        )
    a_attn, b_attn, act_z, dhid_z, sec_all, db_all = jnp.concatenate(parts, axis=1)
    pairs = ((sec_all, dhid_z), (act_z, db_all), (a_attn, b_attn))

    main = jnp.concatenate([t_dot(a[:, :MAIN], b).astype(BF) for a, b in pairs], axis=1)
    last = jnp.concatenate([t_dot(a[:, MAIN:], b).astype(BF) for a, b in pairs], axis=1)
    small_t = pad_cols(small.T.astype(BF), QPAD - 3 * D)
    main = jnp.concatenate([main, small_t[:MAIN]], axis=1).reshape(16, 64, QPAD)
    last = jnp.concatenate([last, small_t[MAIN:]], axis=1).reshape(16, 4, QPAD)
    payload = jnp.concatenate([main, last, jnp.zeros((16, 4, QPAD), BF)], axis=1)
    got = lax.psum_scatter(
        payload.reshape(16 * 72, QPAD), ("x", "y"), scatter_dimension=0, tiled=True
    )
    to_z = jnp.concatenate(
        [got[:64].reshape(4, 16, QPAD), got[64:68].reshape(4, 1, QPAD), jnp.zeros((4, 7, QPAD), BF)],
        axis=1,
    )
    mine = lax.all_to_all(to_z, "z", 0, 0, tiled=True)[:, :SHARD]

    g_up = hidden_to_natural(mine[:, :, :D].transpose(1, 0, 2).reshape(SHARD, FF)).astype(F32)
    cols = jnp.concatenate(
        [mine[:, :, D : 2 * D].reshape(4 * SHARD, D), mine[3, :, 2 * D : 3 * D]], axis=0
    )
    cols = dot_t(cols, order)
    g_qkv = mine[:3, :, 2 * D : 3 * D].transpose(1, 0, 2).reshape(SHARD, 3 * D).astype(F32)
    sums = jnp.sum(mine[:, :, 3 * D : 3 * D + 12].astype(F32), axis=0)
    back = dot_t(jnp.concatenate([result, dx], axis=0), order).astype(BF)
    acts = back[:n].reshape(1, mb, rows, D)
    grads = back[n:].reshape(1, mb, rows, D)
    return (
        acts,
        grads,
        sums[None, :, :8],
        g_qkv[None],
        cols[None, 4 * SHARD :],
        g_up[None],
        sums[:, 8:].T.reshape(1, 4 * SHARD),
        cols[None, : 4 * SHARD],
    )


def solution(mesh):
    grid = Mesh(mesh.devices.reshape(2, 4, 4, 4), ("section", "x", "y", "z"))
    dp = ("x", "y", "z")
    tokens = P(None, dp, None)
    rows = P("section", dp, None)
    in_specs = (tokens, tokens, tokens, rows, rows, rows, rows, P("section", dp), rows)
    stacked = P("section", None, dp, None)
    out_specs = (stacked, stacked, rows, rows, rows, rows, P("section", dp), rows)
    return jax.shard_map(body, mesh=grid, in_specs=in_specs, out_specs=out_specs, check_vma=False)
```

```python
import functools

import jax
import jax.numpy as jnp
import numpy as np
from jax import lax
from jax.experimental import pallas as pl
from jax.experimental.pallas import tpu as pltpu
from jax.sharding import Mesh, PartitionSpec as P

HEADS = 17
HDIM = 64
D = HEADS * HDIM
FF = 4 * D
SHARD = 17
NDP = 64
MAIN = 16 * NDP
PAD = 1152
ROWS = 128
PAIRS = PAD // 128

UP, DOWN, QKV, OUT, BLOCKS = 0, 4, 8, 11, 12
TAIL0 = BLOCKS * PAD
TAILW = 896
WIDTH = TAIL0 + TAILW
SMALLS = 256

NORM_EPSILON = 1e-05
SCORE_SCALE = 0.125
GELU_C = float(np.sqrt(2 / np.pi))
GELU_A = 0.044715
BF = jnp.bfloat16
F32 = jnp.float32
VMEM_BYTES = 58 * 1024 * 1024


def constants():
    n = np.arange(D)
    shard_of = np.where(n < MAIN, n // 16, n - MAIN)
    row_of = np.where(n < MAIN, n % 16, 16)
    order = np.zeros((PAD, D), np.float32)
    order[shard_of * SHARD + row_of, n] = 1
    f = np.arange(D)
    s, a, r = f // 68, (f % 68) // SHARD, f % SHARD
    hid = np.zeros((D, D), np.float32)
    hid[f, np.where(r < 16, a * 256 + s * 16 + r, 1024 + a * 16 + s)] = 1
    k = np.arange(SMALLS)
    is_vec, is_up = k < 136, (k >= 136) & (k < 204)
    k_row = np.where(is_vec, k // 8, np.where(is_up, (k - 136) % SHARD, -1))
    k_out = np.where(is_vec, k % 8, np.where(is_up, 8 + (k - 136) // SHARD, -1))
    pick = (k_out[None, :] == np.arange(16)[:, None]).astype(np.float32)
    spread = (np.arange(NDP)[:, None] == shard_of[None, :]).astype(np.float32)
    keep = (k_row[:, None] == row_of[None, :]).astype(np.float32)
    nat = np.arange(PAD)
    spread_nat = (np.arange(NDP)[:, None] == nat[None, :] // SHARD).astype(np.float32)
    keep_nat = (k_row[:, None] == nat[None, :] % SHARD).astype(np.float32)
    m = np.arange(MAIN)
    turn = np.zeros((MAIN, MAIN), np.float32)
    turn[(m % 16) * NDP + m // 16, m] = 1
    names = ("order", "hid", "pick", "spread", "keep", "spread_nat", "keep_nat", "turn")
    values = (order, hid, pick, spread, keep, spread_nat, keep_nat, turn)
    return {name: jnp.asarray(value, BF) for name, value in zip(names, values)}


def matmul(a, b):
    return jnp.dot(a, b, preferred_element_type=F32)


def dot_t(a, b):
    return lax.dot_general(a, b, (((1,), (1,)), ((), ())), preferred_element_type=F32)


def t_dot(a, b):
    return lax.dot_general(a, b, (((0,), (0,)), ((), ())), preferred_element_type=F32)


def norm_parts(features):
    centred = features - jnp.mean(features, axis=-1, keepdims=True)
    inverse = lax.rsqrt(jnp.mean(centred * centred, axis=-1, keepdims=True) + NORM_EPSILON)
    return centred * inverse, inverse


def norm_back(gradient, normed, inverse, gain):
    scaled = gradient * gain
    centred = scaled - jnp.mean(scaled, axis=-1, keepdims=True)
    return inverse * (centred - normed * jnp.mean(scaled * normed, axis=-1, keepdims=True))


def col_sum(v):
    return jnp.sum(v, axis=0, keepdims=True)


def unpack_kernel(whole, pick, spread, keep, spread_nat, keep_nat, turn, tails, vecs, nat, raw, sem):
    copy = pltpu.make_async_copy(whole.at[:, pl.ds(TAIL0, TAILW)], raw, sem)
    copy.start()
    copy.wait()
    turned = matmul(turn[...], raw[...]).astype(BF)
    for j in range(16):
        tails[:, j * TAILW : (j + 1) * TAILW] = turned[j * NDP : (j + 1) * NDP]
    small = tails[:, TAIL0 : TAIL0 + SMALLS]
    for out, s, k in ((vecs, spread, keep), (nat, spread_nat, keep_nat)):
        wide = t_dot(small, s[...]) * k[...].astype(F32)
        out[...] = matmul(pick[...], wide.astype(BF))


def unpack(whole, c):
    vm = pl.BlockSpec(memory_space=pltpu.VMEM)
    return pl.pallas_call(
        unpack_kernel,
        in_specs=[pl.BlockSpec(memory_space=pl.ANY)] + [vm] * 6,
        out_specs=[vm] * 3,
        out_shape=[
            jax.ShapeDtypeStruct((NDP, 16 * TAILW), BF),
            jax.ShapeDtypeStruct((16, D), F32),
            jax.ShapeDtypeStruct((16, PAD), F32),
        ],
        scratch_shapes=[pltpu.VMEM((MAIN, TAILW), BF), pltpu.SemaphoreType.DMA],
        compiler_params=pltpu.CompilerParams(vmem_limit_bytes=VMEM_BYTES),
        name="unpack",
    )(whole, c["pick"], c["spread"], c["keep"], c["spread_nat"], c["keep_nat"], c["turn"])


class Weights:
    def __init__(self, whole, tails, buf, sems):
        self.whole, self.tails, self.buf, self.sems = whole, tails, buf, sems

    def copies(self, b):
        cols = pl.ds(b * PAD, PAD)
        return (
            pltpu.make_async_copy(
                self.whole.at[:, cols], self.buf.at[b, pl.ds(0, MAIN)], self.sems.at[b, 0]
            ),
            pltpu.make_async_copy(
                self.tails.at[:, cols], self.buf.at[b, pl.ds(MAIN, NDP)], self.sems.at[b, 1]
            ),
        )

    def start(self, blocks):
        for b in blocks:
            for copy in self.copies(b):
                copy.start()

    def wait(self, b):
        for copy in self.copies(b):
            copy.wait()


def pair_masks():
    lane = lax.broadcasted_iota(jnp.int32, (ROWS, 128), 1)
    first = (lane < HDIM).astype(F32)
    return first, 1.0 - first


def stacked(v, masks):
    return jnp.concatenate([(v * m).astype(BF) for m in masks], axis=0)


def soft_pair(q, kk, allowed):
    scores = dot_t(q, kk) * SCORE_SCALE
    halves = []
    for h in range(2):
        s = jnp.where(allowed, scores[:, h * ROWS : (h + 1) * ROWS], -1e30)
        e = jnp.exp(s - jnp.max(s, axis=-1, keepdims=True))
        halves.append(e / jnp.sum(e, axis=-1, keepdims=True))
    return halves


def forward_part(w, wait, x_ref, pairs_ref, vecs, nat, order, r):
    x = x_ref[...].astype(F32)
    normed, _ = norm_parts(x)
    r["entry"][...] = (normed * vecs[0:1] + vecs[1:2]).astype(BF)

    def project(i, carry):
        if wait:
            w.wait(QKV + i)
        shift = jnp.where(i == 0, nat[2:3], jnp.where(i == 2, nat[3:4], 0.0))
        r["packed"][i] = (matmul(r["entry"][...], w.buf[QKV + i]) + shift).astype(BF)
        return carry

    lax.fori_loop(0, 3, project, 0)
    masks = pair_masks()
    allowed = pairs_ref[...] > 0
    for p in range(PAIRS):
        cols = pl.ds(p * 128, 128)
        kk = stacked(r["packed"][1, :, cols].astype(F32), masks)
        vv = stacked(r["packed"][2, :, cols].astype(F32), masks)
        halves = soft_pair(r["packed"][0, :, cols], kk, allowed)
        soft = jnp.concatenate([h.astype(BF) for h in halves], axis=1)
        r["heads"][:, cols] = matmul(soft, vv).astype(BF)
    r["mixed"][...] = matmul(r["heads"][...], order[...]).astype(BF)
    if wait:
        w.wait(OUT)
    branch = matmul(r["mixed"][...], w.buf[OUT])[:, :D]
    middle = x + branch + vecs[4:5]
    r["middle"][...] = middle
    normed, _ = norm_parts(middle)
    r["second"][...] = (normed * vecs[5:6] + vecs[6:7]).astype(BF)
    r["acc"][...] = jnp.zeros((ROWS, PAD), F32)

    def feed(a, carry):
        if wait:
            w.wait(UP + a)
        hidden = matmul(r["second"][...], w.buf[UP + a])[:, :D] + vecs[pl.ds(8 + a, 1)]
        r["hidden"][a] = hidden
        bent = jnp.tanh(GELU_C * (hidden + GELU_A * (hidden * hidden * hidden)))
        r["active"][a] = (0.5 * hidden * (1.0 + bent)).astype(BF)
        if wait:
            w.wait(DOWN + a)
        r["acc"][...] += matmul(r["active"][a], w.buf[DOWN + a])
        return carry

    lax.fori_loop(0, 4, feed, 0)
    r["result"][...] = (r["middle"][...] + r["acc"][:, :D] + vecs[7:8]).astype(BF)


def backward_part(w, wait, grad_ref, x_ref, pairs_ref, vecs, order, r):
    grad = grad_ref[...]
    dres = grad.astype(F32)
    r["acc"][...] = jnp.zeros((ROWS, PAD), F32)

    def feed(a, carry):
        if wait:
            w.wait(DOWN + a)
        dactive = dot_t(grad_ref[...], w.buf[DOWN + a, :, :D])
        h = r["hidden"][a]
        square = h * h
        bent = jnp.tanh(GELU_C * (h + GELU_A * (square * h)))
        slope = 0.5 * (1.0 + bent) + (0.5 * GELU_C) * h * (1.0 - bent * bent) * (
            1.0 + (3 * GELU_A) * square
        )
        dhidden = (dactive * slope).astype(BF)
        r["dhidden"][a] = dhidden
        r["small"][pl.ds(8 + a, 1)] = col_sum(dhidden.astype(F32))
        if wait:
            w.wait(UP + a)
        r["acc"][:, :D] += dot_t(dhidden, w.buf[UP + a, :, :D])
        return carry

    lax.fori_loop(0, 4, feed, 0)
    dsecond = r["acc"][:, :D]
    normed, inverse = norm_parts(r["middle"][...])
    r["small"][5:6] = col_sum(dsecond * normed)
    r["small"][6:7] = col_sum(dsecond)
    r["small"][7:8] = col_sum(dres)
    dmiddle = dres + norm_back(dsecond, normed, inverse, vecs[5:6])
    r["middle"][...] = dmiddle
    dattn = dmiddle.astype(BF)
    r["dpacked"][3] = dattn
    r["small"][4:5] = col_sum(dattn.astype(F32))
    if wait:
        w.wait(OUT)
    dmixed = dot_t(dattn, w.buf[OUT, :, :D]).astype(BF)
    r["heads"][...] = dot_t(dmixed, order[...]).astype(BF)
    masks = pair_masks()
    allowed = pairs_ref[...] > 0
    for p in range(PAIRS):
        cols = pl.ds(p * 128, 128)
        width = min(D - p * 128, 128)
        live = pl.ds(p * 128, width)
        q = r["packed"][0, :, cols]
        kk = stacked(r["packed"][1, :, cols].astype(F32), masks)
        vv = stacked(r["packed"][2, :, cols].astype(F32), masks)
        dm = r["heads"][:, cols]
        halves = soft_pair(q, kk, allowed)
        dsoft = dot_t(dm, vv)
        dscores = []
        for h, p_half in enumerate(halves):
            d_half = dsoft[:, h * ROWS : (h + 1) * ROWS]
            centre = jnp.sum(d_half * p_half, axis=-1, keepdims=True)
            dscores.append((p_half * (d_half - centre)).astype(BF))
        ds = jnp.concatenate(dscores, axis=1)
        soft = jnp.concatenate([h.astype(BF) for h in halves], axis=1)
        dq = matmul(ds, kk) * SCORE_SCALE
        dk = t_dot(ds, q) * SCORE_SCALE
        dv = t_dot(soft, dm)
        dk = dk[:ROWS] * masks[0] + dk[ROWS:] * masks[1]
        dv = dv[:ROWS] * masks[0] + dv[ROWS:] * masks[1]
        for i, v in enumerate((dq, dk, dv)):
            r["dpacked"][i, :, live] = v[:, :width].astype(BF)
    sums = [col_sum(r["dpacked"][i].astype(F32)) for i in (0, 2)]
    sums = jnp.concatenate(sums + [jnp.zeros((14, D), F32)], axis=0).astype(BF)
    r["small"][2:4] = matmul(sums, order[:D])[:2]
    r["acc"][...] = jnp.zeros((ROWS, PAD), F32)

    def project(i, carry):
        if wait:
            w.wait(QKV + i)
        r["acc"][:, :D] += dot_t(r["dpacked"][i], w.buf[QKV + i, :, :D])
        return carry

    lax.fori_loop(0, 3, project, 0)
    dentry = r["acc"][:, :D]
    normed, inverse = norm_parts(x_ref[...].astype(F32))
    r["small"][0:1] = col_sum(dentry * normed)
    r["small"][1:2] = col_sum(dentry)
    r["small"][12:16] = jnp.zeros((4, D), F32)
    r["dx"][...] = (r["middle"][...] + norm_back(dentry, normed, inverse, vecs[0:1])).astype(BF)


ROW = (ROWS, D)
KEPT = {
    "packed": ((3, ROWS, PAD), BF),
    "middle": (ROW, F32),
    "hidden": ((4,) + ROW, F32),
}
FWD_OUT = {
    "result": (ROW, BF),
    "entry": (ROW, BF),
    "mixed": (ROW, BF),
    "second": (ROW, BF),
    "active": ((4,) + ROW, BF),
}
BWD_OUT = {
    "dx": (ROW, BF),
    "dhidden": ((4,) + ROW, BF),
    "dpacked": ((4,) + ROW, BF),
    "small": ((16, D), F32),
}
WORK = {"heads": ((ROWS, PAD), BF), "acc": ((ROWS, PAD), F32)}


def layer_call(kind, whole, tails, vecs, nat, pairs, order, x, grad=None, kept=None):
    outs = dict(FWD_OUT) if kind != "bwd" else {}
    if kind == "fwd":
        outs.update(KEPT)
    else:
        outs.update(BWD_OUT)
    work = dict(WORK)
    if kind == "both":
        work.update(KEPT)
    if kind == "bwd":
        work["middle"] = KEPT["middle"]
    ins = [whole, tails, vecs, nat, pairs, order, x]
    if grad is not None:
        ins.append(grad)
    if kind == "bwd":
        ins += [kept["packed"], kept["middle"], kept["hidden"]]

    def kernel(*refs):
        given, refs = refs[: len(ins)], refs[len(ins) :]
        out_refs, refs = refs[: len(outs)], refs[len(outs) :]
        r = dict(zip(outs, out_refs))
        r.update(zip(work, refs))
        buf, sems = refs[len(work) :]
        w = Weights(given[0], given[1], buf, sems)
        vecs_ref, nat_ref, pairs_ref, order_ref, x_ref = given[2:7]
        if kind == "bwd":
            blocks = [b for a in range(4) for b in (DOWN + a, UP + a)] + [OUT, 8, 9, 10]
            w.start(blocks)
            r["packed"], r["hidden"] = given[8], given[10]
            r["middle"][...] = given[9][...]
            backward_part(w, True, given[7], x_ref, pairs_ref, vecs_ref, order_ref, r)
            return
        w.start([8, 9, 10, OUT] + [b for a in range(4) for b in (UP + a, DOWN + a)])
        forward_part(w, True, x_ref, pairs_ref, vecs_ref, nat_ref, order_ref, r)
        if kind == "both":
            backward_part(w, False, given[7], x_ref, pairs_ref, vecs_ref, order_ref, r)

    vm = pl.BlockSpec(memory_space=pltpu.VMEM)
    hbm = pl.BlockSpec(memory_space=pl.ANY)
    results = pl.pallas_call(
        kernel,
        in_specs=[hbm, hbm] + [vm] * (len(ins) - 2),
        out_specs=[vm] * len(outs),
        out_shape=[jax.ShapeDtypeStruct(s, t) for s, t in outs.values()],
        scratch_shapes=[pltpu.VMEM(s, t) for s, t in work.values()]
        + [pltpu.VMEM((BLOCKS, D, PAD), BF), pltpu.SemaphoreType.DMA((BLOCKS, 2))],
        compiler_params=pltpu.CompilerParams(vmem_limit_bytes=VMEM_BYTES),
        name="layer_" + kind,
    )(*ins)
    return dict(zip(outs, results))


def zeros_of(spec):
    return {name: jnp.zeros(s, t) for name, (s, t) in spec.items()}


def pad_cols(v, width):
    return jnp.pad(v, ((0, 0), (0, width - v.shape[1])))


def body(inputs, cotangent, lengths, vectors, qkv_w, out_w, up_w, up_b, down_w):
    section = lax.axis_index("section")
    zi = lax.axis_index("z")
    mb, rows, _ = inputs.shape
    n = mb * rows
    c = constants()
    order = c["order"]

    outdown = matmul(jnp.concatenate([out_w[0], down_w[0]], axis=0), order[:D]).astype(BF)
    hid = matmul(up_w[0].reshape(SHARD * 4, D), c["hid"]).astype(BF).reshape(SHARD, 4, D)
    hid_main = hid[:, :, :MAIN].reshape(SHARD, 4, 4, 256).transpose(0, 2, 1, 3)
    hid_last = hid[:, :, MAIN:].reshape(SHARD, 4, 4, 16).transpose(0, 2, 1, 3)
    hid = jnp.concatenate(
        [
            hid_main.reshape(SHARD, 4, MAIN),
            hid_last.reshape(SHARD, 4, NDP),
            jnp.zeros((SHARD, 4, PAD - D), BF),
        ],
        axis=2,
    )
    shard = [hid.reshape(SHARD, 4 * PAD)]
    shard += [pad_cols(outdown[SHARD * (1 + a) : SHARD * (2 + a)], PAD) for a in range(4)]
    shard += [pad_cols(qkv_w[0][:, i * D : (i + 1) * D], PAD) for i in range(3)]
    shard += [pad_cols(outdown[:SHARD], PAD)]
    shard = jnp.concatenate(shard, axis=1)
    tail = jnp.concatenate([shard[16], vectors[0].reshape(-1), up_b[0]])
    tail = jnp.pad(tail, (0, 16 * TAILW - tail.shape[0])).reshape(16, TAILW)
    sent = jnp.concatenate([shard[:16], tail], axis=1)
    whole = lax.all_gather(sent, ("x", "y", "z"), axis=0, tiled=True)
    tails, vecs, nat = unpack(whole, c)

    ends = jnp.cumsum(lengths[:, 0], axis=1)
    place = jnp.arange(rows, dtype=jnp.int32)
    seg = jnp.sum((place[None, :, None] >= ends[:, None, :]).astype(jnp.int32), axis=2)
    seg = (seg + 8 * jnp.arange(mb, dtype=jnp.int32)[:, None]).reshape(n)
    at = jnp.arange(n, dtype=jnp.int32)
    pairs = ((seg[:, None] == seg[None, :]) & (at[:, None] >= at[None, :])).astype(F32)

    x0 = matmul(inputs.reshape(n, D), order[:D]).astype(BF)
    cot = matmul(cotangent.reshape(n, D), order[:D]).astype(BF)
    call = functools.partial(
        layer_call, whole=whole, tails=tails, vecs=vecs, nat=nat, pairs=pairs, order=order
    )

    first = lax.cond(
        section == 0,
        lambda: call("fwd", x=x0),
        lambda: zeros_of({**FWD_OUT, **KEPT}),
    )
    arrived = lax.ppermute(first["result"], "section", [(0, 1)])
    kept = {k: first[k] for k in KEPT}
    fwd = {k: first[k] for k in FWD_OUT}

    def top():
        out = call("both", x=arrived, grad=cot)
        return {k: out[k] for k in FWD_OUT}, {k: out[k] for k in BWD_OUT}

    fwd, bwd = lax.cond(section == 1, top, lambda: (fwd, zeros_of(BWD_OUT)))
    coming = lax.ppermute(bwd["dx"], "section", [(1, 0)])
    bwd = lax.cond(
        section == 0, lambda: call("bwd", x=x0, grad=coming, kept=kept), lambda: bwd
    )
    dbranch = jnp.where(section == 0, coming, cot)

    entry = fwd["entry"]
    blocks = jnp.stack(
        [
            jnp.stack([entry, entry, entry, fwd["mixed"]]),
            bwd["dpacked"],
            fwd["active"],
            bwd["dhidden"],
        ]
    )

    def for_z(target):
        own = lax.dynamic_index_in_dim(blocks, target, 1, keepdims=False)
        return jnp.concatenate([own, fwd["second"][None], dbranch[None]], axis=0)

    parts = [for_z(zi)]
    for d in (1, 2, 3):
        parts.append(
            lax.ppermute(for_z((zi + d) % 4), "z", [(i, (i + d) % 4) for i in range(4)])
        )
    a_attn, b_attn, act_z, dhid_z, sec_all, db_all = jnp.concatenate(parts, axis=1)
    wgrads = ((sec_all, dhid_z), (act_z, db_all), (a_attn, b_attn))
    wide = 3 * D + 64

    main = jnp.concatenate([t_dot(a[:, :MAIN], b).astype(BF) for a, b in wgrads], axis=1)
    last = jnp.concatenate([t_dot(a[:, MAIN:], b).astype(BF) for a, b in wgrads], axis=1)
    small = pad_cols(bwd["small"].T.astype(BF), 64)
    main = jnp.concatenate([main, small[:MAIN]], axis=1).reshape(16, 64, wide)
    last = jnp.concatenate([last, small[MAIN:]], axis=1).reshape(16, 4, wide)
    payload = jnp.concatenate([main, last, jnp.zeros((16, 4, wide), BF)], axis=1)
    payload = lax.optimization_barrier(payload.reshape(16 * 72, wide))
    got = lax.psum_scatter(payload, ("x", "y"), scatter_dimension=0, tiled=True)
    got = lax.optimization_barrier(got)
    to_z = jnp.concatenate(
        [got[:64].reshape(4, 16, wide), got[64:68].reshape(4, 1, wide), jnp.zeros((4, 7, wide), BF)],
        axis=1,
    )
    mine = lax.all_to_all(to_z, "z", 0, 0, tiled=True)[:, :SHARD]

    g_hid = mine[:, :, :D].transpose(1, 0, 2)
    g_main = g_hid[:, :, :MAIN].reshape(SHARD, 4, 4, 256).transpose(0, 2, 1, 3)
    g_last = g_hid[:, :, MAIN:].reshape(SHARD, 4, 4, 16).transpose(0, 2, 1, 3)
    g_hid = jnp.concatenate(
        [g_main.reshape(SHARD, 4, MAIN), g_last.reshape(SHARD, 4, NDP)], axis=2
    )
    g_up = dot_t(g_hid.reshape(SHARD * 4, D), c["hid"]).reshape(SHARD, FF)
    cols = jnp.concatenate(
        [mine[:, :, D : 2 * D].reshape(4 * SHARD, D), mine[3, :, 2 * D : 3 * D]], axis=0
    )
    cols = dot_t(cols, order[:D])
    g_qkv = mine[:3, :, 2 * D : 3 * D].transpose(1, 0, 2).reshape(SHARD, 3 * D).astype(F32)
    sums = jnp.sum(mine[:, :, 3 * D : 3 * D + 12].astype(F32), axis=0)
    back = dot_t(jnp.concatenate([fwd["result"], bwd["dx"]], axis=0), order[:D]).astype(BF)
    return (
        back[:n].reshape(1, mb, rows, D),
        back[n:].reshape(1, mb, rows, D),
        sums[None, :, :8],
        g_qkv[None],
        cols[None, 4 * SHARD :],
        g_up[None],
        sums[:, 8:].T.reshape(1, 4 * SHARD),
        cols[None, : 4 * SHARD],
    )


def solution(mesh):
    grid = Mesh(mesh.devices.reshape(2, 4, 4, 4), ("section", "x", "y", "z"))
    dp = ("x", "y", "z")
    tokens = P(None, dp, None)
    rows = P("section", dp, None)
    in_specs = (tokens, tokens, tokens, rows, rows, rows, rows, P("section", dp), rows)
    stacks = P("section", None, dp, None)
    out_specs = (stacks, stacks, rows, rows, rows, rows, P("section", dp), rows)
    return jax.shard_map(body, mesh=grid, in_specs=in_specs, out_specs=out_specs, check_vma=False)
```

```python
import functools

import jax
import jax.numpy as jnp
import numpy as np
from jax import lax
from jax.experimental import pallas as pl
from jax.experimental.pallas import tpu as pltpu
from jax.sharding import Mesh, PartitionSpec as P

HEADS = 17
HDIM = 64
D = HEADS * HDIM
FF = 4 * D
SHARD = 17
NDP = 64
MAIN = 16 * NDP
PAD = 1152
ROWS = 128
PAIRS = PAD // 128

UP, DOWN, QKV, OUT, BLOCKS = 0, 4, 8, 11, 12
TAIL0 = BLOCKS * PAD
TAILW = 896
WIDTH = TAIL0 + TAILW
SMALLS = 256

NORM_EPSILON = 1e-05
SCORE_SCALE = 0.125
GELU_C = float(np.sqrt(2 / np.pi))
GELU_A = 0.044715
BF = jnp.bfloat16
F32 = jnp.float32
VMEM_BYTES = 58 * 1024 * 1024


def constants():
    n = np.arange(D)
    shard_of = np.where(n < MAIN, n // 16, n - MAIN)
    row_of = np.where(n < MAIN, n % 16, 16)
    order = np.zeros((PAD, D), np.float32)
    order[shard_of * SHARD + row_of, n] = 1
    f = np.arange(D)
    s, a, r = f // 68, (f % 68) // SHARD, f % SHARD
    hid = np.zeros((D, D), np.float32)
    hid[f, np.where(r < 16, a * 256 + s * 16 + r, 1024 + a * 16 + s)] = 1
    k = np.arange(SMALLS)
    is_vec, is_up = k < 136, (k >= 136) & (k < 204)
    k_row = np.where(is_vec, k // 8, np.where(is_up, (k - 136) % SHARD, -1))
    k_out = np.where(is_vec, k % 8, np.where(is_up, 8 + (k - 136) // SHARD, -1))
    pick = (k_out[None, :] == np.arange(16)[:, None]).astype(np.float32)
    spread = (np.arange(NDP)[:, None] == shard_of[None, :]).astype(np.float32)
    keep = (k_row[:, None] == row_of[None, :]).astype(np.float32)
    nat = np.arange(PAD)
    spread_nat = (np.arange(NDP)[:, None] == nat[None, :] // SHARD).astype(np.float32)
    keep_nat = (k_row[:, None] == nat[None, :] % SHARD).astype(np.float32)
    m = np.arange(MAIN)
    turn = np.zeros((MAIN, MAIN), np.float32)
    turn[(m % 16) * NDP + m // 16, m] = 1
    names = ("order", "hid", "pick", "spread", "keep", "spread_nat", "keep_nat", "turn")
    values = (order, hid, pick, spread, keep, spread_nat, keep_nat, turn)
    found = {name: jnp.asarray(value, BF) for name, value in zip(names, values)}
    found["order_d"] = jnp.asarray(order[:D], BF)
    return found


def matmul(a, b):
    return jnp.dot(a, b, preferred_element_type=F32)


def dot_t(a, b):
    return lax.dot_general(a, b, (((1,), (1,)), ((), ())), preferred_element_type=F32)


def t_dot(a, b):
    return lax.dot_general(a, b, (((0,), (0,)), ((), ())), preferred_element_type=F32)


def norm_parts(features):
    centred = features - jnp.mean(features, axis=-1, keepdims=True)
    inverse = lax.rsqrt(jnp.mean(centred * centred, axis=-1, keepdims=True) + NORM_EPSILON)
    return centred * inverse, inverse


def norm_back(gradient, normed, inverse, gain):
    scaled = gradient * gain
    centred = scaled - jnp.mean(scaled, axis=-1, keepdims=True)
    return inverse * (centred - normed * jnp.mean(scaled * normed, axis=-1, keepdims=True))


def col_sum(v):
    return jnp.sum(v, axis=0, keepdims=True)


def unpack_kernel(whole, pick, spread, keep, spread_nat, keep_nat, turn, tails, vecs, nat, raw, sem):
    copy = pltpu.make_async_copy(whole.at[:, pl.ds(TAIL0, TAILW)], raw, sem)
    copy.start()
    copy.wait()
    turned = matmul(turn[...], raw[...]).astype(BF)
    for j in range(16):
        tails[:, j * TAILW : (j + 1) * TAILW] = turned[j * NDP : (j + 1) * NDP]
    small = tails[:, TAIL0 : TAIL0 + SMALLS]
    for out, s, k in ((vecs, spread, keep), (nat, spread_nat, keep_nat)):
        wide = t_dot(small, s[...]) * k[...].astype(F32)
        out[...] = matmul(pick[...], wide.astype(BF))


def unpack(whole, c):
    vm = pl.BlockSpec(memory_space=pltpu.VMEM)
    return pl.pallas_call(
        unpack_kernel,
        in_specs=[pl.BlockSpec(memory_space=pl.ANY)] + [vm] * 6,
        out_specs=[vm] * 3,
        out_shape=[
            jax.ShapeDtypeStruct((NDP, 16 * TAILW), BF),
            jax.ShapeDtypeStruct((16, D), F32),
            jax.ShapeDtypeStruct((16, PAD), F32),
        ],
        scratch_shapes=[pltpu.VMEM((MAIN, TAILW), BF), pltpu.SemaphoreType.DMA],
        compiler_params=pltpu.CompilerParams(vmem_limit_bytes=VMEM_BYTES),
        name="unpack",
    )(whole, c["pick"], c["spread"], c["keep"], c["spread_nat"], c["keep_nat"], c["turn"])


class Weights:
    def __init__(self, whole, tails, buf, sems):
        self.whole, self.tails, self.buf, self.sems = whole, tails, buf, sems

    def copies(self, b):
        cols = pl.ds(b * PAD, PAD)
        return (
            pltpu.make_async_copy(
                self.whole.at[:, cols], self.buf.at[b, pl.ds(0, MAIN)], self.sems.at[b, 0]
            ),
            pltpu.make_async_copy(
                self.tails.at[:, cols], self.buf.at[b, pl.ds(MAIN, NDP)], self.sems.at[b, 1]
            ),
        )

    def start(self, blocks):
        for b in blocks:
            for copy in self.copies(b):
                copy.start()

    def wait(self, b):
        for copy in self.copies(b):
            copy.wait()


def pair_masks():
    lane = lax.broadcasted_iota(jnp.int32, (ROWS, 128), 1)
    first = (lane < HDIM).astype(F32)
    return first, 1.0 - first


def stacked(v, masks):
    return jnp.concatenate([(v * m).astype(BF) for m in masks], axis=0)


def soft_pair(q, kk, allowed):
    scores = dot_t(q, kk) * SCORE_SCALE
    halves = []
    for h in range(2):
        s = jnp.where(allowed, scores[:, h * ROWS : (h + 1) * ROWS], -1e30)
        e = jnp.exp(s - jnp.max(s, axis=-1, keepdims=True))
        halves.append(e / jnp.sum(e, axis=-1, keepdims=True))
    return halves


def forward_part(w, wait, x_ref, place, pairs_ref, vecs, nat, order, r):
    x = x_ref[...].astype(F32)
    normed, _ = norm_parts(x)
    r["attn_in"][0] = (normed * vecs[0:1] + vecs[1:2]).astype(BF)

    def project(i, carry):
        if wait:
            w.wait(QKV + i)
        shift = jnp.where(i == 0, nat[2:3], jnp.where(i == 2, nat[3:4], 0.0))
        r["packed"][i] = (matmul(r["attn_in"][0], w.buf[QKV + i]) + shift).astype(BF)
        return carry

    lax.fori_loop(0, 3, project, 0)
    masks = pair_masks()
    allowed = pairs_ref[...] > 0
    for p in range(PAIRS):
        cols = pl.ds(p * 128, 128)
        kk = stacked(r["packed"][1, :, cols].astype(F32), masks)
        vv = stacked(r["packed"][2, :, cols].astype(F32), masks)
        halves = soft_pair(r["packed"][0, :, cols], kk, allowed)
        soft = jnp.concatenate([h.astype(BF) for h in halves], axis=1)
        r["heads"][:, cols] = matmul(soft, vv).astype(BF)
    r["attn_in"][1] = matmul(r["heads"][...], order[...]).astype(BF)
    if wait:
        w.wait(OUT)
    branch = matmul(r["attn_in"][1], w.buf[OUT])[:, :D]
    middle = x + branch + vecs[4:5]
    r["middle"][...] = middle
    normed, _ = norm_parts(middle)
    r["second"][...] = (normed * vecs[5:6] + vecs[6:7]).astype(BF)
    r["acc"][...] = jnp.zeros((ROWS, PAD), F32)

    def feed(a, carry):
        if wait:
            w.wait(UP + a)
        hidden = matmul(r["second"][...], w.buf[UP + a])[:, :D] + vecs[pl.ds(8 + a, 1)]
        r["hidden"][a] = hidden
        bent = jnp.tanh(GELU_C * (hidden + GELU_A * (hidden * hidden * hidden)))
        r["active"][a] = (0.5 * hidden * (1.0 + bent)).astype(BF)
        if wait:
            w.wait(DOWN + a)
        r["acc"][...] += matmul(r["active"][a], w.buf[DOWN + a])
        return carry

    lax.fori_loop(0, 4, feed, 0)
    r["result"][...] = (r["middle"][...] + r["acc"][:, :D] + vecs[7:8]).astype(BF)
    for d in range(4):
        z = lax.rem(place[2] + d, 4)
        out = r[f"early{d}"]
        out[0] = r["second"][...]
        out[1] = r["active"][z]
        out[2] = r["attn_in"][z // 3]


def backward_part(w, wait, grad_ref, x_ref, place, pairs_ref, vecs, order, r):
    grad = grad_ref[...]
    dres = grad.astype(F32)
    r["acc"][...] = jnp.zeros((ROWS, PAD), F32)

    def feed(a, carry):
        if wait:
            w.wait(DOWN + a)
        dactive = dot_t(grad_ref[...], w.buf[DOWN + a, :, :D])
        h = r["hidden"][a]
        square = h * h
        bent = jnp.tanh(GELU_C * (h + GELU_A * (square * h)))
        slope = 0.5 * (1.0 + bent) + (0.5 * GELU_C) * h * (1.0 - bent * bent) * (
            1.0 + (3 * GELU_A) * square
        )
        dhidden = (dactive * slope).astype(BF)
        r["dhidden"][a] = dhidden
        r["small"][pl.ds(8 + a, 1)] = col_sum(dhidden.astype(F32))
        if wait:
            w.wait(UP + a)
        r["acc"][:, :D] += dot_t(dhidden, w.buf[UP + a, :, :D])
        return carry

    lax.fori_loop(0, 4, feed, 0)
    dsecond = r["acc"][:, :D]
    normed, inverse = norm_parts(r["middle"][...])
    r["small"][5:6] = col_sum(dsecond * normed)
    r["small"][6:7] = col_sum(dsecond)
    r["small"][7:8] = col_sum(dres)
    dmiddle = dres + norm_back(dsecond, normed, inverse, vecs[5:6])
    r["middle"][...] = dmiddle
    dattn = dmiddle.astype(BF)
    r["dpacked"][3] = dattn
    r["small"][4:5] = col_sum(dattn.astype(F32))
    if wait:
        w.wait(OUT)
    dmixed = dot_t(dattn, w.buf[OUT, :, :D]).astype(BF)
    r["heads"][...] = dot_t(dmixed, order[...]).astype(BF)
    masks = pair_masks()
    allowed = pairs_ref[...] > 0
    for p in range(PAIRS):
        cols = pl.ds(p * 128, 128)
        width = min(D - p * 128, 128)
        live = pl.ds(p * 128, width)
        q = r["packed"][0, :, cols]
        kk = stacked(r["packed"][1, :, cols].astype(F32), masks)
        vv = stacked(r["packed"][2, :, cols].astype(F32), masks)
        dm = r["heads"][:, cols]
        halves = soft_pair(q, kk, allowed)
        dsoft = dot_t(dm, vv)
        dscores = []
        for h, p_half in enumerate(halves):
            d_half = dsoft[:, h * ROWS : (h + 1) * ROWS]
            centre = jnp.sum(d_half * p_half, axis=-1, keepdims=True)
            dscores.append((p_half * (d_half - centre)).astype(BF))
        ds = jnp.concatenate(dscores, axis=1)
        soft = jnp.concatenate([h.astype(BF) for h in halves], axis=1)
        dq = matmul(ds, kk) * SCORE_SCALE
        dk = t_dot(ds, q) * SCORE_SCALE
        dv = t_dot(soft, dm)
        dk = dk[:ROWS] * masks[0] + dk[ROWS:] * masks[1]
        dv = dv[:ROWS] * masks[0] + dv[ROWS:] * masks[1]
        for i, v in enumerate((dq, dk, dv)):
            r["dpacked"][i, :, live] = v[:, :width].astype(BF)
    sums = [col_sum(r["dpacked"][i].astype(F32)) for i in (0, 2)]
    sums = jnp.concatenate(sums + [jnp.zeros((14, D), F32)], axis=0).astype(BF)
    r["small"][2:4] = matmul(sums, order[:D])[:2]
    r["acc"][...] = jnp.zeros((ROWS, PAD), F32)

    def project(i, carry):
        if wait:
            w.wait(QKV + i)
        r["acc"][:, :D] += dot_t(r["dpacked"][i], w.buf[QKV + i, :, :D])
        return carry

    lax.fori_loop(0, 3, project, 0)
    dentry = r["acc"][:, :D]
    normed, inverse = norm_parts(x_ref[...].astype(F32))
    r["small"][0:1] = col_sum(dentry * normed)
    r["small"][1:2] = col_sum(dentry)
    r["small"][12:16] = jnp.zeros((4, D), F32)
    r["dx"][...] = (r["middle"][...] + norm_back(dentry, normed, inverse, vecs[0:1])).astype(BF)
    for d in range(4):
        z = lax.rem(place[2] + d, 4)
        r[f"late{d}"][0] = r["dhidden"][z]
        r[f"late{d}"][1] = r["dpacked"][z]


ROW = (ROWS, D)
KEPT = {
    "packed": ((3, ROWS, PAD), BF),
    "middle": (ROW, F32),
    "hidden": ((4,) + ROW, F32),
}
FWD_OUT = {"result": (ROW, BF), **{f"early{d}": ((3,) + ROW, BF) for d in range(4)}}
BWD_OUT = {
    "dx": (ROW, BF),
    **{f"late{d}": ((2,) + ROW, BF) for d in range(4)},
    "small": ((16, D), F32),
}
FWD_WORK = {
    "attn_in": ((2,) + ROW, BF),
    "second": (ROW, BF),
    "active": ((4,) + ROW, BF),
}
BWD_WORK = {
    "dhidden": ((4,) + ROW, BF),
    "dpacked": ((4,) + ROW, BF),
}
WORK = {"heads": ((ROWS, PAD), BF), "acc": ((ROWS, PAD), F32)}


def layer_call(kind, whole, tails, vecs, nat, pairs, order, place, x, grad=None, kept=None):
    outs = dict(FWD_OUT) if kind != "bwd" else {}
    work = dict(WORK)
    if kind == "fwd":
        outs.update(KEPT)
    else:
        outs.update(BWD_OUT)
        work.update(BWD_WORK)
    if kind != "bwd":
        work.update(FWD_WORK)
    if kind == "both":
        work.update(KEPT)
    if kind == "bwd":
        work["middle"] = KEPT["middle"]
    ins = [whole, tails, place, vecs, nat, pairs, order, x]
    if grad is not None:
        ins.append(grad)
    if kind == "bwd":
        ins += [kept["packed"], kept["middle"], kept["hidden"]]

    def kernel(*refs):
        given, refs = refs[: len(ins)], refs[len(ins) :]
        out_refs, refs = refs[: len(outs)], refs[len(outs) :]
        r = dict(zip(outs, out_refs))
        r.update(zip(work, refs))
        buf, sems = refs[len(work) :]
        w = Weights(given[0], given[1], buf, sems)
        place_ref, vecs_ref, nat_ref, pairs_ref, order_ref, x_ref = given[2:8]
        if kind == "bwd":
            blocks = [b for a in range(4) for b in (DOWN + a, UP + a)] + [OUT, 8, 9, 10]
            w.start(blocks)
            r["packed"], r["hidden"] = given[9], given[11]
            r["middle"][...] = given[10][...]
            backward_part(w, True, given[8], x_ref, place_ref, pairs_ref, vecs_ref, order_ref, r)
            return
        w.start([8, 9, 10, OUT] + [b for a in range(4) for b in (UP + a, DOWN + a)])
        forward_part(w, True, x_ref, place_ref, pairs_ref, vecs_ref, nat_ref, order_ref, r)
        if kind == "both":
            backward_part(w, False, given[8], x_ref, place_ref, pairs_ref, vecs_ref, order_ref, r)

    vm = pl.BlockSpec(memory_space=pltpu.VMEM)
    hbm = pl.BlockSpec(memory_space=pl.ANY)
    results = pl.pallas_call(
        kernel,
        in_specs=[hbm, hbm, pl.BlockSpec(memory_space=pltpu.SMEM)] + [vm] * (len(ins) - 3),
        out_specs=[vm] * len(outs),
        out_shape=[jax.ShapeDtypeStruct(s, t) for s, t in outs.values()],
        scratch_shapes=[pltpu.VMEM(s, t) for s, t in work.values()]
        + [pltpu.VMEM((BLOCKS, D, PAD), BF), pltpu.SemaphoreType.DMA((BLOCKS, 2))],
        compiler_params=pltpu.CompilerParams(vmem_limit_bytes=VMEM_BYTES),
        name="layer_" + kind,
    )(*ins)
    return dict(zip(outs, results))


CHUNK = 72
HALF = 640
WIDE = (PAD + HALF, PAD + PAD - HALF)


def local_call(kernel, name, place, ins, out_shapes, scratch=()):
    vm = pl.BlockSpec(memory_space=pltpu.VMEM)
    return pl.pallas_call(
        kernel,
        in_specs=[pl.BlockSpec(memory_space=pltpu.SMEM)] + [vm] * len(ins),
        out_specs=[vm] * len(out_shapes),
        out_shape=[jax.ShapeDtypeStruct(s, t) for s, t in out_shapes],
        scratch_shapes=list(scratch),
        compiler_params=pltpu.CompilerParams(vmem_limit_bytes=VMEM_BYTES),
        name=name,
    )(place, *ins)


def products_kernel(place, *refs):
    early, late, branch, small = refs[:4], refs[4:8], refs[8:12], refs[12]
    outs, (first, second) = refs[13:21], refs[21:]

    def rows_of(parts, i=None):
        return jnp.concatenate([p[...] if i is None else p[i] for p in parts], axis=0)

    gap = jnp.zeros((4 * ROWS, PAD - D), BF)
    slot = lax.broadcasted_iota(jnp.int32, (16, PAD), 1) - D
    unit = (slot == lax.broadcasted_iota(jnp.int32, (16, PAD), 0)).astype(F32).astype(BF)
    nothing = jnp.zeros((4, PAD), F32)

    def product(a, b, store):
        last = t_dot(a[:, MAIN:], b)
        for x in range(4):
            main = t_dot(a[:, x * 256 : (x + 1) * 256], b)
            for y in range(4):
                at = (x * 4 + y) * 4
                rows = [main[y * 64 : (y + 1) * 64], last[at : at + 4], nothing]
                store(x, y, jnp.concatenate(rows, axis=0).astype(BF))

    def store_up(x, y, v):
        first[x, y, :, :PAD] = v

    def store_down(x, y, v):
        second[y, x, :, :PAD] = v

    def store_attn(x, y, v):
        first[x, y, :, PAD:] = v[:, :HALF]
        second[y, x, :, PAD:] = v[:, HALF:]

    def wide(v):
        return jnp.concatenate([v, gap], axis=1)

    product(rows_of(early, 1), wide(rows_of(branch)), store_down)
    product(rows_of(early, 0), wide(rows_of(late, 0)), store_up)
    a = jnp.concatenate([rows_of(early, 2), small[...].astype(BF)], axis=0)
    b = jnp.concatenate([wide(rows_of(late, 1)), unit], axis=0)
    product(a, b, store_attn)
    for d in range(4):
        outs[d][...] = first[lax.rem(place[0] + d, 4)]
        outs[4 + d][...] = second[lax.rem(place[1] + d, 4)]


def total(parts):
    return sum((p.astype(F32) for p in parts[1:]), parts[0].astype(F32))


def first_sum_kernel(place, *refs):
    for h, other in ((0, 1), (1, 0)):
        parts, outs = refs[4 * h : 4 * h + 4], refs[8 + 4 * h : 12 + 4 * h]
        for d in range(4):
            i = lax.rem(place[other] + d, 4)
            outs[d][...] = total([p[i] for p in parts]).astype(BF)


def second_sum_kernel(place, *refs):
    outs, held = refs[8:12], refs[12]
    for h in range(2):
        full = total([p[...] for p in refs[4 * h : 4 * h + 4]])
        start = h * WIDE[0]
        empty = jnp.zeros((7, WIDE[h]), F32)
        for z in range(4):
            rows = [full[z * 16 : (z + 1) * 16], full[64 + z : 65 + z], empty]
            held[z, :, start : start + WIDE[h]] = jnp.concatenate(rows, axis=0).astype(BF)
    for d in range(4):
        outs[d][...] = held[lax.rem(place[2] + d, 4)]


def final_kernel(place, *refs):
    parts, (hid, order), outs, held = refs[:4], refs[4:6], refs[6:11], refs[11]
    g_up, g_down, g_out, g_qkv, sums = outs
    for d in range(4):
        held[lax.rem(place[2] + 4 - d, 4)] = parts[d][...]
    up = []
    for j in range(4):
        pieces = [held[a, :, j * 256 : (j + 1) * 256] for a in range(4)]
        pieces += [held[a, :, MAIN + j * 16 : MAIN + (j + 1) * 16] for a in range(4)]
        up.append(jnp.concatenate(pieces, axis=1))
    up = dot_t(jnp.concatenate(up, axis=0), hid[...])
    for j in range(4):
        g_up[:, j * D : (j + 1) * D] = up[j * 24 : j * 24 + SHARD]
    start = WIDE[0]
    attn = [
        jnp.concatenate([held[a, :, PAD:start], held[a, :, start + PAD :]], axis=1)
        for a in range(4)
    ]
    rows = [held[a, :, start : start + D] for a in range(4)] + [attn[3][:, :D]]
    rows = dot_t(jnp.concatenate(rows, axis=0), order[...])
    for a in range(4):
        g_down[a * SHARD : (a + 1) * SHARD] = rows[a * 24 : a * 24 + SHARD]
    g_out[...] = rows[96 : 96 + SHARD]
    for i in range(3):
        g_qkv[:, i * D : (i + 1) * D] = attn[i][:SHARD, :D].astype(F32)
    sums[...] = total([v[:SHARD, D:] for v in attn])


def ring(v, axis, d):
    return lax.ppermute(v, axis, [(i, (i + d) % 4) for i in range(4)])


def zeros_of(spec):
    return {name: jnp.zeros(s, t) for name, (s, t) in spec.items()}


def pad_cols(v, width):
    return jnp.pad(v, ((0, 0), (0, width - v.shape[1])))


def body(inputs, cotangent, lengths, vectors, qkv_w, out_w, up_w, up_b, down_w):
    section = lax.axis_index("section")
    mb, rows, _ = inputs.shape
    n = mb * rows
    c = constants()
    order = c["order"]

    outdown = matmul(jnp.concatenate([out_w[0], down_w[0]], axis=0), c["order_d"]).astype(BF)
    hid = matmul(up_w[0].reshape(SHARD * 4, D), c["hid"]).astype(BF).reshape(SHARD, 4, D)
    hid_main = hid[:, :, :MAIN].reshape(SHARD, 4, 4, 256).transpose(0, 2, 1, 3)
    hid_last = hid[:, :, MAIN:].reshape(SHARD, 4, 4, 16).transpose(0, 2, 1, 3)
    hid = jnp.concatenate(
        [
            hid_main.reshape(SHARD, 4, MAIN),
            hid_last.reshape(SHARD, 4, NDP),
            jnp.zeros((SHARD, 4, PAD - D), BF),
        ],
        axis=2,
    )
    shard = [hid.reshape(SHARD, 4 * PAD)]
    shard += [pad_cols(outdown[SHARD * (1 + a) : SHARD * (2 + a)], PAD) for a in range(4)]
    shard += [pad_cols(qkv_w[0][:, i * D : (i + 1) * D], PAD) for i in range(3)]
    shard += [pad_cols(outdown[:SHARD], PAD)]
    shard = jnp.concatenate(shard, axis=1)
    tail = jnp.concatenate([shard[16], vectors[0].reshape(-1), up_b[0]])
    tail = jnp.pad(tail, (0, 16 * TAILW - tail.shape[0])).reshape(16, TAILW)
    sent = jnp.concatenate([shard[:16], tail], axis=1)
    whole = lax.all_gather(sent, ("x", "y", "z"), axis=0, tiled=True)
    tails, vecs, nat = unpack(whole, c)

    ends = jnp.cumsum(lengths[:, 0], axis=1)
    place = jnp.arange(rows, dtype=jnp.int32)
    seg = jnp.sum((place[None, :, None] >= ends[:, None, :]).astype(jnp.int32), axis=2)
    seg = (seg + 8 * jnp.arange(mb, dtype=jnp.int32)[:, None]).reshape(n)
    at = jnp.arange(n, dtype=jnp.int32)
    pairs = ((seg[:, None] == seg[None, :]) & (at[:, None] >= at[None, :])).astype(F32)

    order_d = c["order_d"]
    x0 = matmul(inputs.reshape(n, D), order_d).astype(BF)
    cot = matmul(cotangent.reshape(n, D), order_d).astype(BF)
    place = jnp.stack([lax.axis_index("x"), lax.axis_index("y"), lax.axis_index("z")])
    call = functools.partial(
        layer_call,
        whole=whole,
        tails=tails,
        vecs=vecs,
        nat=nat,
        pairs=pairs,
        order=order,
        place=place,
    )

    first = lax.cond(
        section == 0,
        lambda: call("fwd", x=x0),
        lambda: zeros_of({**FWD_OUT, **KEPT}),
    )
    arrived = lax.ppermute(first["result"], "section", [(0, 1)])
    kept = {k: first[k] for k in KEPT}
    fwd = {k: first[k] for k in FWD_OUT}

    def top():
        out = call("both", x=arrived, grad=cot)
        return {k: out[k] for k in FWD_OUT}, {k: out[k] for k in BWD_OUT}

    fwd, bwd = lax.cond(section == 1, top, lambda: (fwd, zeros_of(BWD_OUT)))
    coming = lax.ppermute(bwd["dx"], "section", [(1, 0)])
    early = [fwd["early0"]] + [ring(fwd[f"early{d}"], "z", d) for d in (1, 3, 2)]
    branch = jnp.where(section == 0, coming, cot)
    branches = [branch] + [ring(branch, "z", d) for d in (1, 3, 2)]
    bwd = lax.cond(
        section == 0, lambda: call("bwd", x=x0, grad=coming, kept=kept), lambda: bwd
    )
    late = [bwd["late0"]] + [ring(bwd[f"late{d}"], "z", d) for d in (1, 3, 2)]

    vmem = pltpu.VMEM
    out = local_call(
        products_kernel,
        "products",
        place,
        [*early, *late, *branches, bwd["small"]],
        [((4, CHUNK, WIDE[h]), BF) for h in (0, 1) for _ in range(4)],
        [vmem((4, 4, CHUNK, WIDE[h]), BF) for h in (0, 1)],
    )
    got = []
    for h, axis in ((0, "x"), (1, "y")):
        got += [out[4 * h]] + [ring(out[4 * h + d], axis, d) for d in (1, 3, 2)]
    out = local_call(
        first_sum_kernel,
        "first_sum",
        place,
        got,
        [((CHUNK, WIDE[h]), BF) for h in (0, 1) for _ in range(4)],
    )
    got = []
    for h, axis in ((0, "y"), (1, "x")):
        got += [out[4 * h]] + [ring(out[4 * h + d], axis, d) for d in (1, 3, 2)]
    out = local_call(
        second_sum_kernel,
        "second_sum",
        place,
        got,
        [((24, sum(WIDE)), BF)] * 4,
        [vmem((4, 24, sum(WIDE)), BF)],
    )
    got = [out[0]] + [ring(out[d], "z", d) for d in (1, 2, 3)]
    g_up, g_down, g_out, g_qkv, sums = local_call(
        final_kernel,
        "owners",
        place,
        [*got, c["hid"], order_d],
        [
            ((SHARD, FF), F32),
            ((4 * SHARD, D), F32),
            ((SHARD, D), F32),
            ((SHARD, 3 * D), F32),
            ((SHARD, PAD - D), F32),
        ],
        [vmem((4, 24, sum(WIDE)), BF)],
    )
    acts = dot_t(fwd["result"], order_d).astype(BF)
    grads = dot_t(bwd["dx"], order_d).astype(BF)
    return (
        acts.reshape(1, mb, rows, D),
        grads.reshape(1, mb, rows, D),
        sums[None, :, :8],
        g_qkv[None],
        g_out[None],
        g_up[None],
        sums[:, 8:12].T.reshape(1, 4 * SHARD),
        g_down[None],
    )


def solution(mesh):
    grid = Mesh(mesh.devices.reshape(2, 4, 4, 4), ("section", "x", "y", "z"))
    dp = ("x", "y", "z")
    tokens = P(None, dp, None)
    rows = P("section", dp, None)
    in_specs = (tokens, tokens, tokens, rows, rows, rows, rows, P("section", dp), rows)
    stacks = P("section", None, dp, None)
    out_specs = (stacks, stacks, rows, rows, rows, rows, P("section", dp), rows)
    return jax.shard_map(body, mesh=grid, in_specs=in_specs, out_specs=out_specs, check_vma=False)
```

```python
import functools

import jax
import jax.numpy as jnp
import numpy as np
from jax import lax
from jax.experimental import pallas as pl
from jax.experimental.pallas import tpu as pltpu
from jax.sharding import Mesh, PartitionSpec as P

HEADS = 17
HDIM = 64
D = HEADS * HDIM
FF = 4 * D
SHARD = 17
NDP = 64
MAIN = 16 * NDP
PAD = 1152
ROWS = 128
PAIRS = PAD // 128

UP, DOWN, QKV, OUT, BLOCKS = 0, 4, 8, 11, 12
TAIL0 = BLOCKS * PAD
TAILW = 896
WIDTH = TAIL0 + TAILW
SMALLS = 256

NORM_EPSILON = 1e-05
SCORE_SCALE = 0.125
GELU_C = float(np.sqrt(2 / np.pi))
GELU_A = 0.044715
BF = jnp.bfloat16
F32 = jnp.float32
VMEM_BYTES = 58 * 1024 * 1024


def constants():
    n = np.arange(D)
    shard_of = np.where(n < MAIN, n // 16, n - MAIN)
    row_of = np.where(n < MAIN, n % 16, 16)
    order = np.zeros((PAD, D), np.float32)
    order[shard_of * SHARD + row_of, n] = 1
    f = np.arange(D)
    s, a, r = f // 68, (f % 68) // SHARD, f % SHARD
    hid = np.zeros((D, D), np.float32)
    hid[f, np.where(r < 16, a * 256 + s * 16 + r, 1024 + a * 16 + s)] = 1
    k = np.arange(SMALLS)
    is_vec, is_up = k < 136, (k >= 136) & (k < 204)
    k_row = np.where(is_vec, k // 8, np.where(is_up, (k - 136) % SHARD, -1))
    k_out = np.where(is_vec, k % 8, np.where(is_up, 8 + (k - 136) // SHARD, -1))
    pick = (k_out[None, :] == np.arange(16)[:, None]).astype(np.float32)
    spread = (np.arange(NDP)[:, None] == shard_of[None, :]).astype(np.float32)
    keep = (k_row[:, None] == row_of[None, :]).astype(np.float32)
    nat = np.arange(PAD)
    spread_nat = (np.arange(NDP)[:, None] == nat[None, :] // SHARD).astype(np.float32)
    keep_nat = (k_row[:, None] == nat[None, :] % SHARD).astype(np.float32)
    m = np.arange(MAIN)
    turn = np.zeros((MAIN, MAIN), np.float32)
    turn[(m % 16) * NDP + m // 16, m] = 1
    names = ("order", "hid", "pick", "spread", "keep", "spread_nat", "keep_nat", "turn")
    values = (order, hid, pick, spread, keep, spread_nat, keep_nat, turn)
    found = {name: jnp.asarray(value, BF) for name, value in zip(names, values)}
    found["order_d"] = jnp.asarray(order[:D], BF)
    found["hid_t"] = jnp.asarray(hid.T, BF)
    return found


def matmul(a, b):
    return jnp.dot(a, b, preferred_element_type=F32)


def dot_t(a, b):
    return lax.dot_general(a, b, (((1,), (1,)), ((), ())), preferred_element_type=F32)


def t_dot(a, b):
    return lax.dot_general(a, b, (((0,), (0,)), ((), ())), preferred_element_type=F32)


def norm_parts(features):
    centred = features - jnp.mean(features, axis=-1, keepdims=True)
    inverse = lax.rsqrt(jnp.mean(centred * centred, axis=-1, keepdims=True) + NORM_EPSILON)
    return centred * inverse, inverse


def norm_back(gradient, normed, inverse, gain):
    scaled = gradient * gain
    centred = scaled - jnp.mean(scaled, axis=-1, keepdims=True)
    return inverse * (centred - normed * jnp.mean(scaled * normed, axis=-1, keepdims=True))


def col_sum(v):
    return jnp.sum(v, axis=0, keepdims=True)


def unpack_kernel(whole, pick, spread, keep, spread_nat, keep_nat, turn, tails, vecs, nat, raw, sem):
    copy = pltpu.make_async_copy(whole.at[:, pl.ds(TAIL0, TAILW)], raw, sem)
    copy.start()
    copy.wait()
    turned = matmul(turn[...], raw[...]).astype(BF)
    for j in range(16):
        tails[:, j * TAILW : (j + 1) * TAILW] = turned[j * NDP : (j + 1) * NDP]
    small = tails[:, TAIL0 : TAIL0 + SMALLS]
    for out, s, k in ((vecs, spread, keep), (nat, spread_nat, keep_nat)):
        wide = t_dot(small, s[...]) * k[...].astype(F32)
        out[...] = matmul(pick[...], wide.astype(BF))


def unpack(whole, c):
    vm = pl.BlockSpec(memory_space=pltpu.VMEM)
    return pl.pallas_call(
        unpack_kernel,
        in_specs=[pl.BlockSpec(memory_space=pl.ANY)] + [vm] * 6,
        out_specs=[vm] * 3,
        out_shape=[
            jax.ShapeDtypeStruct((NDP, 16 * TAILW), BF),
            jax.ShapeDtypeStruct((16, D), F32),
            jax.ShapeDtypeStruct((16, PAD), F32),
        ],
        scratch_shapes=[pltpu.VMEM((MAIN, TAILW), BF), pltpu.SemaphoreType.DMA],
        compiler_params=pltpu.CompilerParams(vmem_limit_bytes=VMEM_BYTES),
        name="unpack",
    )(whole, c["pick"], c["spread"], c["keep"], c["spread_nat"], c["keep_nat"], c["turn"])


class Weights:
    def __init__(self, whole, tails, buf, sems):
        self.whole, self.tails, self.buf, self.sems = whole, tails, buf, sems

    def copies(self, b):
        cols = pl.ds(b * PAD, PAD)
        return (
            pltpu.make_async_copy(
                self.whole.at[:, cols], self.buf.at[b, pl.ds(0, MAIN)], self.sems.at[b, 0]
            ),
            pltpu.make_async_copy(
                self.tails.at[:, cols], self.buf.at[b, pl.ds(MAIN, NDP)], self.sems.at[b, 1]
            ),
        )

    def start(self, blocks):
        for b in blocks:
            for copy in self.copies(b):
                copy.start()

    def wait(self, b):
        for copy in self.copies(b):
            copy.wait()


def pair_masks():
    lane = lax.broadcasted_iota(jnp.int32, (ROWS, 128), 1)
    first = (lane < HDIM).astype(F32)
    return first, 1.0 - first


def stacked(v, masks):
    return jnp.concatenate([(v * m).astype(BF) for m in masks], axis=0)


def soft_pair(q, kk, allowed):
    scores = dot_t(q, kk) * SCORE_SCALE
    halves = []
    for h in range(2):
        s = jnp.where(allowed, scores[:, h * ROWS : (h + 1) * ROWS], -1e30)
        e = jnp.exp(s - jnp.max(s, axis=-1, keepdims=True))
        halves.append(e / jnp.sum(e, axis=-1, keepdims=True))
    return halves


def forward_part(w, wait, x_ref, place, pairs_ref, vecs, nat, order, r):
    x = x_ref[...].astype(F32)
    normed, _ = norm_parts(x)
    r["attn_in"][0] = (normed * vecs[0:1] + vecs[1:2]).astype(BF)

    def project(i, carry):
        if wait:
            w.wait(QKV + i)
        shift = jnp.where(i == 0, nat[2:3], jnp.where(i == 2, nat[3:4], 0.0))
        r["packed"][i] = (matmul(r["attn_in"][0], w.buf[QKV + i]) + shift).astype(BF)
        return carry

    lax.fori_loop(0, 3, project, 0)
    masks = pair_masks()
    allowed = pairs_ref[...] > 0
    for p in range(PAIRS):
        cols = pl.ds(p * 128, 128)
        kk = stacked(r["packed"][1, :, cols].astype(F32), masks)
        vv = stacked(r["packed"][2, :, cols].astype(F32), masks)
        halves = soft_pair(r["packed"][0, :, cols], kk, allowed)
        soft = jnp.concatenate([h.astype(BF) for h in halves], axis=1)
        r["heads"][:, cols] = matmul(soft, vv).astype(BF)
    r["attn_in"][1] = matmul(r["heads"][...], order[...]).astype(BF)
    if wait:
        w.wait(OUT)
    branch = matmul(r["attn_in"][1], w.buf[OUT])[:, :D]
    middle = x + branch + vecs[4:5]
    r["middle"][...] = middle
    normed, _ = norm_parts(middle)
    r["second"][...] = (normed * vecs[5:6] + vecs[6:7]).astype(BF)
    r["acc"][...] = jnp.zeros((ROWS, PAD), F32)

    def feed(a, carry):
        if wait:
            w.wait(UP + a)
        hidden = matmul(r["second"][...], w.buf[UP + a])[:, :D] + vecs[pl.ds(8 + a, 1)]
        r["hidden"][a] = hidden
        bent = jnp.tanh(GELU_C * (hidden + GELU_A * (hidden * hidden * hidden)))
        r["active"][a] = (0.5 * hidden * (1.0 + bent)).astype(BF)
        if wait:
            w.wait(DOWN + a)
        r["acc"][...] += matmul(r["active"][a], w.buf[DOWN + a])
        return carry

    lax.fori_loop(0, 4, feed, 0)
    r["result"][...] = (r["middle"][...] + r["acc"][:, :D] + vecs[7:8]).astype(BF)
    for d in range(4):
        z = lax.rem(place[2] + d, 4)
        out = r[f"early{d}"]
        out[0, :, :D] = r["second"][...]
        out[1, :, :D] = r["active"][z]
        out[2, :, :D] = r["attn_in"][z // 3]


def backward_part(w, wait, grad_ref, x_ref, place, pairs_ref, vecs, order, r):
    grad = grad_ref[...]
    dres = grad.astype(F32)
    r["acc"][...] = jnp.zeros((ROWS, PAD), F32)

    def feed(a, carry):
        if wait:
            w.wait(DOWN + a)
        dactive = dot_t(grad_ref[...], w.buf[DOWN + a, :, :D])
        h = r["hidden"][a]
        square = h * h
        bent = jnp.tanh(GELU_C * (h + GELU_A * (square * h)))
        slope = 0.5 * (1.0 + bent) + (0.5 * GELU_C) * h * (1.0 - bent * bent) * (
            1.0 + (3 * GELU_A) * square
        )
        dhidden = (dactive * slope).astype(BF)
        r["dhidden"][a] = dhidden
        r["small"][pl.ds(8 + a, 1)] = col_sum(dhidden.astype(F32))
        if wait:
            w.wait(UP + a)
        r["acc"][:, :D] += dot_t(dhidden, w.buf[UP + a, :, :D])
        return carry

    lax.fori_loop(0, 4, feed, 0)
    dsecond = r["acc"][:, :D]
    normed, inverse = norm_parts(r["middle"][...])
    r["small"][5:6] = col_sum(dsecond * normed)
    r["small"][6:7] = col_sum(dsecond)
    r["small"][7:8] = col_sum(dres)
    dmiddle = dres + norm_back(dsecond, normed, inverse, vecs[5:6])
    r["middle"][...] = dmiddle
    dattn = dmiddle.astype(BF)
    r["dpacked"][3] = dattn
    r["small"][4:5] = col_sum(dattn.astype(F32))
    if wait:
        w.wait(OUT)
    dmixed = dot_t(dattn, w.buf[OUT, :, :D]).astype(BF)
    r["heads"][...] = dot_t(dmixed, order[...]).astype(BF)
    masks = pair_masks()
    allowed = pairs_ref[...] > 0
    for p in range(PAIRS):
        cols = pl.ds(p * 128, 128)
        width = min(D - p * 128, 128)
        live = pl.ds(p * 128, width)
        q = r["packed"][0, :, cols]
        kk = stacked(r["packed"][1, :, cols].astype(F32), masks)
        vv = stacked(r["packed"][2, :, cols].astype(F32), masks)
        dm = r["heads"][:, cols]
        halves = soft_pair(q, kk, allowed)
        dsoft = dot_t(dm, vv)
        dscores = []
        for h, p_half in enumerate(halves):
            d_half = dsoft[:, h * ROWS : (h + 1) * ROWS]
            centre = jnp.sum(d_half * p_half, axis=-1, keepdims=True)
            dscores.append((p_half * (d_half - centre)).astype(BF))
        ds = jnp.concatenate(dscores, axis=1)
        soft = jnp.concatenate([h.astype(BF) for h in halves], axis=1)
        dq = matmul(ds, kk) * SCORE_SCALE
        dk = t_dot(ds, q) * SCORE_SCALE
        dv = t_dot(soft, dm)
        dk = dk[:ROWS] * masks[0] + dk[ROWS:] * masks[1]
        dv = dv[:ROWS] * masks[0] + dv[ROWS:] * masks[1]
        for i, v in enumerate((dq, dk, dv)):
            r["dpacked"][i, :, live] = v[:, :width].astype(BF)
    sums = [col_sum(r["dpacked"][i].astype(F32)) for i in (0, 2)]
    sums = jnp.concatenate(sums + [jnp.zeros((14, D), F32)], axis=0).astype(BF)
    r["small"][2:4] = matmul(sums, order[:D])[:2]
    r["acc"][...] = jnp.zeros((ROWS, PAD), F32)

    def project(i, carry):
        if wait:
            w.wait(QKV + i)
        r["acc"][:, :D] += dot_t(r["dpacked"][i], w.buf[QKV + i, :, :D])
        return carry

    lax.fori_loop(0, 3, project, 0)
    dentry = r["acc"][:, :D]
    normed, inverse = norm_parts(x_ref[...].astype(F32))
    r["small"][0:1] = col_sum(dentry * normed)
    r["small"][1:2] = col_sum(dentry)
    r["small"][12:16] = jnp.zeros((4, D), F32)
    r["dx"][...] = (r["middle"][...] + norm_back(dentry, normed, inverse, vecs[0:1])).astype(BF)
    for d in range(4):
        z = lax.rem(place[2] + d, 4)
        r[f"late{d}"][0, :, :D] = r["dhidden"][z]
        r[f"late{d}"][1, :, :D] = r["dpacked"][z]


ROW = (ROWS, D)
KEPT = {
    "packed": ((3, ROWS, PAD), BF),
    "middle": (ROW, F32),
    "hidden": ((4,) + ROW, F32),
}
FWD_OUT = {"result": (ROW, BF), **{f"early{d}": ((3, ROWS, PAD), BF) for d in range(4)}}
BWD_OUT = {
    "dx": (ROW, BF),
    **{f"late{d}": ((2, ROWS, PAD), BF) for d in range(4)},
    "small": ((16, D), F32),
}
FWD_WORK = {
    "attn_in": ((2,) + ROW, BF),
    "second": (ROW, BF),
    "active": ((4,) + ROW, BF),
}
BWD_WORK = {
    "dhidden": ((4,) + ROW, BF),
    "dpacked": ((4,) + ROW, BF),
}
WORK = {"heads": ((ROWS, PAD), BF), "acc": ((ROWS, PAD), F32)}


def layer_call(kind, whole, tails, vecs, nat, pairs, order, place, x, grad=None, old=None):
    outs = dict(FWD_OUT) if kind != "bwd" else {}
    work = dict(WORK)
    if kind == "fwd":
        outs.update(KEPT)
    else:
        outs.update(BWD_OUT)
        work.update(BWD_WORK)
    if kind != "bwd":
        work.update(FWD_WORK)
    else:
        work["active"] = FWD_WORK["active"]
    if kind != "fwd":
        work.update(KEPT)
    passed = {"fwd": {}, "both": FWD_OUT, "bwd": BWD_OUT}[kind]
    loaded = KEPT if kind == "bwd" else {}
    far = [whole, tails] + [old[k] for k in (*passed, *loaded)]
    near = [vecs, nat, pairs, order, x] + ([] if grad is None else [grad])
    section = 1 if kind == "both" else 0

    def kernel(place_ref, *refs):
        far_refs, refs = refs[: len(far)], refs[len(far) :]
        near_refs, refs = refs[: len(near)], refs[len(near) :]
        r = dict(zip(outs, refs))
        refs = refs[len(outs) :]
        r.update(zip(work, refs))
        buf, sems, old_sems = refs[len(work) :]
        w = Weights(far_refs[0], far_refs[1], buf, sems)
        vecs_ref, nat_ref, pairs_ref, order_ref, x_ref = near_refs[:5]
        old_refs = dict(zip((*passed, *loaded), far_refs[2:]))

        def fetch(names):
            return [
                pltpu.make_async_copy(old_refs[k], r[k], old_sems.at[i])
                for i, k in enumerate(names)
            ]

        @pl.when(place_ref[3] == section)
        def _():
            if kind == "bwd":
                w.start([DOWN])
                copies = fetch(loaded)
                for copy in copies:
                    copy.start()
                w.start([UP] + [b for a in range(1, 4) for b in (DOWN + a, UP + a)])
                w.start([OUT, 8, 9, 10])
                for copy in copies:
                    copy.wait()
            else:
                w.start([8, 9, 10, OUT] + [b for a in range(4) for b in (UP + a, DOWN + a)])
                forward_part(w, True, x_ref, place_ref, pairs_ref, vecs_ref, nat_ref, order_ref, r)
            if kind != "fwd":
                backward_part(
                    w,
                    kind == "bwd",
                    near_refs[5],
                    x_ref,
                    place_ref,
                    pairs_ref,
                    vecs_ref,
                    order_ref,
                    r,
                )

        if passed:

            @pl.when(place_ref[3] != section)
            def _():
                copies = fetch(passed)
                for copy in copies:
                    copy.start()
                for copy in copies:
                    copy.wait()

    vm = pl.BlockSpec(memory_space=pltpu.VMEM)
    results = pl.pallas_call(
        kernel,
        in_specs=[pl.BlockSpec(memory_space=pltpu.SMEM)]
        + [pl.BlockSpec(memory_space=pl.ANY)] * len(far)
        + [vm] * len(near),
        out_specs=[vm] * len(outs),
        out_shape=[jax.ShapeDtypeStruct(s, t) for s, t in outs.values()],
        scratch_shapes=[pltpu.VMEM(s, t) for s, t in work.values()]
        + [
            pltpu.VMEM((BLOCKS, D, PAD), BF),
            pltpu.SemaphoreType.DMA((BLOCKS, 2)),
            pltpu.SemaphoreType.DMA((16,)),
        ],
        compiler_params=pltpu.CompilerParams(vmem_limit_bytes=VMEM_BYTES),
        cost_estimate=pl.CostEstimate(
            flops={"fwd": 4, "both": 12, "bwd": 8}[kind] * 10**9,
            bytes_accessed=BLOCKS * D * PAD * 2,
            transcendentals=10**6,
        ),
        name="layer_" + kind,
    )(place, *far, *near)
    return dict(zip(outs, results))


CHUNK = 72
HALF = 768
WIDE = (PAD + HALF, PAD + PAD - HALF)


def local_call(kernel, name, place, ins, out_shapes, scratch=(), far=()):
    vm = pl.BlockSpec(memory_space=pltpu.VMEM)
    hbm = pl.BlockSpec(memory_space=pl.ANY)
    return pl.pallas_call(
        kernel,
        in_specs=[pl.BlockSpec(memory_space=pltpu.SMEM)] + [hbm] * len(far) + [vm] * len(ins),
        out_specs=[vm] * len(out_shapes),
        out_shape=[jax.ShapeDtypeStruct(s, t) for s, t in out_shapes],
        scratch_shapes=list(scratch),
        compiler_params=pltpu.CompilerParams(vmem_limit_bytes=VMEM_BYTES),
        name=name,
    )(place, *far, *ins)


def products_kernel(place, *refs):
    given, small, outs = refs[:12], refs[12], refs[13:21]
    first, second, early, late, branch, sems = refs[21:]
    copies = []
    for g, held in enumerate((early, late, branch)):
        for d in range(4):
            i = 4 * g + d
            copies.append(pltpu.make_async_copy(given[i], held.at[d], sems.at[i]))
    for i in (8, 9, 10, 11, 0, 1, 2, 3, 4, 5, 6, 7):
        copies[i].start()

    def wait(g):
        for copy in copies[4 * g : 4 * g + 4]:
            copy.wait()

    def rows_of(held, i=None):
        parts = [held[d] if i is None else held[d, i, :, :D] for d in range(4)]
        return jnp.concatenate(parts, axis=0)

    gap = jnp.zeros((4 * ROWS, PAD - D), BF)
    slot = lax.broadcasted_iota(jnp.int32, (16, PAD), 1) - D
    unit = (slot == lax.broadcasted_iota(jnp.int32, (16, PAD), 0)).astype(F32).astype(BF)
    nothing = jnp.zeros((4, PAD), F32)

    def product(a, b, store):
        last = t_dot(a[:, MAIN:], b)
        for x in range(4):
            main = t_dot(a[:, x * 256 : (x + 1) * 256], b)
            for y in range(4):
                at = (x * 4 + y) * 4
                rows = [main[y * 64 : (y + 1) * 64], last[at : at + 4], nothing]
                store(x, y, jnp.concatenate(rows, axis=0).astype(BF))

    def store_up(x, y, v):
        first[x, y, :, :PAD] = v

    def store_down(x, y, v):
        second[y, x, :, :PAD] = v

    def store_attn(x, y, v):
        first[x, y, :, PAD:] = v[:, :HALF]
        second[y, x, :, PAD:] = v[:, HALF:]

    def wide(v):
        return jnp.concatenate([v, gap], axis=1)

    wait(2)
    wait(0)
    product(rows_of(early, 1), wide(rows_of(branch)), store_down)
    wait(1)
    product(rows_of(early, 0), wide(rows_of(late, 0)), store_up)
    a = jnp.concatenate([rows_of(early, 2), small[...].astype(BF)], axis=0)
    b = jnp.concatenate([wide(rows_of(late, 1)), unit], axis=0)
    product(a, b, store_attn)
    for d in range(4):
        outs[d][...] = first[lax.rem(place[0] + d, 4)]
        outs[4 + d][...] = second[lax.rem(place[1] + d, 4)]


def total(parts):
    return sum((p.astype(F32) for p in parts[1:]), parts[0].astype(F32))


def first_sum_kernel(place, *refs):
    for h, other in ((0, 1), (1, 0)):
        parts, outs = refs[4 * h : 4 * h + 4], refs[8 + 4 * h : 12 + 4 * h]
        for d in range(4):
            i = lax.rem(place[other] + d, 4)
            outs[d][...] = total([p[i] for p in parts]).astype(BF)


def second_sum_kernel(place, *refs):
    outs, held = refs[8:12], refs[12]
    for h in range(2):
        full = total([p[...] for p in refs[4 * h : 4 * h + 4]])
        start = h * WIDE[0]
        empty = jnp.zeros((7, WIDE[h]), F32)
        for z in range(4):
            rows = [full[z * 16 : (z + 1) * 16], full[64 + z : 65 + z], empty]
            held[z, :, start : start + WIDE[h]] = jnp.concatenate(rows, axis=0).astype(BF)
    for d in range(4):
        outs[d][...] = held[lax.rem(place[2] + d, 4)]


def final_kernel(place, *refs):
    parts, (hid, order), outs, held = refs[:4], refs[4:6], refs[6:11], refs[11]
    g_up, g_down, g_out, g_qkv, sums = outs
    for d in range(4):
        held[lax.rem(place[2] + 4 - d, 4)] = parts[d][...]
    up = []
    for j in range(4):
        pieces = [held[a, :, j * 256 : (j + 1) * 256] for a in range(4)]
        pieces += [held[a, :, MAIN + j * 16 : MAIN + (j + 1) * 16] for a in range(4)]
        up.append(jnp.concatenate(pieces, axis=1))
    up = matmul(jnp.concatenate(up, axis=0), hid[...])
    up = jnp.concatenate([up[j * 24 : (j + 1) * 24] for j in range(4)], axis=1)
    for i in range(SHARD):
        g_up[i] = up[i : i + 1]
    start = WIDE[0]
    attn = [
        jnp.concatenate([held[a, :, PAD:start], held[a, :, start + PAD :]], axis=1)
        for a in range(4)
    ]
    rows = [held[a, :, start : start + D] for a in range(4)] + [attn[3][:, :D]]
    rows = dot_t(jnp.concatenate(rows, axis=0), order[:D])
    qkv = jnp.concatenate([v[:, :D].astype(F32) for v in attn[:3]], axis=1)
    for i in range(SHARD):
        for a in range(4):
            g_down[a * SHARD + i] = rows[a * 24 + i : a * 24 + i + 1]
        g_out[i] = rows[96 + i : 97 + i]
        g_qkv[i] = qkv[i : i + 1]
    sums[...] = total([v[:SHARD, D:] for v in attn])


def ring(v, axis, d):
    return lax.ppermute(v, axis, [(i, (i + d) % 4) for i in range(4)])


def restore_kernel(place, order, result, dx, acts, grads):
    acts[...] = dot_t(result[...], order[:D]).astype(BF)
    grads[...] = dot_t(dx[...], order[:D]).astype(BF)


def pad_cols(v, width):
    return jnp.pad(v, ((0, 0), (0, width - v.shape[1])))


def body(inputs, cotangent, lengths, vectors, qkv_w, out_w, up_w, up_b, down_w):
    section = lax.axis_index("section")
    mb, rows, _ = inputs.shape
    n = mb * rows
    c = constants()
    order = c["order"]

    outdown = matmul(jnp.concatenate([out_w[0], down_w[0]], axis=0), c["order_d"]).astype(BF)
    hid = matmul(up_w[0].reshape(SHARD * 4, D), c["hid"]).astype(BF).reshape(SHARD, 4, D)
    hid_main = hid[:, :, :MAIN].reshape(SHARD, 4, 4, 256).transpose(0, 2, 1, 3)
    hid_last = hid[:, :, MAIN:].reshape(SHARD, 4, 4, 16).transpose(0, 2, 1, 3)
    hid = jnp.concatenate(
        [
            hid_main.reshape(SHARD, 4, MAIN),
            hid_last.reshape(SHARD, 4, NDP),
            jnp.zeros((SHARD, 4, PAD - D), BF),
        ],
        axis=2,
    )
    shard = [hid.reshape(SHARD, 4 * PAD)]
    shard += [pad_cols(outdown[SHARD * (1 + a) : SHARD * (2 + a)], PAD) for a in range(4)]
    shard += [pad_cols(qkv_w[0][:, i * D : (i + 1) * D], PAD) for i in range(3)]
    shard += [pad_cols(outdown[:SHARD], PAD)]
    shard = jnp.concatenate(shard, axis=1)
    tail = jnp.concatenate([shard[16], vectors[0].reshape(-1), up_b[0]])
    tail = jnp.pad(tail, (0, 16 * TAILW - tail.shape[0])).reshape(16, TAILW)
    sent = jnp.concatenate([shard[:16], tail], axis=1)
    whole = lax.all_gather(sent, ("x", "y", "z"), axis=0, tiled=True)
    tails, vecs, nat = unpack(whole, c)

    ends = jnp.cumsum(lengths[:, 0], axis=1)
    place = jnp.arange(rows, dtype=jnp.int32)
    seg = jnp.sum((place[None, :, None] >= ends[:, None, :]).astype(jnp.int32), axis=2)
    seg = (seg + 8 * jnp.arange(mb, dtype=jnp.int32)[:, None]).reshape(n)
    at = jnp.arange(n, dtype=jnp.int32)
    pairs = ((seg[:, None] == seg[None, :]) & (at[:, None] >= at[None, :])).astype(F32)

    order_d = c["order_d"]
    x0 = matmul(inputs.reshape(n, D), order_d).astype(BF)
    cot = matmul(cotangent.reshape(n, D), order_d).astype(BF)
    place = jnp.stack([lax.axis_index("x"), lax.axis_index("y"), lax.axis_index("z"), section])
    call = functools.partial(
        layer_call,
        whole=whole,
        tails=tails,
        vecs=vecs,
        nat=nat,
        pairs=pairs,
        order=order,
        place=place,
    )

    first = call("fwd", x=x0)
    arrived = lax.ppermute(first["result"], "section", [(0, 1)])
    top = call("both", x=arrived, grad=cot, old=first)
    coming = lax.ppermute(top["dx"], "section", [(1, 0)])
    early = [top["early0"]] + [ring(top[f"early{d}"], "z", d) for d in (1, 3, 2)]
    coming, *early = lax.optimization_barrier((coming, *early))
    branch = jnp.where(section == 0, coming, cot)
    branches = [branch] + [ring(branch, "z", d) for d in (1, 3, 2)]
    kept = {k: first[k] for k in KEPT}
    bwd = call("bwd", x=x0, grad=coming, old={**{k: top[k] for k in BWD_OUT}, **kept})
    late = [bwd["late0"]] + [ring(bwd[f"late{d}"], "z", d) for d in (1, 3, 2)]

    vmem = pltpu.VMEM
    out = local_call(
        products_kernel,
        "products",
        place,
        [bwd["small"]],
        [((4, CHUNK, WIDE[h]), BF) for h in (0, 1) for _ in range(4)],
        [vmem((4, 4, CHUNK, WIDE[h]), BF) for h in (0, 1)]
        + [vmem((4, k, ROWS, PAD), BF) for k in (3, 2)]
        + [vmem((4,) + ROW, BF), pltpu.SemaphoreType.DMA((12,))],
        far=[*early, *late, *branches],
    )
    got = [out[0]] + [ring(out[d], "x", d) for d in (2, 1, 3)]
    after = ring(out[5], "y", 1)
    held, after = lax.optimization_barrier((out[7], after))
    got += [out[4], ring(out[6], "y", 2), after, ring(held, "y", 3)]
    out = local_call(
        first_sum_kernel,
        "first_sum",
        place,
        got,
        [((CHUNK, WIDE[h]), BF) for h in (0, 1) for _ in range(4)],
    )
    got = []
    for h, axis in ((0, "y"), (1, "x")):
        got += [out[4 * h]] + [ring(out[4 * h + d], axis, d) for d in (1, 3, 2)]
    out = local_call(
        second_sum_kernel,
        "second_sum",
        place,
        got,
        [((24, sum(WIDE)), BF)] * 4,
        [vmem((4, 24, sum(WIDE)), BF)],
    )
    got = [out[0]] + [ring(out[d], "z", d) for d in (1, 2, 3)]
    g_up, g_down, g_out, g_qkv, sums = local_call(
        final_kernel,
        "owners",
        place,
        [*got, c["hid_t"], order],
        [
            ((SHARD, 1, FF), F32),
            ((4 * SHARD, 1, D), F32),
            ((SHARD, 1, D), F32),
            ((SHARD, 1, 3 * D), F32),
            ((SHARD, PAD - D), F32),
        ],
        [vmem((4, 24, sum(WIDE)), BF)],
    )
    acts, grads = local_call(
        restore_kernel, "restore", place, [order, top["result"], bwd["dx"]], [(ROW, BF)] * 2
    )
    return (
        acts.reshape(1, mb, rows, D),
        grads.reshape(1, mb, rows, D),
        sums[None, :, :8],
        g_qkv.reshape(1, SHARD, 3 * D),
        g_out.reshape(1, SHARD, D),
        g_up.reshape(1, SHARD, FF),
        sums[:, 8:12].T.reshape(1, 4 * SHARD),
        g_down.reshape(1, 4 * SHARD, D),
    )


def solution(mesh):
    grid = Mesh(mesh.devices.reshape(2, 4, 4, 4), ("section", "x", "y", "z"))
    dp = ("x", "y", "z")
    tokens = P(None, dp, None)
    rows = P("section", dp, None)
    in_specs = (tokens, tokens, tokens, rows, rows, rows, rows, P("section", dp), rows)
    stacks = P("section", None, dp, None)
    out_specs = (stacks, stacks, rows, rows, rows, rows, P("section", dp), rows)
    return jax.shard_map(body, mesh=grid, in_specs=in_specs, out_specs=out_specs, check_vma=False)
```

```python
import functools

import jax
import jax.numpy as jnp
import numpy as np
from jax import lax
from jax.experimental import pallas as pl
from jax.experimental.pallas import tpu as pltpu
from jax.sharding import Mesh, PartitionSpec as P

HEADS = 17
HDIM = 64
D = HEADS * HDIM
FF = 4 * D
SHARD = 17
NDP = 64
MAIN = 16 * NDP
PAD = 1152
ROWS = 128
PAIRS = PAD // 128

UP, DOWN, QKV, OUT, BLOCKS = 0, 4, 8, 11, 12
TAIL0 = BLOCKS * PAD
TAILW = 896
WIDTH = TAIL0 + TAILW
SMALLS = 256

NORM_EPSILON = 1e-05
SCORE_SCALE = 0.125
GELU_C = float(np.sqrt(2 / np.pi))
GELU_A = 0.044715
BF = jnp.bfloat16
F32 = jnp.float32
WINDOW = 4
VMEM_BYTES = 58 * 1024 * 1024


def constants():
    n = np.arange(D)
    shard_of = np.where(n < MAIN, n // 16, n - MAIN)
    row_of = np.where(n < MAIN, n % 16, 16)
    order = np.zeros((PAD, D), np.float32)
    order[shard_of * SHARD + row_of, n] = 1
    f = np.arange(D)
    s, a, r = f // 68, (f % 68) // SHARD, f % SHARD
    hid = np.zeros((D, D), np.float32)
    hid[f, np.where(r < 16, a * 256 + s * 16 + r, 1024 + a * 16 + s)] = 1
    k = np.arange(SMALLS)
    is_vec, is_up = k < 136, (k >= 136) & (k < 204)
    k_row = np.where(is_vec, k // 8, np.where(is_up, (k - 136) % SHARD, -1))
    k_out = np.where(is_vec, k % 8, np.where(is_up, 8 + (k - 136) // SHARD, -1))
    pick = (k_out[None, :] == np.arange(16)[:, None]).astype(np.float32)
    spread = (np.arange(NDP)[:, None] == shard_of[None, :]).astype(np.float32)
    keep = (k_row[:, None] == row_of[None, :]).astype(np.float32)
    nat = np.arange(PAD)
    spread_nat = (np.arange(NDP)[:, None] == nat[None, :] // SHARD).astype(np.float32)
    keep_nat = (k_row[:, None] == nat[None, :] % SHARD).astype(np.float32)
    m = np.arange(MAIN)
    turn = np.zeros((MAIN, MAIN), np.float32)
    turn[(m % 16) * NDP + m // 16, m] = 1
    names = ("order", "hid", "pick", "spread", "keep", "spread_nat", "keep_nat", "turn")
    values = (order, hid, pick, spread, keep, spread_nat, keep_nat, turn)
    found = {name: jnp.asarray(value, BF) for name, value in zip(names, values)}
    found["order_d"] = jnp.asarray(order[:D], BF)
    found["hid_t"] = jnp.asarray(hid.T, BF)
    return found


def matmul(a, b):
    return jnp.dot(a, b, preferred_element_type=F32)


def dot_t(a, b):
    return lax.dot_general(a, b, (((1,), (1,)), ((), ())), preferred_element_type=F32)


def t_dot(a, b):
    return lax.dot_general(a, b, (((0,), (0,)), ((), ())), preferred_element_type=F32)


def norm_parts(features):
    centred = features - jnp.mean(features, axis=-1, keepdims=True)
    inverse = lax.rsqrt(jnp.mean(centred * centred, axis=-1, keepdims=True) + NORM_EPSILON)
    return centred * inverse, inverse


def norm_back(gradient, normed, inverse, gain):
    scaled = gradient * gain
    centred = scaled - jnp.mean(scaled, axis=-1, keepdims=True)
    return inverse * (centred - normed * jnp.mean(scaled * normed, axis=-1, keepdims=True))


def col_sum(v):
    return jnp.sum(v, axis=0, keepdims=True)


def unpack_kernel(whole, pick, spread, keep, spread_nat, keep_nat, turn, tails, vecs, nat, raw, sem):
    copy = pltpu.make_async_copy(whole.at[:, pl.ds(TAIL0, TAILW)], raw, sem)
    copy.start()
    copy.wait()
    turned = matmul(turn[...], raw[...]).astype(BF)
    for j in range(16):
        tails[:, j * TAILW : (j + 1) * TAILW] = turned[j * NDP : (j + 1) * NDP]
    small = tails[:, TAIL0 : TAIL0 + SMALLS]
    for out, s, k in ((vecs, spread, keep), (nat, spread_nat, keep_nat)):
        wide = t_dot(small, s[...]) * k[...].astype(F32)
        out[...] = matmul(pick[...], wide.astype(BF))


def unpack(whole, c):
    vm = pl.BlockSpec(memory_space=pltpu.VMEM)
    return pl.pallas_call(
        unpack_kernel,
        in_specs=[pl.BlockSpec(memory_space=pl.ANY)] + [vm] * 6,
        out_specs=[vm] * 3,
        out_shape=[
            jax.ShapeDtypeStruct((NDP, 16 * TAILW), BF),
            jax.ShapeDtypeStruct((16, D), F32),
            jax.ShapeDtypeStruct((16, PAD), F32),
        ],
        scratch_shapes=[pltpu.VMEM((MAIN, TAILW), BF), pltpu.SemaphoreType.DMA],
        compiler_params=pltpu.CompilerParams(vmem_limit_bytes=VMEM_BYTES),
        name="unpack",
    )(whole, c["pick"], c["spread"], c["keep"], c["spread_nat"], c["keep_nat"], c["turn"])


class Weights:
    def __init__(self, whole, tails, buf, sems, kind):
        self.whole, self.tails, self.buf, self.sems, self.kind = whole, tails, buf, sems, kind

    def block(self, p):
        if self.kind == "bwd":
            pair = (p % 2 == 0) * DOWN + p // 2
            rest = OUT * (p == 8) + (p - 1) * (p > 8)
            return pair * (p < 8) + rest * (p >= 8)
        q = p - 4
        return (p < 4) * (QKV + p) + (p >= 4) * ((q % 2) * DOWN + q // 2)

    def copies(self, p):
        b = self.block(p)
        cols = pl.ds(pl.multiple_of(b * PAD, 128), PAD)
        return (
            pltpu.make_async_copy(
                self.whole.at[:, cols], self.buf.at[b, pl.ds(0, MAIN)], self.sems.at[b, 0]
            ),
            pltpu.make_async_copy(
                self.tails.at[:, cols], self.buf.at[b, pl.ds(MAIN, NDP)], self.sems.at[b, 1]
            ),
        )

    def start(self, p):
        for copy in self.copies(p):
            copy.start()

    def begin(self):
        for p in range(WINDOW):
            self.start(p)

    def wait(self, p):
        for copy in self.copies(p):
            copy.wait()
        if isinstance(p, int):
            if p + WINDOW < BLOCKS:
                self.start(p + WINDOW)
        else:

            @pl.when(p + WINDOW < BLOCKS)
            def _():
                self.start(p + WINDOW)


def pair_masks():
    lane = lax.broadcasted_iota(jnp.int32, (ROWS, 128), 1)
    first = (lane < HDIM).astype(F32)
    return first, 1.0 - first


def stacked(v, masks):
    return jnp.concatenate([(v * m).astype(BF) for m in masks], axis=0)


def soft_pair(q, kk, allowed):
    scores = dot_t(q, kk) * SCORE_SCALE
    halves = []
    for h in range(2):
        s = jnp.where(allowed, scores[:, h * ROWS : (h + 1) * ROWS], -1e30)
        e = jnp.exp(s - jnp.max(s, axis=-1, keepdims=True))
        halves.append(e / jnp.sum(e, axis=-1, keepdims=True))
    return halves


def forward_part(w, send, x_ref, place, pairs_ref, vecs, nat, order, r):
    x = x_ref[...].astype(F32)
    normed, _ = norm_parts(x)
    r["attn_in"][0, :, :D] = (normed * vecs[0:1] + vecs[1:2]).astype(BF)

    def project(i, carry):
        w.wait(i)
        shift = jnp.where(i == 0, nat[2:3], jnp.where(i == 2, nat[3:4], 0.0))
        r["packed"][i] = (matmul(r["attn_in"][0, :, :D], w.buf[QKV + i]) + shift).astype(BF)
        return carry

    lax.fori_loop(0, 3, project, 0)
    send("packed")
    masks = pair_masks()
    allowed = pairs_ref[...] > 0
    for p in range(PAIRS):
        cols = pl.ds(p * 128, 128)
        kk = stacked(r["packed"][1, :, cols].astype(F32), masks)
        vv = stacked(r["packed"][2, :, cols].astype(F32), masks)
        halves = soft_pair(r["packed"][0, :, cols], kk, allowed)
        soft = jnp.concatenate([h.astype(BF) for h in halves], axis=1)
        r["heads"][:, cols] = matmul(soft, vv).astype(BF)
    order.wait()
    mixed = matmul(r["heads"][...], order.ref[...]).astype(BF)
    r["attn_in"][1, :, :D] = mixed
    w.wait(3)
    branch = matmul(mixed, w.buf[OUT])[:, :D]
    middle = x + branch + vecs[4:5]
    r["middle"][...] = middle
    send("middle")
    normed, _ = norm_parts(middle)
    r["second"][:, :D] = (normed * vecs[5:6] + vecs[6:7]).astype(BF)
    r["acc"][...] = jnp.zeros((ROWS, PAD), F32)

    def feed(a, carry):
        w.wait(4 + 2 * a)
        hidden = matmul(r["second"][:, :D], w.buf[UP + a])[:, :D] + vecs[pl.ds(8 + a, 1)]
        r["hidden"][a] = hidden
        bent = jnp.tanh(GELU_C * (hidden + GELU_A * (hidden * hidden * hidden)))
        r["active"][a, :, :D] = (0.5 * hidden * (1.0 + bent)).astype(BF)
        w.wait(5 + 2 * a)
        r["acc"][...] += matmul(r["active"][a, :, :D], w.buf[DOWN + a])
        return carry

    lax.fori_loop(0, 4, feed, 0)
    r["result"][...] = (r["middle"][...] + r["acc"][:, :D] + vecs[7:8]).astype(BF)
    send("hidden")
    send("early")


def backward_part(w, wait, send, grad_ref, x_ref, place, pairs_ref, vecs, order, r):
    grad = grad_ref[...]
    dres = grad.astype(F32)
    r["branch"][:, :D] = grad
    r["acc"][...] = jnp.zeros((ROWS, PAD), F32)

    def feed(a, carry):
        if wait:
            w.wait(2 * a)
        dactive = dot_t(grad_ref[...], w.buf[DOWN + a, :, :D])
        h = r["hidden"][a]
        square = h * h
        bent = jnp.tanh(GELU_C * (h + GELU_A * (square * h)))
        slope = 0.5 * (1.0 + bent) + (0.5 * GELU_C) * h * (1.0 - bent * bent) * (
            1.0 + (3 * GELU_A) * square
        )
        dhidden = (dactive * slope).astype(BF)
        r["dhidden"][a, :, :D] = dhidden
        r["small"][pl.ds(8 + a, 1)] = col_sum(dhidden.astype(F32))
        if wait:
            w.wait(2 * a + 1)
        r["acc"][:, :D] += dot_t(dhidden, w.buf[UP + a, :, :D])
        return carry

    lax.fori_loop(0, 4, feed, 0)
    send("late_first")
    dsecond = r["acc"][:, :D]
    normed, inverse = norm_parts(r["middle"][...])
    r["small"][5:6] = col_sum(dsecond * normed)
    r["small"][6:7] = col_sum(dsecond)
    r["small"][7:8] = col_sum(dres)
    dmiddle = dres + norm_back(dsecond, normed, inverse, vecs[5:6])
    r["middle"][...] = dmiddle
    dattn = dmiddle.astype(BF)
    r["dpacked"][3, :, :D] = dattn
    r["small"][4:5] = col_sum(dattn.astype(F32))
    if wait:
        w.wait(8)
    dmixed = dot_t(dattn, w.buf[OUT, :, :D]).astype(BF)
    if wait:
        order.wait()
    r["heads"][...] = dot_t(dmixed, order.ref[...]).astype(BF)
    masks = pair_masks()
    allowed = pairs_ref[...] > 0
    for p in range(PAIRS):
        cols = pl.ds(p * 128, 128)
        width = min(D - p * 128, 128)
        live = pl.ds(p * 128, width)
        q = r["packed"][0, :, cols]
        kk = stacked(r["packed"][1, :, cols].astype(F32), masks)
        vv = stacked(r["packed"][2, :, cols].astype(F32), masks)
        dm = r["heads"][:, cols]
        halves = soft_pair(q, kk, allowed)
        dsoft = dot_t(dm, vv)
        dscores = []
        for h, p_half in enumerate(halves):
            d_half = dsoft[:, h * ROWS : (h + 1) * ROWS]
            centre = jnp.sum(d_half * p_half, axis=-1, keepdims=True)
            dscores.append((p_half * (d_half - centre)).astype(BF))
        ds = jnp.concatenate(dscores, axis=1)
        soft = jnp.concatenate([h.astype(BF) for h in halves], axis=1)
        dq = matmul(ds, kk) * SCORE_SCALE
        dk = t_dot(ds, q) * SCORE_SCALE
        dv = t_dot(soft, dm)
        dk = dk[:ROWS] * masks[0] + dk[ROWS:] * masks[1]
        dv = dv[:ROWS] * masks[0] + dv[ROWS:] * masks[1]
        for i, v in enumerate((dq, dk, dv)):
            r["dpacked"][i, :, live] = v[:, :width].astype(BF)
    send("late_second")
    sums = [col_sum(r["dpacked"][i, :, :D].astype(F32)) for i in (0, 2)]
    sums = jnp.concatenate(sums + [jnp.zeros((14, D), F32)], axis=0).astype(BF)
    r["small"][2:4] = matmul(sums, order.ref[:D])[:2]
    r["acc"][...] = jnp.zeros((ROWS, PAD), F32)

    def project(i, carry):
        if wait:
            w.wait(9 + i)
        r["acc"][:, :D] += dot_t(r["dpacked"][i, :, :D], w.buf[QKV + i, :, :D])
        return carry

    lax.fori_loop(0, 3, project, 0)
    dentry = r["acc"][:, :D]
    normed, inverse = norm_parts(x_ref[...].astype(F32))
    r["small"][0:1] = col_sum(dentry * normed)
    r["small"][1:2] = col_sum(dentry)
    r["small"][12:16] = jnp.zeros((4, D), F32)
    r["dx"][...] = (r["middle"][...] + norm_back(dentry, normed, inverse, vecs[0:1])).astype(BF)


ROW = (ROWS, D)
WIDEROW = (ROWS, PAD)
KEPT = {
    "packed": ((3,) + WIDEROW, BF),
    "middle": (ROW, F32),
    "hidden": ((4,) + ROW, F32),
}
EARLY = {f"early{d}": ((3,) + WIDEROW, BF) for d in range(4)}
LATE = {f"late{d}": ((3,) + WIDEROW, BF) for d in range(4)}
RESULT = {"result": (ROW, BF)}
GRADS = {"dx": (ROW, BF), "small": ((16, D), F32)}
FWD_WORK = {
    "attn_in": ((2,) + WIDEROW, BF),
    "second": (WIDEROW, BF),
    "active": ((4,) + WIDEROW, BF),
}
BWD_WORK = {
    "dhidden": ((4,) + WIDEROW, BF),
    "dpacked": ((4,) + WIDEROW, BF),
    "branch": (WIDEROW, BF),
}
WORK = {"heads": (WIDEROW, BF), "acc": (WIDEROW, F32)}


class Fetched:
    def __init__(self, source, ref, sem):
        self.ref, self.copy = ref, pltpu.make_async_copy(source, ref, sem)

    def start(self):
        self.copy.start()

    def wait(self):
        self.copy.wait()


def layer_call(kind, whole, tails, vecs, nat, pairs, order, place, x, grad=None, old=None):
    near_out = {"fwd": RESULT, "both": {**RESULT, **GRADS}, "bwd": GRADS}[kind]
    far_out = {"fwd": {**EARLY, **KEPT}, "both": {**EARLY, **LATE}, "bwd": LATE}[kind]
    outs = {**near_out, **far_out}
    work = {**WORK, **KEPT}
    if kind != "bwd":
        work.update(FWD_WORK)
    if kind != "fwd":
        work.update(BWD_WORK)
    passed = {"fwd": {}, "both": {**RESULT, **EARLY}, "bwd": {**GRADS, **LATE}}[kind]
    loaded = KEPT if kind == "bwd" else {}
    far = [whole, tails, order] + [old[k] for k in (*passed, *loaded)]
    near = [vecs, nat, pairs, x] + ([] if grad is None else [grad])
    section = 1 if kind == "both" else 0

    def kernel(place_ref, *refs):
        far_refs, refs = refs[: len(far)], refs[len(far) :]
        near_refs, refs = refs[: len(near)], refs[len(near) :]
        out = dict(zip(outs, refs))
        refs = refs[len(outs) :]
        r = {**dict(zip(work, refs)), **{k: out[k] for k in near_out}}
        buf, order_buf, sems, old_sems, order_sem, out_sems = refs[len(work) :]
        w = Weights(far_refs[0], far_refs[1], buf, sems, kind)
        order_in = Fetched(far_refs[2], order_buf, order_sem)
        vecs_ref, nat_ref, pairs_ref, x_ref = near_refs[:4]
        old_refs = dict(zip((*passed, *loaded), far_refs[3:]))
        sent = []

        def send(name):
            if name in KEPT:
                moves = [(r[name], out[name])] if name in out else []
            else:
                moves = []
                for d in range(4):
                    z = lax.rem(place_ref[2] + d, 4)
                    if name == "early":
                        sources = (r["second"], r["active"].at[z], r["attn_in"].at[z // 3])
                        moves += [(v, out[f"early{d}"].at[i]) for i, v in enumerate(sources)]
                    elif name == "late_first":
                        moves.append((r["branch"], out[f"late{d}"].at[0]))
                        moves.append((r["dhidden"].at[z], out[f"late{d}"].at[1]))
                    else:
                        moves.append((r["dpacked"].at[z], out[f"late{d}"].at[2]))
            for source, target in moves:
                copy = pltpu.make_async_copy(source, target, out_sems.at[len(sent)])
                copy.start()
                sent.append(copy)

        @pl.when(place_ref[3] == section)
        def _():
            fetched = [
                Fetched(old_refs[k], r[k], old_sems.at[i]) for i, k in enumerate(loaded)
            ]
            for copy in fetched:
                copy.start()
            w.begin()
            order_in.start()
            if kind != "bwd":
                forward_part(
                    w, send, x_ref, place_ref, pairs_ref, vecs_ref, nat_ref, order_in, r
                )
            for copy in fetched:
                copy.wait()
            if kind != "fwd":
                backward_part(
                    w,
                    kind == "bwd",
                    send,
                    near_refs[4],
                    x_ref,
                    place_ref,
                    pairs_ref,
                    vecs_ref,
                    order_in,
                    r,
                )
            for copy in sent:
                copy.wait()

        if passed:

            @pl.when(place_ref[3] != section)
            def _():
                copies = [
                    pltpu.make_async_copy(old_refs[k], out[k], old_sems.at[i])
                    for i, k in enumerate(passed)
                ]
                for copy in copies:
                    copy.start()
                for copy in copies:
                    copy.wait()

    vm = pl.BlockSpec(memory_space=pltpu.VMEM)
    hbm = pl.BlockSpec(memory_space=pl.ANY)
    results = pl.pallas_call(
        kernel,
        in_specs=[pl.BlockSpec(memory_space=pltpu.SMEM)] + [hbm] * len(far) + [vm] * len(near),
        out_specs=[vm] * len(near_out) + [hbm] * len(far_out),
        out_shape=[jax.ShapeDtypeStruct(s, t) for s, t in outs.values()],
        scratch_shapes=[pltpu.VMEM(s, t) for s, t in work.values()]
        + [
            pltpu.VMEM((BLOCKS, D, PAD), BF),
            pltpu.VMEM((PAD, D), BF),
            pltpu.SemaphoreType.DMA((BLOCKS, 2)),
            pltpu.SemaphoreType.DMA((8,)),
            pltpu.SemaphoreType.DMA,
            pltpu.SemaphoreType.DMA((32,)),
        ],
        compiler_params=pltpu.CompilerParams(vmem_limit_bytes=VMEM_BYTES),
        cost_estimate=pl.CostEstimate(
            flops={"fwd": 4, "both": 12, "bwd": 8}[kind] * 10**9,
            bytes_accessed=BLOCKS * D * PAD * 2,
            transcendentals=10**6,
        ),
        name="layer_" + kind,
    )(place, *far, *near)
    return dict(zip(outs, results))


CHUNK = 72
HALF = 768
WIDE = (PAD + HALF, PAD + PAD - HALF)


def local_call(kernel, name, place, ins, out_shapes, scratch=(), far=(), far_out=False):
    vm = pl.BlockSpec(memory_space=pltpu.VMEM)
    hbm = pl.BlockSpec(memory_space=pl.ANY)
    return pl.pallas_call(
        kernel,
        in_specs=[pl.BlockSpec(memory_space=pltpu.SMEM)] + [hbm] * len(far) + [vm] * len(ins),
        out_specs=[hbm if far_out else vm] * len(out_shapes),
        out_shape=[jax.ShapeDtypeStruct(s, t) for s, t in out_shapes],
        scratch_shapes=list(scratch),
        compiler_params=pltpu.CompilerParams(vmem_limit_bytes=VMEM_BYTES),
        name=name,
    )(place, *far, *ins)


def products_kernel(place, *refs):
    given, small, outs = refs[:8], refs[8], refs[9:17]
    first, second, early, late, sems, out_sems = refs[17:]
    copies = {}
    for i, v in ((1, 0), (0, 1), (1, 1), (0, 0), (0, 2), (1, 2)):
        held, source = ((early, given[:4]), (late, given[4:]))[i]
        copies[i, v] = [
            pltpu.make_async_copy(source[d].at[v], held.at[d, v], sems.at[i, v, d])
            for d in range(4)
        ]
        for copy in copies[i, v]:
            copy.start()

    def rows_of(i, v):
        for copy in copies[i, v]:
            copy.wait()
        return jnp.concatenate([(early, late)[i][d, v, :, :D] for d in range(4)], axis=0)

    gap = jnp.zeros((4 * ROWS, PAD - D), BF)
    slot = lax.broadcasted_iota(jnp.int32, (16, PAD), 1) - D
    unit = (slot == lax.broadcasted_iota(jnp.int32, (16, PAD), 0)).astype(F32).astype(BF)
    nothing = jnp.zeros((4, PAD), F32)

    def product(a, b, store):
        last = t_dot(a[:, MAIN:], b)
        for x in range(4):
            main = t_dot(a[:, x * 256 : (x + 1) * 256], b)
            for y in range(4):
                at = (x * 4 + y) * 4
                rows = [main[y * 64 : (y + 1) * 64], last[at : at + 4], nothing]
                store(x, y, jnp.concatenate(rows, axis=0).astype(BF))

    def store_up(x, y, v):
        first[x, y, :, :PAD] = v

    def store_down(x, y, v):
        second[y, x, :, :PAD] = v

    def store_attn(x, y, v):
        first[x, y, :, PAD:] = v[:, :HALF]
        second[y, x, :, PAD:] = v[:, HALF:]

    def wide(v):
        return jnp.concatenate([v, gap], axis=1)

    sent = []

    def send(h, start, size):
        held = (first, second)[h]
        for d in range(4):
            cols = pl.ds(start, size)
            source = held.at[lax.rem(place[h] + d, 4), :, :, cols]
            copy = pltpu.make_async_copy(
                source, outs[4 * h + d].at[:, :, cols], out_sems.at[len(sent)]
            )
            copy.start()
            sent.append(copy)

    product(rows_of(0, 1), wide(rows_of(1, 0)), store_down)
    send(1, 0, PAD)
    product(rows_of(0, 0), wide(rows_of(1, 1)), store_up)
    send(0, 0, PAD)
    a = jnp.concatenate([rows_of(0, 2), small[...].astype(BF)], axis=0)
    b = jnp.concatenate([wide(rows_of(1, 2)), unit], axis=0)
    product(a, b, store_attn)
    send(0, PAD, HALF)
    send(1, PAD, PAD - HALF)
    for copy in sent:
        copy.wait()


def total(parts):
    return sum((p.astype(F32) for p in parts[1:]), parts[0].astype(F32))


def first_sum_kernel(place, *refs):
    given, outs, held, sems = refs[:8], refs[8:16], refs[16:18], refs[18]
    copies = {}
    for d in range(4):
        for h, other in ((0, 1), (1, 0)):
            i = lax.rem(place[other] + d, 4)
            copies[h, d] = [
                pltpu.make_async_copy(
                    given[4 * h + k].at[i], held[h].at[d, k], sems.at[h, d, k]
                )
                for k in range(4)
            ]
            for copy in copies[h, d]:
                copy.start()
    for d in range(4):
        for h in range(2):
            for copy in copies[h, d]:
                copy.wait()
            outs[4 * h + d][...] = total([held[h][d, k] for k in range(4)]).astype(BF)


def second_sum_kernel(place, *refs):
    outs, held = refs[8:12], refs[12]
    for h in range(2):
        full = total([p[...] for p in refs[4 * h : 4 * h + 4]])
        start = h * WIDE[0]
        empty = jnp.zeros((7, WIDE[h]), F32)
        for z in range(4):
            rows = [full[z * 16 : (z + 1) * 16], full[64 + z : 65 + z], empty]
            held[z, :, start : start + WIDE[h]] = jnp.concatenate(rows, axis=0).astype(BF)
    for d in range(4):
        outs[d][...] = held[lax.rem(place[2] + d, 4)]


def final_kernel(place, *refs):
    hid_in, order_in, parts, outs = refs[0], refs[1], refs[2:6], refs[6:11]
    held, hid, order, sems = refs[11:]
    g_up, g_down, g_out, g_qkv, sums = outs
    hid_copy = pltpu.make_async_copy(hid_in, hid, sems.at[0])
    order_copy = pltpu.make_async_copy(order_in, order, sems.at[1])
    hid_copy.start()
    order_copy.start()
    for d in range(4):
        held[lax.rem(place[2] + 4 - d, 4)] = parts[d][...]
    up = []
    for j in range(4):
        pieces = [held[a, :, j * 256 : (j + 1) * 256] for a in range(4)]
        pieces += [held[a, :, MAIN + j * 16 : MAIN + (j + 1) * 16] for a in range(4)]
        up.append(jnp.concatenate(pieces, axis=1))
    hid_copy.wait()
    up = matmul(jnp.concatenate(up, axis=0), hid[...])
    up = jnp.concatenate([up[j * 24 : (j + 1) * 24] for j in range(4)], axis=1)
    for i in range(SHARD):
        g_up[i] = up[i : i + 1]
    start = WIDE[0]
    attn = [
        jnp.concatenate([held[a, :, PAD:start], held[a, :, start + PAD :]], axis=1)
        for a in range(4)
    ]
    rows = [held[a, :, start : start + D] for a in range(4)] + [attn[3][:, :D]]
    order_copy.wait()
    rows = dot_t(jnp.concatenate(rows, axis=0), order[:D])
    qkv = jnp.concatenate([v[:, :D].astype(F32) for v in attn[:3]], axis=1)
    for i in range(SHARD):
        for a in range(4):
            g_down[a * SHARD + i] = rows[a * 24 + i : a * 24 + i + 1]
        g_out[i] = rows[96 + i : 97 + i]
        g_qkv[i] = qkv[i : i + 1]
    sums[...] = total([v[:SHARD, D:] for v in attn])


def ring(v, axis, d):
    return lax.ppermute(v, axis, [(i, (i + d) % 4) for i in range(4)])


def restore_kernel(place, order, result, dx, acts, grads):
    acts[...] = dot_t(result[...], order[:D]).astype(BF)
    grads[...] = dot_t(dx[...], order[:D]).astype(BF)


def pad_cols(v, width):
    return jnp.pad(v, ((0, 0), (0, width - v.shape[1])))


def body(inputs, cotangent, lengths, vectors, qkv_w, out_w, up_w, up_b, down_w):
    section = lax.axis_index("section")
    mb, rows, _ = inputs.shape
    n = mb * rows
    c = constants()
    order = c["order"]

    outdown = matmul(jnp.concatenate([out_w[0], down_w[0]], axis=0), c["order_d"]).astype(BF)
    hid = matmul(up_w[0].reshape(SHARD * 4, D), c["hid"]).astype(BF).reshape(SHARD, 4, D)
    hid_main = hid[:, :, :MAIN].reshape(SHARD, 4, 4, 256).transpose(0, 2, 1, 3)
    hid_last = hid[:, :, MAIN:].reshape(SHARD, 4, 4, 16).transpose(0, 2, 1, 3)
    hid = jnp.concatenate(
        [
            hid_main.reshape(SHARD, 4, MAIN),
            hid_last.reshape(SHARD, 4, NDP),
            jnp.zeros((SHARD, 4, PAD - D), BF),
        ],
        axis=2,
    )
    shard = [hid.reshape(SHARD, 4 * PAD)]
    shard += [pad_cols(outdown[SHARD * (1 + a) : SHARD * (2 + a)], PAD) for a in range(4)]
    shard += [pad_cols(qkv_w[0][:, i * D : (i + 1) * D], PAD) for i in range(3)]
    shard += [pad_cols(outdown[:SHARD], PAD)]
    shard = jnp.concatenate(shard, axis=1)
    tail = jnp.concatenate([shard[16], vectors[0].reshape(-1), up_b[0]])
    tail = jnp.pad(tail, (0, 16 * TAILW - tail.shape[0])).reshape(16, TAILW)
    sent = jnp.concatenate([shard[:16], tail], axis=1)
    whole = lax.all_gather(sent, ("x", "y", "z"), axis=0, tiled=True)
    tails, vecs, nat = unpack(whole, c)

    ends = jnp.cumsum(lengths[:, 0], axis=1)
    place = jnp.arange(rows, dtype=jnp.int32)
    seg = jnp.sum((place[None, :, None] >= ends[:, None, :]).astype(jnp.int32), axis=2)
    seg = (seg + 8 * jnp.arange(mb, dtype=jnp.int32)[:, None]).reshape(n)
    at = jnp.arange(n, dtype=jnp.int32)
    pairs = ((seg[:, None] == seg[None, :]) & (at[:, None] >= at[None, :])).astype(F32)

    order_d = c["order_d"]
    x0 = matmul(inputs.reshape(n, D), order_d).astype(BF)
    cot = matmul(cotangent.reshape(n, D), order_d).astype(BF)
    place = jnp.stack([lax.axis_index("x"), lax.axis_index("y"), lax.axis_index("z"), section])
    call = functools.partial(
        layer_call,
        whole=whole,
        tails=tails,
        vecs=vecs,
        nat=nat,
        pairs=pairs,
        order=order,
        place=place,
    )

    first = call("fwd", x=x0)
    arrived = lax.ppermute(first["result"], "section", [(0, 1)])
    top = call("both", x=arrived, grad=cot, old=first)
    coming = lax.ppermute(top["dx"], "section", [(1, 0)])
    early = [top["early0"]] + [ring(top[f"early{d}"], "z", d) for d in (1, 3, 2)]
    kept = {k: first[k] for k in KEPT}
    old = {**{k: top[k] for k in (*GRADS, *LATE)}, **kept}
    bwd = call("bwd", x=x0, grad=coming, old=old)
    sends = [bwd[f"late{d}"] for d in (1, 3, 2)]
    early, sends = lax.optimization_barrier((early, sends))
    late = [bwd["late0"]] + [ring(v, "z", d) for v, d in zip(sends, (1, 3, 2))]

    vmem, sem = pltpu.VMEM, pltpu.SemaphoreType.DMA
    out = local_call(
        products_kernel,
        "products",
        place,
        [bwd["small"]],
        [((4, CHUNK, WIDE[h]), BF) for h in (0, 1) for _ in range(4)],
        [vmem((4, 4, CHUNK, WIDE[h]), BF) for h in (0, 1)]
        + [vmem((4, 3) + WIDEROW, BF)] * 2
        + [sem((2, 3, 4)), sem((16,))],
        far=[*early, *late],
        far_out=True,
    )
    got = [out[0]] + [ring(out[d], "x", d) for d in (2, 1, 3)]
    after = ring(out[5], "y", 1)
    held, after = lax.optimization_barrier((out[7], after))
    got += [out[4], ring(out[6], "y", 2), after, ring(held, "y", 3)]
    out = local_call(
        first_sum_kernel,
        "first_sum",
        place,
        [],
        [((CHUNK, WIDE[h]), BF) for h in (0, 1) for _ in range(4)],
        [vmem((4, 4, CHUNK, WIDE[h]), BF) for h in (0, 1)] + [sem((2, 4, 4))],
        far=got,
    )
    got = []
    for h, axis in ((0, "y"), (1, "x")):
        got += [out[4 * h]] + [ring(out[4 * h + d], axis, d) for d in (1, 3, 2)]
    out = local_call(
        second_sum_kernel,
        "second_sum",
        place,
        got,
        [((24, sum(WIDE)), BF)] * 4,
        [vmem((4, 24, sum(WIDE)), BF)],
    )
    got = [out[0]] + [ring(out[d], "z", d) for d in (1, 2, 3)]
    g_up, g_down, g_out, g_qkv, sums = local_call(
        final_kernel,
        "owners",
        place,
        got,
        [
            ((SHARD, 1, FF), F32),
            ((4 * SHARD, 1, D), F32),
            ((SHARD, 1, D), F32),
            ((SHARD, 1, 3 * D), F32),
            ((SHARD, PAD - D), F32),
        ],
        [
            vmem((4, 24, sum(WIDE)), BF),
            vmem((D, D), BF),
            vmem((PAD, D), BF),
            pltpu.SemaphoreType.DMA((2,)),
        ],
        far=[c["hid_t"], order],
    )
    acts, grads = local_call(
        restore_kernel, "restore", place, [order, top["result"], bwd["dx"]], [(ROW, BF)] * 2
    )
    return (
        acts.reshape(1, mb, rows, D),
        grads.reshape(1, mb, rows, D),
        sums[None, :, :8],
        g_qkv.reshape(1, SHARD, 3 * D),
        g_out.reshape(1, SHARD, D),
        g_up.reshape(1, SHARD, FF),
        sums[:, 8:12].T.reshape(1, 4 * SHARD),
        g_down.reshape(1, 4 * SHARD, D),
    )


def solution(mesh):
    grid = Mesh(mesh.devices.reshape(2, 4, 4, 4), ("section", "x", "y", "z"))
    dp = ("x", "y", "z")
    tokens = P(None, dp, None)
    rows = P("section", dp, None)
    in_specs = (tokens, tokens, tokens, rows, rows, rows, rows, P("section", dp), rows)
    stacks = P("section", None, dp, None)
    out_specs = (stacks, stacks, rows, rows, rows, rows, P("section", dp), rows)
    return jax.shard_map(body, mesh=grid, in_specs=in_specs, out_specs=out_specs, check_vma=False)
```

```python
import functools

import jax
import jax.numpy as jnp
import numpy as np
from jax import lax
from jax.experimental import pallas as pl
from jax.experimental.pallas import tpu as pltpu
from jax.sharding import Mesh, PartitionSpec as P

HEADS = 17
HDIM = 64
D = HEADS * HDIM
FF = 4 * D
SHARD = 17
NDP = 64
MAIN = 16 * NDP
PAD = 1152
ROWS = 128
PAIRS = PAD // 128

UP, DOWN, QKV, OUT, BLOCKS = 0, 4, 8, 11, 12
TAIL0 = BLOCKS * PAD
TAILW = 896
WIDTH = TAIL0 + TAILW
SMALLS = 256

NORM_EPSILON = 1e-05
SCORE_SCALE = 0.125
GELU_C = float(np.sqrt(2 / np.pi))
GELU_A = 0.044715
BF = jnp.bfloat16
F32 = jnp.float32
WINDOW = 3
VMEM_BYTES = 58 * 1024 * 1024


def constants():
    n = np.arange(D)
    shard_of = np.where(n < MAIN, n // 16, n - MAIN)
    row_of = np.where(n < MAIN, n % 16, 16)
    order = np.zeros((PAD, D), np.float32)
    order[shard_of * SHARD + row_of, n] = 1
    f = np.arange(D)
    s, a, r = f // 68, (f % 68) // SHARD, f % SHARD
    hid = np.zeros((D, D), np.float32)
    hid[f, np.where(r < 16, a * 256 + s * 16 + r, 1024 + a * 16 + s)] = 1
    k = np.arange(SMALLS)
    is_vec, is_up = k < 136, (k >= 136) & (k < 204)
    k_row = np.where(is_vec, k // 8, np.where(is_up, (k - 136) % SHARD, -1))
    k_out = np.where(is_vec, k % 8, np.where(is_up, 8 + (k - 136) // SHARD, -1))
    pick = (k_out[None, :] == np.arange(16)[:, None]).astype(np.float32)
    spread = (np.arange(NDP)[:, None] == shard_of[None, :]).astype(np.float32)
    keep = (k_row[:, None] == row_of[None, :]).astype(np.float32)
    nat = np.arange(PAD)
    spread_nat = (np.arange(NDP)[:, None] == nat[None, :] // SHARD).astype(np.float32)
    keep_nat = (k_row[:, None] == nat[None, :] % SHARD).astype(np.float32)
    m = np.arange(MAIN)
    turn = np.zeros((MAIN, MAIN), np.float32)
    turn[(m % 16) * NDP + m // 16, m] = 1
    names = ("order", "hid", "pick", "spread", "keep", "spread_nat", "keep_nat", "turn")
    values = (order, hid, pick, spread, keep, spread_nat, keep_nat, turn)
    found = {name: jnp.asarray(value, BF) for name, value in zip(names, values)}
    found["order_d"] = jnp.asarray(order[:D], BF)
    found["hid_t"] = jnp.asarray(hid.T, BF)
    return found


def matmul(a, b):
    return jnp.dot(a, b, preferred_element_type=F32)


def dot_t(a, b):
    return lax.dot_general(a, b, (((1,), (1,)), ((), ())), preferred_element_type=F32)


def t_dot(a, b):
    return lax.dot_general(a, b, (((0,), (0,)), ((), ())), preferred_element_type=F32)


def norm_parts(features):
    centred = features - jnp.mean(features, axis=-1, keepdims=True)
    inverse = lax.rsqrt(jnp.mean(centred * centred, axis=-1, keepdims=True) + NORM_EPSILON)
    return centred * inverse, inverse


def norm_back(gradient, normed, inverse, gain):
    scaled = gradient * gain
    centred = scaled - jnp.mean(scaled, axis=-1, keepdims=True)
    return inverse * (centred - normed * jnp.mean(scaled * normed, axis=-1, keepdims=True))


def col_sum(v):
    return jnp.sum(v, axis=0, keepdims=True)


def unpack_kernel(whole, pick, spread, keep, spread_nat, keep_nat, turn, tails, vecs, nat, raw, sem):
    copy = pltpu.make_async_copy(whole.at[:, pl.ds(TAIL0, TAILW)], raw, sem)
    copy.start()
    copy.wait()
    turned = matmul(turn[...], raw[...]).astype(BF)
    for j in range(16):
        tails[:, j * TAILW : (j + 1) * TAILW] = turned[j * NDP : (j + 1) * NDP]
    small = tails[:, TAIL0 : TAIL0 + SMALLS]
    for out, s, k in ((vecs, spread, keep), (nat, spread_nat, keep_nat)):
        wide = t_dot(small, s[...]) * k[...].astype(F32)
        out[...] = matmul(pick[...], wide.astype(BF))


def unpack(whole, c):
    vm = pl.BlockSpec(memory_space=pltpu.VMEM)
    return pl.pallas_call(
        unpack_kernel,
        in_specs=[pl.BlockSpec(memory_space=pl.ANY)] + [vm] * 6,
        out_specs=[vm] * 3,
        out_shape=[
            jax.ShapeDtypeStruct((NDP, 16 * TAILW), BF),
            jax.ShapeDtypeStruct((16, D), F32),
            jax.ShapeDtypeStruct((16, PAD), F32),
        ],
        scratch_shapes=[pltpu.VMEM((MAIN, TAILW), BF), pltpu.SemaphoreType.DMA],
        compiler_params=pltpu.CompilerParams(vmem_limit_bytes=VMEM_BYTES),
        name="unpack",
    )(whole, c["pick"], c["spread"], c["keep"], c["spread_nat"], c["keep_nat"], c["turn"])


class Weights:
    def __init__(self, whole, tails, buf, sems, kind):
        self.whole, self.tails, self.buf, self.sems, self.kind = whole, tails, buf, sems, kind

    def block(self, p):
        if self.kind == "bwd":
            pair = (p % 2 == 0) * DOWN + p // 2
            rest = OUT * (p == 8) + (p - 1) * (p > 8)
            return pair * (p < 8) + rest * (p >= 8)
        q = p - 4
        return (p < 4) * (QKV + p) + (p >= 4) * ((q % 2) * DOWN + q // 2)

    def copies(self, p):
        b = self.block(p)
        cols = pl.ds(pl.multiple_of(b * PAD, 128), PAD)
        return (
            pltpu.make_async_copy(
                self.whole.at[:, cols], self.buf.at[b, pl.ds(0, MAIN)], self.sems.at[b, 0]
            ),
            pltpu.make_async_copy(
                self.tails.at[:, cols], self.buf.at[b, pl.ds(MAIN, NDP)], self.sems.at[b, 1]
            ),
        )

    def start(self, p):
        for copy in self.copies(p):
            copy.start()

    def begin(self):
        for p in range(WINDOW):
            self.start(p)

    def wait(self, p):
        for copy in self.copies(p):
            copy.wait()
        if isinstance(p, int):
            if p + WINDOW < BLOCKS:
                self.start(p + WINDOW)
        else:

            @pl.when(p + WINDOW < BLOCKS)
            def _():
                self.start(p + WINDOW)


def pair_masks():
    lane = lax.broadcasted_iota(jnp.int32, (ROWS, 128), 1)
    first = (lane < HDIM).astype(F32)
    return first, 1.0 - first


def stacked(v, masks):
    return jnp.concatenate([(v * m).astype(BF) for m in masks], axis=0)


def soft_pair(q, kk, allowed):
    scores = dot_t(q, kk) * SCORE_SCALE
    halves = []
    for h in range(2):
        s = jnp.where(allowed, scores[:, h * ROWS : (h + 1) * ROWS], -1e30)
        e = jnp.exp(s - jnp.max(s, axis=-1, keepdims=True))
        halves.append(e / jnp.sum(e, axis=-1, keepdims=True))
    return halves


def forward_part(w, send, x_ref, place, pairs_ref, vecs, nat, order, r):
    x = x_ref[...].astype(F32)
    normed, _ = norm_parts(x)
    r["attn_in"][0, :, :D] = (normed * vecs[0:1] + vecs[1:2]).astype(BF)

    def project(i, carry):
        w.wait(i)
        shift = jnp.where(i == 0, nat[2:3], jnp.where(i == 2, nat[3:4], 0.0))
        r["packed"][i] = (matmul(r["attn_in"][0, :, :D], w.buf[QKV + i]) + shift).astype(BF)
        return carry

    lax.fori_loop(0, 3, project, 0)
    send("packed")
    masks = pair_masks()
    allowed = pairs_ref[...] > 0
    for p in range(PAIRS):
        cols = pl.ds(p * 128, 128)
        kk = stacked(r["packed"][1, :, cols].astype(F32), masks)
        vv = stacked(r["packed"][2, :, cols].astype(F32), masks)
        halves = soft_pair(r["packed"][0, :, cols], kk, allowed)
        soft = jnp.concatenate([h.astype(BF) for h in halves], axis=1)
        r["heads"][:, cols] = matmul(soft, vv).astype(BF)
    order.wait()
    mixed = matmul(r["heads"][...], order.ref[...]).astype(BF)
    r["attn_in"][1, :, :D] = mixed
    w.wait(3)
    branch = matmul(mixed, w.buf[OUT])[:, :D]
    middle = x + branch + vecs[4:5]
    r["middle"][...] = middle
    send("middle")
    normed, _ = norm_parts(middle)
    r["second"][:, :D] = (normed * vecs[5:6] + vecs[6:7]).astype(BF)
    r["acc"][...] = jnp.zeros((ROWS, PAD), F32)

    def feed(a, carry):
        w.wait(4 + 2 * a)
        hidden = matmul(r["second"][:, :D], w.buf[UP + a])[:, :D] + vecs[pl.ds(8 + a, 1)]
        r["hidden"][a] = hidden
        bent = jnp.tanh(GELU_C * (hidden + GELU_A * (hidden * hidden * hidden)))
        r["active"][a, :, :D] = (0.5 * hidden * (1.0 + bent)).astype(BF)
        w.wait(5 + 2 * a)
        r["acc"][...] += matmul(r["active"][a, :, :D], w.buf[DOWN + a])
        return carry

    lax.fori_loop(0, 4, feed, 0)
    r["result"][...] = (r["middle"][...] + r["acc"][:, :D] + vecs[7:8]).astype(BF)
    send("hidden")
    send("early")


def backward_part(w, wait, send, grad_ref, x_ref, place, pairs_ref, vecs, order, r):
    grad = grad_ref[...]
    dres = grad.astype(F32)
    r["acc"][...] = jnp.zeros((ROWS, PAD), F32)

    def feed(a, carry):
        if wait:
            w.wait(2 * a)
        dactive = dot_t(grad_ref[...], w.buf[DOWN + a, :, :D])
        h = r["hidden"][a]
        square = h * h
        bent = jnp.tanh(GELU_C * (h + GELU_A * (square * h)))
        slope = 0.5 * (1.0 + bent) + (0.5 * GELU_C) * h * (1.0 - bent * bent) * (
            1.0 + (3 * GELU_A) * square
        )
        dhidden = (dactive * slope).astype(BF)
        r["dhidden"][a, :, :D] = dhidden
        r["small"][pl.ds(8 + a, 1)] = col_sum(dhidden.astype(F32))
        if wait:
            w.wait(2 * a + 1)
        r["acc"][:, :D] += dot_t(dhidden, w.buf[UP + a, :, :D])
        return carry

    lax.fori_loop(0, 4, feed, 0)
    send("late_first")
    dsecond = r["acc"][:, :D]
    normed, inverse = norm_parts(r["middle"][...])
    r["small"][5:6] = col_sum(dsecond * normed)
    r["small"][6:7] = col_sum(dsecond)
    r["small"][7:8] = col_sum(dres)
    dmiddle = dres + norm_back(dsecond, normed, inverse, vecs[5:6])
    r["middle"][...] = dmiddle
    dattn = dmiddle.astype(BF)
    r["dpacked"][3, :, :D] = dattn
    r["small"][4:5] = col_sum(dattn.astype(F32))
    if wait:
        w.wait(8)
    dmixed = dot_t(dattn, w.buf[OUT, :, :D]).astype(BF)
    if wait:
        order.wait()
    r["heads"][...] = dot_t(dmixed, order.ref[...]).astype(BF)
    masks = pair_masks()
    allowed = pairs_ref[...] > 0
    for p in range(PAIRS):
        cols = pl.ds(p * 128, 128)
        width = min(D - p * 128, 128)
        live = pl.ds(p * 128, width)
        q = r["packed"][0, :, cols]
        kk = stacked(r["packed"][1, :, cols].astype(F32), masks)
        vv = stacked(r["packed"][2, :, cols].astype(F32), masks)
        dm = r["heads"][:, cols]
        halves = soft_pair(q, kk, allowed)
        dsoft = dot_t(dm, vv)
        dscores = []
        for h, p_half in enumerate(halves):
            d_half = dsoft[:, h * ROWS : (h + 1) * ROWS]
            centre = jnp.sum(d_half * p_half, axis=-1, keepdims=True)
            dscores.append((p_half * (d_half - centre)).astype(BF))
        ds = jnp.concatenate(dscores, axis=1)
        soft = jnp.concatenate([h.astype(BF) for h in halves], axis=1)
        dq = matmul(ds, kk) * SCORE_SCALE
        dk = t_dot(ds, q) * SCORE_SCALE
        dv = t_dot(soft, dm)
        dk = dk[:ROWS] * masks[0] + dk[ROWS:] * masks[1]
        dv = dv[:ROWS] * masks[0] + dv[ROWS:] * masks[1]
        for i, v in enumerate((dq, dk, dv)):
            r["dpacked"][i, :, live] = v[:, :width].astype(BF)
    send("late_second")
    sums = [col_sum(r["dpacked"][i, :, :D].astype(F32)) for i in (0, 2)]
    sums = jnp.concatenate(sums + [jnp.zeros((14, D), F32)], axis=0).astype(BF)
    r["small"][2:4] = matmul(sums, order.ref[:D])[:2]
    r["acc"][...] = jnp.zeros((ROWS, PAD), F32)

    def project(i, carry):
        if wait:
            w.wait(9 + i)
        r["acc"][:, :D] += dot_t(r["dpacked"][i, :, :D], w.buf[QKV + i, :, :D])
        return carry

    lax.fori_loop(0, 3, project, 0)
    dentry = r["acc"][:, :D]
    normed, inverse = norm_parts(x_ref[...].astype(F32))
    r["small"][0:1] = col_sum(dentry * normed)
    r["small"][1:2] = col_sum(dentry)
    r["small"][12:16] = jnp.zeros((4, D), F32)
    r["dx"][...] = (r["middle"][...] + norm_back(dentry, normed, inverse, vecs[0:1])).astype(BF)


ROW = (ROWS, D)
WIDEROW = (ROWS, PAD)
KEPT = {
    "packed": ((3,) + WIDEROW, BF),
    "middle": (ROW, F32),
    "hidden": ((4,) + ROW, F32),
}
EARLY = {f"early{d}": ((3,) + WIDEROW, BF) for d in range(4)}
LATE = {f"late{d}": ((2,) + WIDEROW, BF) for d in range(4)}
RESULT = {"result": (ROW, BF)}
GRADS = {"dx": (ROW, BF), "small": ((16, D), F32)}
FWD_WORK = {
    "attn_in": ((2,) + WIDEROW, BF),
    "second": (WIDEROW, BF),
    "active": ((4,) + WIDEROW, BF),
}
BWD_WORK = {
    "dhidden": ((4,) + WIDEROW, BF),
    "dpacked": ((4,) + WIDEROW, BF),
}
WORK = {"heads": (WIDEROW, BF), "acc": (WIDEROW, F32)}


class Fetched:
    def __init__(self, source, ref, sem):
        self.ref, self.copy = ref, pltpu.make_async_copy(source, ref, sem)

    def start(self):
        self.copy.start()

    def wait(self):
        self.copy.wait()


def layer_call(kind, whole, tails, vecs, nat, pairs, order, place, x, grad=None, old=None):
    near_out = {"fwd": RESULT, "both": {**RESULT, **GRADS}, "bwd": GRADS}[kind]
    far_out = {"fwd": {**EARLY, **KEPT}, "both": {**EARLY, **LATE}, "bwd": LATE}[kind]
    outs = {**near_out, **far_out}
    work = {**WORK, **KEPT}
    if kind != "bwd":
        work.update(FWD_WORK)
    if kind != "fwd":
        work.update(BWD_WORK)
    passed = {"fwd": {}, "both": {**RESULT, **EARLY}, "bwd": {**GRADS, **LATE}}[kind]
    loaded = KEPT if kind == "bwd" else {}
    far = [whole, tails, order] + [old[k] for k in (*passed, *loaded)]
    near = [vecs, nat, pairs, x] + ([] if grad is None else [grad])
    section = 1 if kind == "both" else 0

    def kernel(place_ref, *refs):
        far_refs, refs = refs[: len(far)], refs[len(far) :]
        near_refs, refs = refs[: len(near)], refs[len(near) :]
        out = dict(zip(outs, refs))
        refs = refs[len(outs) :]
        r = {**dict(zip(work, refs)), **{k: out[k] for k in near_out}}
        buf, order_buf, sems, old_sems, order_sem, out_sems = refs[len(work) :]
        w = Weights(far_refs[0], far_refs[1], buf, sems, kind)
        order_in = Fetched(far_refs[2], order_buf, order_sem)
        vecs_ref, nat_ref, pairs_ref, x_ref = near_refs[:4]
        old_refs = dict(zip((*passed, *loaded), far_refs[3:]))
        sent = []

        def send(name):
            if name in KEPT:
                moves = [(r[name], out[name])] if name in out else []
            else:
                moves = []
                for d in range(4):
                    z = lax.rem(place_ref[2] + d, 4)
                    if name == "early":
                        sources = (r["second"], r["active"].at[z], r["attn_in"].at[z // 3])
                        moves += [(v, out[f"early{d}"].at[i]) for i, v in enumerate(sources)]
                    elif name == "late_first":
                        moves.append((r["dhidden"].at[z], out[f"late{d}"].at[0]))
                    else:
                        moves.append((r["dpacked"].at[z], out[f"late{d}"].at[1]))
            for source, target in moves:
                copy = pltpu.make_async_copy(source, target, out_sems.at[len(sent)])
                copy.start()
                sent.append(copy)

        @pl.when(place_ref[3] == section)
        def _():
            fetched = [
                Fetched(old_refs[k], r[k], old_sems.at[i]) for i, k in enumerate(loaded)
            ]
            for copy in fetched:
                copy.start()
            w.begin()
            order_in.start()
            if kind != "bwd":
                forward_part(
                    w, send, x_ref, place_ref, pairs_ref, vecs_ref, nat_ref, order_in, r
                )
            for copy in fetched:
                copy.wait()
            if kind != "fwd":
                backward_part(
                    w,
                    kind == "bwd",
                    send,
                    near_refs[4],
                    x_ref,
                    place_ref,
                    pairs_ref,
                    vecs_ref,
                    order_in,
                    r,
                )
            for copy in sent:
                copy.wait()

        if passed:

            @pl.when(place_ref[3] != section)
            def _():
                into, back = [], []
                for i, k in enumerate(passed):
                    if k in near_out:
                        into.append(pltpu.make_async_copy(old_refs[k], out[k], old_sems.at[i]))
                        continue
                    for j in range(passed[k][0][0]):
                        held = buf.at[i, pl.ds(j * ROWS, ROWS)]
                        n = len(back)
                        into.append(
                            pltpu.make_async_copy(old_refs[k].at[j], held, out_sems.at[n])
                        )
                        back.append(
                            pltpu.make_async_copy(held, out[k].at[j], out_sems.at[16 + n])
                        )
                for copies in (into, back):
                    for copy in copies:
                        copy.start()
                    for copy in copies:
                        copy.wait()

    vm = pl.BlockSpec(memory_space=pltpu.VMEM)
    hbm = pl.BlockSpec(memory_space=pl.ANY)
    results = pl.pallas_call(
        kernel,
        in_specs=[pl.BlockSpec(memory_space=pltpu.SMEM)] + [hbm] * len(far) + [vm] * len(near),
        out_specs=[vm] * len(near_out) + [hbm] * len(far_out),
        out_shape=[jax.ShapeDtypeStruct(s, t) for s, t in outs.values()],
        scratch_shapes=[pltpu.VMEM(s, t) for s, t in work.values()]
        + [
            pltpu.VMEM((BLOCKS, D, PAD), BF),
            pltpu.VMEM((PAD, D), BF),
            pltpu.SemaphoreType.DMA((BLOCKS, 2)),
            pltpu.SemaphoreType.DMA((8,)),
            pltpu.SemaphoreType.DMA,
            pltpu.SemaphoreType.DMA((32,)),
        ],
        compiler_params=pltpu.CompilerParams(vmem_limit_bytes=VMEM_BYTES),
        cost_estimate=pl.CostEstimate(
            flops={"fwd": 4, "both": 12, "bwd": 8}[kind] * 10**9,
            bytes_accessed=BLOCKS * D * PAD * 2,
            transcendentals=10**6,
        ),
        name="layer_" + kind,
    )(place, *far, *near)
    return dict(zip(outs, results))


CHUNK = 72
BLOCK = ((4, CHUNK, PAD), BF)
WIDE = (PAD, 2 * PAD)


def local_call(kernel, name, place, ins, out_shapes, scratch=(), far=(), far_out=False):
    vm = pl.BlockSpec(memory_space=pltpu.VMEM)
    hbm = pl.BlockSpec(memory_space=pl.ANY)
    return pl.pallas_call(
        kernel,
        in_specs=[pl.BlockSpec(memory_space=pltpu.SMEM)] + [hbm] * len(far) + [vm] * len(ins),
        out_specs=[hbm if far_out else vm] * len(out_shapes),
        out_shape=[jax.ShapeDtypeStruct(s, t) for s, t in out_shapes],
        scratch_shapes=list(scratch),
        compiler_params=pltpu.CompilerParams(vmem_limit_bytes=VMEM_BYTES),
        name=name,
    )(place, *far, *ins)


def product(a, b, held, outs, sems, place, axis):
    last = t_dot(a[:, MAIN:], b)
    nothing = jnp.zeros((4, PAD), F32)
    for x in range(4):
        main = t_dot(a[:, x * 256 : (x + 1) * 256], b)
        for y in range(4):
            at = (x * 4 + y) * 4
            rows = [main[y * 64 : (y + 1) * 64], last[at : at + 4], nothing]
            i, j = (x, y) if axis == 0 else (y, x)
            held[i, j] = jnp.concatenate(rows, axis=0).astype(BF)
    copies = []
    for d in range(4):
        source = held.at[lax.rem(place[axis] + d, 4)]
        copies.append(pltpu.make_async_copy(source, outs[d], sems.at[d]))
        copies[-1].start()
    return copies


def load(sources, held, sems):
    copies = []
    for d in range(4):
        copies.append(pltpu.make_async_copy(sources[d], held.at[d], sems.at[d]))
        copies[-1].start()

    def rows():
        for copy in copies:
            copy.wait()
        return jnp.concatenate([held[d, :, :D] for d in range(4)], axis=0)

    return rows


def wide(v):
    return jnp.concatenate([v, jnp.zeros((v.shape[0], PAD - D), v.dtype)], axis=1)


def down_products_kernel(place, *refs):
    early, branch, outs = refs[:4], refs[4:8], refs[8:12]
    block, a_held, b_held, sems = refs[12:]
    a = load([e.at[1] for e in early], a_held, sems.at[0])
    b = load(branch, b_held, sems.at[1])
    for copy in product(a(), wide(b()), block, outs, sems.at[2], place, 1):
        copy.wait()


def products_kernel(place, *refs):
    early, late, small, outs = refs[:4], refs[4:8], refs[8], refs[9:17]
    up, attn, held, sems = refs[17:]
    a_up = load([e.at[0] for e in early], held.at[0], sems.at[0])
    b_up = load([v.at[0] for v in late], held.at[1], sems.at[1])
    a_attn = load([e.at[2] for e in early], held.at[2], sems.at[2])
    b_attn = load([v.at[1] for v in late], held.at[3], sems.at[3])
    slot = lax.broadcasted_iota(jnp.int32, (16, PAD), 1) - D
    unit = (slot == lax.broadcasted_iota(jnp.int32, (16, PAD), 0)).astype(F32).astype(BF)
    copies = product(a_up(), wide(b_up()), up, outs[:4], sems.at[4], place, 0)
    a = jnp.concatenate([a_attn(), small[...].astype(BF)], axis=0)
    b = jnp.concatenate([wide(b_attn()), unit], axis=0)
    copies += product(a, b, attn, outs[4:], sems.at[5], place, 1)
    for copy in copies:
        copy.wait()


def total(parts):
    return sum((p.astype(F32) for p in parts[1:]), parts[0].astype(F32))


def first_sum_kernel(place, *refs):
    given, outs, held, sems = refs[:12], refs[12:20], refs[20], refs[21]
    copies = {}
    for d in range(4):
        for g, other in ((1, 0), (0, 1), (2, 0)):
            i = lax.rem(place[other] + d, 4)
            copies[g, d] = [
                pltpu.make_async_copy(given[4 * g + k].at[i], held.at[g, d, k], sems.at[g, d, k])
                for k in range(4)
            ]
            for copy in copies[g, d]:
                copy.start()
    for d in range(4):
        for g, (h, start) in ((1, (1, 0)), (0, (0, 0)), (2, (1, PAD))):
            for copy in copies[g, d]:
                copy.wait()
            summed = total([held[g, d, k] for k in range(4)]).astype(BF)
            outs[4 * h + d][:, start : start + PAD] = summed


def second_sum_kernel(place, *refs):
    outs, held = refs[8:12], refs[12]
    for h in range(2):
        full = total([p[...] for p in refs[4 * h : 4 * h + 4]])
        start = h * WIDE[0]
        empty = jnp.zeros((7, WIDE[h]), F32)
        for z in range(4):
            rows = [full[z * 16 : (z + 1) * 16], full[64 + z : 65 + z], empty]
            held[z, :, start : start + WIDE[h]] = jnp.concatenate(rows, axis=0).astype(BF)
    for d in range(4):
        outs[d][...] = held[lax.rem(place[2] + d, 4)]


def final_kernel(place, *refs):
    hid_in, order_in, parts, outs = refs[0], refs[1], refs[2:6], refs[6:11]
    held, hid, order, sems = refs[11:]
    g_up, g_down, g_out, g_qkv, sums = outs
    hid_copy = pltpu.make_async_copy(hid_in, hid, sems.at[0])
    order_copy = pltpu.make_async_copy(order_in, order, sems.at[1])
    hid_copy.start()
    order_copy.start()
    for d in range(4):
        held[lax.rem(place[2] + 4 - d, 4)] = parts[d][...]
    up = []
    for j in range(4):
        pieces = [held[a, :, j * 256 : (j + 1) * 256] for a in range(4)]
        pieces += [held[a, :, MAIN + j * 16 : MAIN + (j + 1) * 16] for a in range(4)]
        up.append(jnp.concatenate(pieces, axis=1))
    hid_copy.wait()
    up = matmul(jnp.concatenate(up, axis=0), hid[...])
    up = jnp.concatenate([up[j * 24 : (j + 1) * 24] for j in range(4)], axis=1)
    for i in range(SHARD):
        g_up[i] = up[i : i + 1]
    start = WIDE[0]
    attn = [held[a, :, start + PAD :] for a in range(4)]
    rows = [held[a, :, start : start + D] for a in range(4)] + [attn[3][:, :D]]
    order_copy.wait()
    rows = dot_t(jnp.concatenate(rows, axis=0), order[:D])
    qkv = jnp.concatenate([v[:, :D].astype(F32) for v in attn[:3]], axis=1)
    for i in range(SHARD):
        for a in range(4):
            g_down[a * SHARD + i] = rows[a * 24 + i : a * 24 + i + 1]
        g_out[i] = rows[96 + i : 97 + i]
        g_qkv[i] = qkv[i : i + 1]
    sums[...] = total([v[:SHARD, D:] for v in attn])


def ring(v, axis, d):
    return lax.ppermute(v, axis, [(i, (i + d) % 4) for i in range(4)])


def restore_kernel(place, order, result, dx, acts, grads):
    acts[...] = dot_t(result[...], order[:D]).astype(BF)
    grads[...] = dot_t(dx[...], order[:D]).astype(BF)


def pad_cols(v, width):
    return jnp.pad(v, ((0, 0), (0, width - v.shape[1])))


def body(inputs, cotangent, lengths, vectors, qkv_w, out_w, up_w, up_b, down_w):
    section = lax.axis_index("section")
    mb, rows, _ = inputs.shape
    n = mb * rows
    c = constants()
    order = c["order"]

    outdown = matmul(jnp.concatenate([out_w[0], down_w[0]], axis=0), c["order_d"]).astype(BF)
    hid = matmul(up_w[0].reshape(SHARD * 4, D), c["hid"]).astype(BF).reshape(SHARD, 4, D)
    hid_main = hid[:, :, :MAIN].reshape(SHARD, 4, 4, 256).transpose(0, 2, 1, 3)
    hid_last = hid[:, :, MAIN:].reshape(SHARD, 4, 4, 16).transpose(0, 2, 1, 3)
    hid = jnp.concatenate(
        [
            hid_main.reshape(SHARD, 4, MAIN),
            hid_last.reshape(SHARD, 4, NDP),
            jnp.zeros((SHARD, 4, PAD - D), BF),
        ],
        axis=2,
    )
    shard = [hid.reshape(SHARD, 4 * PAD)]
    shard += [pad_cols(outdown[SHARD * (1 + a) : SHARD * (2 + a)], PAD) for a in range(4)]
    shard += [pad_cols(qkv_w[0][:, i * D : (i + 1) * D], PAD) for i in range(3)]
    shard += [pad_cols(outdown[:SHARD], PAD)]
    shard = jnp.concatenate(shard, axis=1)
    tail = jnp.concatenate([shard[16], vectors[0].reshape(-1), up_b[0]])
    tail = jnp.pad(tail, (0, 16 * TAILW - tail.shape[0])).reshape(16, TAILW)
    sent = jnp.concatenate([shard[:16], tail], axis=1)
    whole = lax.all_gather(sent, ("x", "y", "z"), axis=0, tiled=True)
    tails, vecs, nat = unpack(whole, c)

    ends = jnp.cumsum(lengths[:, 0], axis=1)
    place = jnp.arange(rows, dtype=jnp.int32)
    seg = jnp.sum((place[None, :, None] >= ends[:, None, :]).astype(jnp.int32), axis=2)
    seg = (seg + 8 * jnp.arange(mb, dtype=jnp.int32)[:, None]).reshape(n)
    at = jnp.arange(n, dtype=jnp.int32)
    pairs = ((seg[:, None] == seg[None, :]) & (at[:, None] >= at[None, :])).astype(F32)

    order_d = c["order_d"]
    x0 = matmul(inputs.reshape(n, D), order_d).astype(BF)
    cot = matmul(cotangent.reshape(n, D), order_d).astype(BF)
    place = jnp.stack([lax.axis_index("x"), lax.axis_index("y"), lax.axis_index("z"), section])
    call = functools.partial(
        layer_call,
        whole=whole,
        tails=tails,
        vecs=vecs,
        nat=nat,
        pairs=pairs,
        order=order,
        place=place,
    )

    first = call("fwd", x=x0)
    arrived = lax.ppermute(first["result"], "section", [(0, 1)])
    top = call("both", x=arrived, grad=cot, old=first)
    coming = lax.ppermute(top["dx"], "section", [(1, 0)])
    early = [top["early0"]] + [ring(top[f"early{d}"], "z", d) for d in (1, 3, 2)]
    coming, early[1], early[2] = lax.optimization_barrier((coming, early[1], early[2]))
    branch = jnp.where(section == 0, coming, cot)
    branches = [branch] + [ring(branch, "z", d) for d in (1, 3, 2)]
    kept = {k: first[k] for k in KEPT}
    old = {**{k: top[k] for k in (*GRADS, *LATE)}, **kept}
    bwd = call("bwd", x=x0, grad=coming, old=old)
    sends = [bwd[f"late{d}"] for d in (1, 3, 2)]
    early, branches, sends = lax.optimization_barrier((early, branches, sends))
    late = [bwd["late0"]] + [ring(v, "z", d) for v, d in zip(sends, (1, 3, 2))]

    vmem, sem = pltpu.VMEM, pltpu.SemaphoreType.DMA
    down = local_call(
        down_products_kernel,
        "down_products",
        place,
        [],
        [BLOCK] * 4,
        [vmem((4, 4, CHUNK, PAD), BF), vmem((4,) + WIDEROW, BF), vmem((4,) + ROW, BF), sem((3, 4))],
        far=[*early, *branches],
        far_out=True,
    )
    late, down = lax.optimization_barrier((late, down))
    small, down = lax.optimization_barrier((bwd["small"], down))
    down = [down[0]] + [ring(down[d], "y", d) for d in (2, 1, 3)]
    out = local_call(
        products_kernel,
        "products",
        place,
        [small],
        [BLOCK] * 8,
        [vmem((4, 4, CHUNK, PAD), BF)] * 2 + [vmem((4, 4) + WIDEROW, BF), sem((6, 4))],
        far=[*early, *late],
        far_out=True,
    )
    down, out = lax.optimization_barrier((down, out))
    up = [out[0]] + [ring(out[d], "x", d) for d in (2, 1, 3)]
    after = ring(out[5], "y", 1)
    held, after = lax.optimization_barrier((out[7], after))
    attn = [out[4], ring(out[6], "y", 2), after, ring(held, "y", 3)]
    out = local_call(
        first_sum_kernel,
        "first_sum",
        place,
        [],
        [((CHUNK, WIDE[h]), BF) for h in (0, 1) for _ in range(4)],
        [vmem((3, 4, 4, CHUNK, PAD), BF), sem((3, 4, 4))],
        far=[*up, *down, *attn],
    )
    got = []
    for h, axis in ((0, "y"), (1, "x")):
        got += [out[4 * h]] + [ring(out[4 * h + d], axis, d) for d in (1, 3, 2)]
    out = local_call(
        second_sum_kernel,
        "second_sum",
        place,
        got,
        [((24, sum(WIDE)), BF)] * 4,
        [vmem((4, 24, sum(WIDE)), BF)],
    )
    got = [out[0]] + [ring(out[d], "z", d) for d in (1, 2, 3)]
    g_up, g_down, g_out, g_qkv, sums = local_call(
        final_kernel,
        "owners",
        place,
        got,
        [
            ((SHARD, 1, FF), F32),
            ((4 * SHARD, 1, D), F32),
            ((SHARD, 1, D), F32),
            ((SHARD, 1, 3 * D), F32),
            ((SHARD, PAD - D), F32),
        ],
        [
            vmem((4, 24, sum(WIDE)), BF),
            vmem((D, D), BF),
            vmem((PAD, D), BF),
            pltpu.SemaphoreType.DMA((2,)),
        ],
        far=[c["hid_t"], order],
    )
    acts, grads = local_call(
        restore_kernel, "restore", place, [order, top["result"], bwd["dx"]], [(ROW, BF)] * 2
    )
    return (
        acts.reshape(1, mb, rows, D),
        grads.reshape(1, mb, rows, D),
        sums[None, :, :8],
        g_qkv.reshape(1, SHARD, 3 * D),
        g_out.reshape(1, SHARD, D),
        g_up.reshape(1, SHARD, FF),
        sums[:, 8:12].T.reshape(1, 4 * SHARD),
        g_down.reshape(1, 4 * SHARD, D),
    )


def solution(mesh):
    grid = Mesh(mesh.devices.reshape(2, 4, 4, 4), ("section", "x", "y", "z"))
    dp = ("x", "y", "z")
    tokens = P(None, dp, None)
    rows = P("section", dp, None)
    in_specs = (tokens, tokens, tokens, rows, rows, rows, rows, P("section", dp), rows)
    stacks = P("section", None, dp, None)
    out_specs = (stacks, stacks, rows, rows, rows, rows, P("section", dp), rows)
    return jax.shard_map(body, mesh=grid, in_specs=in_specs, out_specs=out_specs, check_vma=False)
```

```python
import functools

import jax
import jax.numpy as jnp
import numpy as np
from jax import lax
from jax.experimental import pallas as pl
from jax.experimental.pallas import tpu as pltpu
from jax.sharding import Mesh, PartitionSpec as P

HEADS = 17
HDIM = 64
D = HEADS * HDIM
FF = 4 * D
SHARD = 17
NDP = 64
MAIN = 16 * NDP
PAD = 1152
ROWS = 128
PAIRS = PAD // 128

UP, DOWN, QKV, OUT, BLOCKS = 0, 4, 8, 11, 12
TAIL0 = BLOCKS * PAD
TAILW = 896
WIDTH = TAIL0 + TAILW
SMALLS = 256

NORM_EPSILON = 1e-05
SCORE_SCALE = 0.125
GELU_C = float(np.sqrt(2 / np.pi))
GELU_A = 0.044715
BF = jnp.bfloat16
F32 = jnp.float32
WINDOW = 3
VMEM_BYTES = 58 * 1024 * 1024


def constants():
    n = np.arange(D)
    shard_of = np.where(n < MAIN, n // 16, n - MAIN)
    row_of = np.where(n < MAIN, n % 16, 16)
    order = np.zeros((PAD, D), np.float32)
    order[shard_of * SHARD + row_of, n] = 1
    f = np.arange(D)
    s, a, r = f // 68, (f % 68) // SHARD, f % SHARD
    hid = np.zeros((D, D), np.float32)
    hid[f, np.where(r < 16, a * 256 + s * 16 + r, 1024 + a * 16 + s)] = 1
    k = np.arange(SMALLS)
    is_vec, is_up = k < 136, (k >= 136) & (k < 204)
    k_row = np.where(is_vec, k // 8, np.where(is_up, (k - 136) % SHARD, -1))
    k_out = np.where(is_vec, k % 8, np.where(is_up, 8 + (k - 136) // SHARD, -1))
    pick = (k_out[None, :] == np.arange(16)[:, None]).astype(np.float32)
    spread = (np.arange(NDP)[:, None] == shard_of[None, :]).astype(np.float32)
    keep = (k_row[:, None] == row_of[None, :]).astype(np.float32)
    nat = np.arange(PAD)
    spread_nat = (np.arange(NDP)[:, None] == nat[None, :] // SHARD).astype(np.float32)
    keep_nat = (k_row[:, None] == nat[None, :] % SHARD).astype(np.float32)
    m = np.arange(MAIN)
    turn = np.zeros((MAIN, MAIN), np.float32)
    turn[(m % 16) * NDP + m // 16, m] = 1
    names = ("order", "hid", "pick", "spread", "keep", "spread_nat", "keep_nat", "turn")
    values = (order, hid, pick, spread, keep, spread_nat, keep_nat, turn)
    found = {name: jnp.asarray(value, BF) for name, value in zip(names, values)}
    found["order_d"] = jnp.asarray(order[:D], BF)
    found["hid_t"] = jnp.asarray(hid.T, BF)
    return found


def matmul(a, b):
    return jnp.dot(a, b, preferred_element_type=F32)


def dot_t(a, b):
    return lax.dot_general(a, b, (((1,), (1,)), ((), ())), preferred_element_type=F32)


def t_dot(a, b):
    return lax.dot_general(a, b, (((0,), (0,)), ((), ())), preferred_element_type=F32)


def norm_parts(features):
    centred = features - jnp.mean(features, axis=-1, keepdims=True)
    inverse = lax.rsqrt(jnp.mean(centred * centred, axis=-1, keepdims=True) + NORM_EPSILON)
    return centred * inverse, inverse


def norm_back(gradient, normed, inverse, gain):
    scaled = gradient * gain
    centred = scaled - jnp.mean(scaled, axis=-1, keepdims=True)
    return inverse * (centred - normed * jnp.mean(scaled * normed, axis=-1, keepdims=True))


def col_sum(v):
    return jnp.sum(v, axis=0, keepdims=True)


def unpack_kernel(whole, *refs):
    given, (tails, vecs, nat), (raw, table, *held), sems = refs[:6], refs[6:9], refs[9:17], refs[17]
    copies = [pltpu.make_async_copy(whole.at[:, pl.ds(TAIL0, TAILW)], raw, sems.at[0])]
    for i, (source, target) in enumerate(zip(given, held)):
        copies.append(pltpu.make_async_copy(source, target, sems.at[1 + i]))
    for copy in copies:
        copy.start()
    turn, pick, spread, keep, spread_nat, keep_nat = held
    copies[0].wait()
    copies[1].wait()
    turned = matmul(turn[...], raw[...]).astype(BF)
    for j in range(16):
        table[:, j * TAILW : (j + 1) * TAILW] = turned[j * NDP : (j + 1) * NDP]
    out = pltpu.make_async_copy(table, tails, sems.at[7])
    out.start()
    for copy in copies[2:]:
        copy.wait()
    small = table[:, TAIL0 : TAIL0 + SMALLS]
    for result, s, k in ((vecs, spread, keep), (nat, spread_nat, keep_nat)):
        wide_rows = t_dot(small, s[...]) * k[...].astype(F32)
        result[...] = matmul(pick[...], wide_rows.astype(BF))
    out.wait()


def unpack(whole, c):
    vm = pl.BlockSpec(memory_space=pltpu.VMEM)
    hbm = pl.BlockSpec(memory_space=pl.ANY)
    consts = [c[k] for k in ("turn", "pick", "spread", "keep", "spread_nat", "keep_nat")]
    table = (NDP, 16 * TAILW)
    return pl.pallas_call(
        unpack_kernel,
        in_specs=[hbm] * 7,
        out_specs=[hbm, vm, vm],
        out_shape=[
            jax.ShapeDtypeStruct(table, BF),
            jax.ShapeDtypeStruct((16, D), F32),
            jax.ShapeDtypeStruct((16, PAD), F32),
        ],
        scratch_shapes=[pltpu.VMEM((MAIN, TAILW), BF), pltpu.VMEM(table, BF)]
        + [pltpu.VMEM(v.shape, BF) for v in consts]
        + [pltpu.SemaphoreType.DMA((8,))],
        compiler_params=pltpu.CompilerParams(vmem_limit_bytes=VMEM_BYTES),
        name="unpack",
    )(whole, *consts)


class Weights:
    def __init__(self, whole, tails, buf, sems, kind):
        self.whole, self.tails, self.buf, self.sems, self.kind = whole, tails, buf, sems, kind

    def block(self, p):
        if self.kind == "bwd":
            pair = (p % 2 == 0) * DOWN + p // 2
            rest = OUT * (p == 8) + (p - 1) * (p > 8)
            return pair * (p < 8) + rest * (p >= 8)
        q = p - 4
        return (p < 4) * (QKV + p) + (p >= 4) * ((q % 2) * DOWN + q // 2)

    def copies(self, p):
        b = self.block(p)
        cols = pl.ds(pl.multiple_of(b * PAD, 128), PAD)
        return (
            pltpu.make_async_copy(
                self.whole.at[:, cols], self.buf.at[b, pl.ds(0, MAIN)], self.sems.at[b, 0]
            ),
            pltpu.make_async_copy(
                self.tails.at[:, cols], self.buf.at[b, pl.ds(MAIN, NDP)], self.sems.at[b, 1]
            ),
        )

    def start(self, p):
        for copy in self.copies(p):
            copy.start()

    def begin(self):
        for p in range(WINDOW):
            self.start(p)

    def wait(self, p):
        for copy in self.copies(p):
            copy.wait()
        if isinstance(p, int):
            if p + WINDOW < BLOCKS:
                self.start(p + WINDOW)
        else:

            @pl.when(p + WINDOW < BLOCKS)
            def _():
                self.start(p + WINDOW)


def pair_masks():
    lane = lax.broadcasted_iota(jnp.int32, (ROWS, 128), 1)
    first = (lane < HDIM).astype(F32)
    return first, 1.0 - first


def stacked(v, masks):
    return jnp.concatenate([(v * m).astype(BF) for m in masks], axis=0)


def soft_pair(q, kk, allowed):
    scores = dot_t(q, kk) * SCORE_SCALE
    halves = []
    for h in range(2):
        s = jnp.where(allowed, scores[:, h * ROWS : (h + 1) * ROWS], -1e30)
        e = jnp.exp(s - jnp.max(s, axis=-1, keepdims=True))
        halves.append(e / jnp.sum(e, axis=-1, keepdims=True))
    return halves


def forward_part(w, send, x_ref, place, pairs_ref, vecs, nat, order, r):
    x = x_ref[...].astype(F32)
    normed, _ = norm_parts(x)
    r["attn_in"][0, :, :D] = (normed * vecs[0:1] + vecs[1:2]).astype(BF)

    def project(i, carry):
        w.wait(i)
        shift = jnp.where(i == 0, nat[2:3], jnp.where(i == 2, nat[3:4], 0.0))
        r["packed"][i] = (matmul(r["attn_in"][0, :, :D], w.buf[QKV + i]) + shift).astype(BF)
        return carry

    lax.fori_loop(0, 3, project, 0)
    send("packed")
    masks = pair_masks()
    allowed = pairs_ref[...] > 0
    for p in range(PAIRS):
        cols = pl.ds(p * 128, 128)
        kk = stacked(r["packed"][1, :, cols].astype(F32), masks)
        vv = stacked(r["packed"][2, :, cols].astype(F32), masks)
        halves = soft_pair(r["packed"][0, :, cols], kk, allowed)
        soft = jnp.concatenate([h.astype(BF) for h in halves], axis=1)
        r["heads"][:, cols] = matmul(soft, vv).astype(BF)
    order.wait()
    mixed = matmul(r["heads"][...], order.ref[...]).astype(BF)
    r["attn_in"][1, :, :D] = mixed
    w.wait(3)
    branch = matmul(mixed, w.buf[OUT])[:, :D]
    middle = x + branch + vecs[4:5]
    r["middle"][...] = middle
    send("middle")
    normed, _ = norm_parts(middle)
    r["second"][:, :D] = (normed * vecs[5:6] + vecs[6:7]).astype(BF)
    r["acc"][...] = jnp.zeros((ROWS, PAD), F32)

    def feed(a, carry):
        w.wait(4 + 2 * a)
        hidden = matmul(r["second"][:, :D], w.buf[UP + a])[:, :D] + vecs[pl.ds(8 + a, 1)]
        r["hidden"][a] = hidden
        bent = jnp.tanh(GELU_C * (hidden + GELU_A * (hidden * hidden * hidden)))
        r["active"][a, :, :D] = (0.5 * hidden * (1.0 + bent)).astype(BF)
        w.wait(5 + 2 * a)
        r["acc"][...] += matmul(r["active"][a, :, :D], w.buf[DOWN + a])
        return carry

    lax.fori_loop(0, 4, feed, 0)
    r["result"][...] = (r["middle"][...] + r["acc"][:, :D] + vecs[7:8]).astype(BF)
    send("hidden")
    send("early")


def backward_part(w, wait, send, grad_ref, x_ref, place, pairs_ref, vecs, order, r):
    grad = grad_ref[...]
    dres = grad.astype(F32)
    r["acc"][...] = jnp.zeros((ROWS, PAD), F32)

    def feed(a, carry):
        if wait:
            w.wait(2 * a)
        dactive = dot_t(grad_ref[...], w.buf[DOWN + a, :, :D])
        h = r["hidden"][a]
        square = h * h
        bent = jnp.tanh(GELU_C * (h + GELU_A * (square * h)))
        slope = 0.5 * (1.0 + bent) + (0.5 * GELU_C) * h * (1.0 - bent * bent) * (
            1.0 + (3 * GELU_A) * square
        )
        dhidden = (dactive * slope).astype(BF)
        r["dhidden"][a, :, :D] = dhidden
        r["small"][pl.ds(8 + a, 1)] = col_sum(dhidden.astype(F32))
        if wait:
            w.wait(2 * a + 1)
        r["acc"][:, :D] += dot_t(dhidden, w.buf[UP + a, :, :D])
        return carry

    lax.fori_loop(0, 4, feed, 0)
    send("late_first")
    dsecond = r["acc"][:, :D]
    normed, inverse = norm_parts(r["middle"][...])
    r["small"][5:6] = col_sum(dsecond * normed)
    r["small"][6:7] = col_sum(dsecond)
    r["small"][7:8] = col_sum(dres)
    dmiddle = dres + norm_back(dsecond, normed, inverse, vecs[5:6])
    r["middle"][...] = dmiddle
    dattn = dmiddle.astype(BF)
    r["dpacked"][3, :, :D] = dattn
    r["small"][4:5] = col_sum(dattn.astype(F32))
    if wait:
        w.wait(8)
    dmixed = dot_t(dattn, w.buf[OUT, :, :D]).astype(BF)
    if wait:
        order.wait()
    r["heads"][...] = dot_t(dmixed, order.ref[...]).astype(BF)
    masks = pair_masks()
    allowed = pairs_ref[...] > 0
    for p in range(PAIRS):
        cols = pl.ds(p * 128, 128)
        width = min(D - p * 128, 128)
        live = pl.ds(p * 128, width)
        q = r["packed"][0, :, cols]
        kk = stacked(r["packed"][1, :, cols].astype(F32), masks)
        vv = stacked(r["packed"][2, :, cols].astype(F32), masks)
        dm = r["heads"][:, cols]
        halves = soft_pair(q, kk, allowed)
        dsoft = dot_t(dm, vv)
        dscores = []
        for h, p_half in enumerate(halves):
            d_half = dsoft[:, h * ROWS : (h + 1) * ROWS]
            centre = jnp.sum(d_half * p_half, axis=-1, keepdims=True)
            dscores.append((p_half * (d_half - centre)).astype(BF))
        ds = jnp.concatenate(dscores, axis=1)
        soft = jnp.concatenate([h.astype(BF) for h in halves], axis=1)
        dq = matmul(ds, kk) * SCORE_SCALE
        dk = t_dot(ds, q) * SCORE_SCALE
        dv = t_dot(soft, dm)
        dk = dk[:ROWS] * masks[0] + dk[ROWS:] * masks[1]
        dv = dv[:ROWS] * masks[0] + dv[ROWS:] * masks[1]
        for i, v in enumerate((dq, dk, dv)):
            r["dpacked"][i, :, live] = v[:, :width].astype(BF)
    send("late_second")
    sums = [col_sum(r["dpacked"][i, :, :D].astype(F32)) for i in (0, 2)]
    sums = jnp.concatenate(sums + [jnp.zeros((14, D), F32)], axis=0).astype(BF)
    r["small"][2:4] = matmul(sums, order.ref[:D])[:2]
    r["acc"][...] = jnp.zeros((ROWS, PAD), F32)

    def project(i, carry):
        if wait:
            w.wait(9 + i)
        r["acc"][:, :D] += dot_t(r["dpacked"][i, :, :D], w.buf[QKV + i, :, :D])
        return carry

    lax.fori_loop(0, 3, project, 0)
    dentry = r["acc"][:, :D]
    normed, inverse = norm_parts(x_ref[...].astype(F32))
    r["small"][0:1] = col_sum(dentry * normed)
    r["small"][1:2] = col_sum(dentry)
    r["small"][12:16] = jnp.zeros((4, D), F32)
    r["dx"][...] = (r["middle"][...] + norm_back(dentry, normed, inverse, vecs[0:1])).astype(BF)


ROW = (ROWS, D)
WIDEROW = (ROWS, PAD)
KEPT = {
    "packed": ((3,) + WIDEROW, BF),
    "middle": (ROW, F32),
    "hidden": ((4,) + ROW, F32),
}
EARLY = {f"early{d}": ((3,) + WIDEROW, BF) for d in range(4)}
LATE = {f"late{d}": ((2,) + WIDEROW, BF) for d in range(4)}
RESULT = {"result": (ROW, BF)}
GRADS = {"dx": (ROW, BF), "small": ((16, D), F32)}
FWD_WORK = {
    "attn_in": ((2,) + WIDEROW, BF),
    "second": (WIDEROW, BF),
    "active": ((4,) + WIDEROW, BF),
}
BWD_WORK = {
    "dhidden": ((4,) + WIDEROW, BF),
    "dpacked": ((4,) + WIDEROW, BF),
}
WORK = {"heads": (WIDEROW, BF), "acc": (WIDEROW, F32)}


class Fetched:
    def __init__(self, source, ref, sem):
        self.ref, self.copy = ref, pltpu.make_async_copy(source, ref, sem)

    def start(self):
        self.copy.start()

    def wait(self):
        self.copy.wait()


def layer_call(kind, whole, tails, vecs, nat, pairs, order, place, x, grad=None, old=None):
    near_out = {"fwd": RESULT, "both": {**RESULT, **GRADS}, "bwd": GRADS}[kind]
    far_out = {"fwd": {**EARLY, **KEPT}, "both": {**EARLY, **LATE}, "bwd": LATE}[kind]
    outs = {**near_out, **far_out}
    work = {**WORK, **KEPT}
    if kind != "bwd":
        work.update(FWD_WORK)
    if kind != "fwd":
        work.update(BWD_WORK)
    passed = {"fwd": {}, "both": {**RESULT, **EARLY}, "bwd": {**GRADS, **LATE}}[kind]
    loaded = KEPT if kind == "bwd" else {}
    far = [whole, tails, order] + [old[k] for k in (*passed, *loaded)]
    near = [vecs, nat, pairs, x] + ([] if grad is None else [grad])
    section = 1 if kind == "both" else 0

    def kernel(place_ref, *refs):
        far_refs, refs = refs[: len(far)], refs[len(far) :]
        near_refs, refs = refs[: len(near)], refs[len(near) :]
        out = dict(zip(outs, refs))
        refs = refs[len(outs) :]
        r = {**dict(zip(work, refs)), **{k: out[k] for k in near_out}}
        buf, order_buf, sems, old_sems, order_sem, out_sems = refs[len(work) :]
        w = Weights(far_refs[0], far_refs[1], buf, sems, kind)
        order_in = Fetched(far_refs[2], order_buf, order_sem)
        vecs_ref, nat_ref, pairs_ref, x_ref = near_refs[:4]
        old_refs = dict(zip((*passed, *loaded), far_refs[3:]))
        sent = []

        def send(name):
            if name in KEPT:
                moves = [(r[name], out[name])] if name in out else []
            else:
                moves = []
                for d in range(4):
                    z = lax.rem(place_ref[2] + d, 4)
                    if name == "early":
                        sources = (r["second"], r["active"].at[z], r["attn_in"].at[z // 3])
                        moves += [(v, out[f"early{d}"].at[i]) for i, v in enumerate(sources)]
                    elif name == "late_first":
                        moves.append((r["dhidden"].at[z], out[f"late{d}"].at[0]))
                    else:
                        moves.append((r["dpacked"].at[z], out[f"late{d}"].at[1]))
            for source, target in moves:
                copy = pltpu.make_async_copy(source, target, out_sems.at[len(sent)])
                copy.start()
                sent.append(copy)

        @pl.when(place_ref[3] == section)
        def _():
            fetched = [
                Fetched(old_refs[k], r[k], old_sems.at[i]) for i, k in enumerate(loaded)
            ]
            for copy in fetched:
                copy.start()
            w.begin()
            order_in.start()
            if kind != "bwd":
                forward_part(
                    w, send, x_ref, place_ref, pairs_ref, vecs_ref, nat_ref, order_in, r
                )
            for copy in fetched:
                copy.wait()
            if kind != "fwd":
                backward_part(
                    w,
                    kind == "bwd",
                    send,
                    near_refs[4],
                    x_ref,
                    place_ref,
                    pairs_ref,
                    vecs_ref,
                    order_in,
                    r,
                )
            for copy in sent:
                copy.wait()

        if passed:

            @pl.when(place_ref[3] != section)
            def _():
                into, back = [], []
                for i, k in enumerate(passed):
                    if k in near_out:
                        into.append(pltpu.make_async_copy(old_refs[k], out[k], old_sems.at[i]))
                        continue
                    for j in range(passed[k][0][0]):
                        held = buf.at[i, pl.ds(j * ROWS, ROWS)]
                        n = len(back)
                        into.append(
                            pltpu.make_async_copy(old_refs[k].at[j], held, out_sems.at[n])
                        )
                        back.append(
                            pltpu.make_async_copy(held, out[k].at[j], out_sems.at[16 + n])
                        )
                for copies in (into, back):
                    for copy in copies:
                        copy.start()
                    for copy in copies:
                        copy.wait()

    vm = pl.BlockSpec(memory_space=pltpu.VMEM)
    hbm = pl.BlockSpec(memory_space=pl.ANY)
    results = pl.pallas_call(
        kernel,
        in_specs=[pl.BlockSpec(memory_space=pltpu.SMEM)] + [hbm] * len(far) + [vm] * len(near),
        out_specs=[vm] * len(near_out) + [hbm] * len(far_out),
        out_shape=[jax.ShapeDtypeStruct(s, t) for s, t in outs.values()],
        scratch_shapes=[pltpu.VMEM(s, t) for s, t in work.values()]
        + [
            pltpu.VMEM((BLOCKS, D, PAD), BF),
            pltpu.VMEM((PAD, D), BF),
            pltpu.SemaphoreType.DMA((BLOCKS, 2)),
            pltpu.SemaphoreType.DMA((8,)),
            pltpu.SemaphoreType.DMA,
            pltpu.SemaphoreType.DMA((32,)),
        ],
        compiler_params=pltpu.CompilerParams(vmem_limit_bytes=VMEM_BYTES),
        cost_estimate=pl.CostEstimate(
            flops={"fwd": 4, "both": 12, "bwd": 8}[kind] * 10**9,
            bytes_accessed=BLOCKS * D * PAD * 2,
            transcendentals=10**6,
        ),
        name="layer_" + kind,
    )(place, *far, *near)
    return dict(zip(outs, results))


CHUNK = 72
PART = 384
WIDE = (PAD + PART, PAD + PAD - PART)


def block(width):
    return ((4, CHUNK, width), BF)


def local_call(kernel, name, place, ins, out_shapes, scratch=(), far=(), far_out=False):
    vm = pl.BlockSpec(memory_space=pltpu.VMEM)
    hbm = pl.BlockSpec(memory_space=pl.ANY)
    return pl.pallas_call(
        kernel,
        in_specs=[pl.BlockSpec(memory_space=pltpu.SMEM)] + [hbm] * len(far) + [vm] * len(ins),
        out_specs=[hbm if far_out else vm] * len(out_shapes),
        out_shape=[jax.ShapeDtypeStruct(s, t) for s, t in out_shapes],
        scratch_shapes=list(scratch),
        compiler_params=pltpu.CompilerParams(vmem_limit_bytes=VMEM_BYTES),
        name=name,
    )(place, *far, *ins)


def product(a, b, store):
    last = t_dot(a[:, MAIN:], b)
    nothing = jnp.zeros((4, PAD), F32)
    for x in range(4):
        main = t_dot(a[:, x * 256 : (x + 1) * 256], b)
        for y in range(4):
            at = (x * 4 + y) * 4
            rows = [main[y * 64 : (y + 1) * 64], last[at : at + 4], nothing]
            store(x, y, jnp.concatenate(rows, axis=0).astype(BF))


def send_blocks(held, first, outs, sems, cols=None):
    copies = []
    for d in range(4):
        source, target = held.at[lax.rem(first + d, 4)], outs[d]
        if cols is not None:
            source, target = source.at[:, :, cols], target.at[:, :, cols]
        copies.append(pltpu.make_async_copy(source, target, sems.at[d]))
        copies[-1].start()
    return copies


def load(sources, held, sems):
    copies = []
    for d in range(4):
        copies.append(pltpu.make_async_copy(sources[d], held.at[d], sems.at[d]))
        copies[-1].start()

    def rows():
        for copy in copies:
            copy.wait()
        return jnp.concatenate([held[d, :, :D] for d in range(4)], axis=0)

    return rows


def wide(v):
    return jnp.concatenate([v, jnp.zeros((v.shape[0], PAD - D), v.dtype)], axis=1)


def down_products_kernel(place, *refs):
    early, branch, outs = refs[:4], refs[4:8], refs[8:12]
    held, a_held, b_held, sems = refs[12:]
    a = load([e.at[1] for e in early], a_held, sems.at[0])
    b = load(branch, b_held, sems.at[1])

    def store(x, y, v):
        held[y, x] = v

    product(a(), wide(b()), store)
    for copy in send_blocks(held, place[1], outs, sems.at[2]):
        copy.wait()


def products_kernel(place, *refs):
    early, late, small, outs = refs[:4], refs[4:8], refs[8], refs[9:17]
    first, second, held, sems = refs[17:]
    a_up = load([e.at[0] for e in early], held.at[0], sems.at[0])
    b_up = load([v.at[0] for v in late], held.at[1], sems.at[1])
    a_attn = load([e.at[2] for e in early], held.at[2], sems.at[2])
    b_attn = load([v.at[1] for v in late], held.at[3], sems.at[3])
    slot = lax.broadcasted_iota(jnp.int32, (16, PAD), 1) - D
    unit = (slot == lax.broadcasted_iota(jnp.int32, (16, PAD), 0)).astype(F32).astype(BF)

    def store_up(x, y, v):
        first[x, y, :, :PAD] = v

    def store_attn(x, y, v):
        first[x, y, :, PAD:] = v[:, :PART]
        second[y, x] = v[:, PART:]

    product(a_up(), wide(b_up()), store_up)
    copies = send_blocks(first, place[0], outs[:4], sems.at[4], pl.ds(0, PAD))
    a = jnp.concatenate([a_attn(), small[...].astype(BF)], axis=0)
    b = jnp.concatenate([wide(b_attn()), unit], axis=0)
    product(a, b, store_attn)
    copies += send_blocks(first, place[0], outs[:4], sems.at[5], pl.ds(PAD, PART))
    copies += send_blocks(second, place[1], outs[4:], sems.at[6])
    for copy in copies:
        copy.wait()


def total(parts):
    return sum((p.astype(F32) for p in parts[1:]), parts[0].astype(F32))


def first_sum_kernel(place, *refs):
    given, outs, held, sems = refs[:12], refs[12:20], refs[20:23], refs[23]
    copies = {}
    for d in range(4):
        for g, other in ((1, 0), (0, 1), (2, 0)):
            i = lax.rem(place[other] + d, 4)
            copies[g, d] = [
                pltpu.make_async_copy(given[4 * g + k].at[i], held[g].at[d, k], sems.at[g, d, k])
                for k in range(4)
            ]
            for copy in copies[g, d]:
                copy.start()
    for d in range(4):
        for g, h, start in ((1, 1, 0), (0, 0, 0), (2, 1, PAD)):
            for copy in copies[g, d]:
                copy.wait()
            summed = total([held[g][d, k] for k in range(4)]).astype(BF)
            outs[4 * h + d][:, start : start + summed.shape[1]] = summed


def second_sum_kernel(place, *refs):
    outs, held = refs[8:12], refs[12]
    for h in range(2):
        full = total([p[...] for p in refs[4 * h : 4 * h + 4]])
        start = h * WIDE[0]
        empty = jnp.zeros((7, WIDE[h]), F32)
        for z in range(4):
            rows = [full[z * 16 : (z + 1) * 16], full[64 + z : 65 + z], empty]
            held[z, :, start : start + WIDE[h]] = jnp.concatenate(rows, axis=0).astype(BF)
    for d in range(4):
        outs[d][...] = held[lax.rem(place[2] + d, 4)]


def final_kernel(place, *refs):
    hid_in, order_in, parts, outs = refs[0], refs[1], refs[2:6], refs[6:11]
    held, hid, order, sems = refs[11:]
    g_up, g_down, g_out, g_qkv, sums = outs
    hid_copy = pltpu.make_async_copy(hid_in, hid, sems.at[0])
    order_copy = pltpu.make_async_copy(order_in, order, sems.at[1])
    hid_copy.start()
    order_copy.start()
    for d in range(4):
        held[lax.rem(place[2] + 4 - d, 4)] = parts[d][...]
    up = []
    for j in range(4):
        pieces = [held[a, :, j * 256 : (j + 1) * 256] for a in range(4)]
        pieces += [held[a, :, MAIN + j * 16 : MAIN + (j + 1) * 16] for a in range(4)]
        up.append(jnp.concatenate(pieces, axis=1))
    hid_copy.wait()
    up = matmul(jnp.concatenate(up, axis=0), hid[...])
    up = jnp.concatenate([up[j * 24 : (j + 1) * 24] for j in range(4)], axis=1)
    for i in range(SHARD):
        g_up[i] = up[i : i + 1]
    start = WIDE[0]
    attn = [
        jnp.concatenate([held[a, :, PAD:start], held[a, :, start + PAD :]], axis=1)
        for a in range(4)
    ]
    rows = [held[a, :, start : start + D] for a in range(4)] + [attn[3][:, :D]]
    order_copy.wait()
    rows = dot_t(jnp.concatenate(rows, axis=0), order[:D])
    qkv = jnp.concatenate([v[:, :D].astype(F32) for v in attn[:3]], axis=1)
    for i in range(SHARD):
        for a in range(4):
            g_down[a * SHARD + i] = rows[a * 24 + i : a * 24 + i + 1]
        g_out[i] = rows[96 + i : 97 + i]
        g_qkv[i] = qkv[i : i + 1]
    sums[...] = total([v[:SHARD, D:] for v in attn])


def ring(v, axis, d):
    return lax.ppermute(v, axis, [(i, (i + d) % 4) for i in range(4)])


def restore_kernel(place, order, result, dx, acts, grads):
    acts[...] = dot_t(result[...], order[:D]).astype(BF)
    grads[...] = dot_t(dx[...], order[:D]).astype(BF)


def pad_cols(v, width):
    return jnp.pad(v, ((0, 0), (0, width - v.shape[1])))


def body(inputs, cotangent, lengths, vectors, qkv_w, out_w, up_w, up_b, down_w):
    section = lax.axis_index("section")
    mb, rows, _ = inputs.shape
    n = mb * rows
    c = constants()
    order = c["order"]

    outdown = matmul(jnp.concatenate([out_w[0], down_w[0]], axis=0), c["order_d"]).astype(BF)
    hid = matmul(up_w[0].reshape(SHARD * 4, D), c["hid"]).astype(BF).reshape(SHARD, 4, D)
    hid_main = hid[:, :, :MAIN].reshape(SHARD, 4, 4, 256).transpose(0, 2, 1, 3)
    hid_last = hid[:, :, MAIN:].reshape(SHARD, 4, 4, 16).transpose(0, 2, 1, 3)
    hid = jnp.concatenate(
        [
            hid_main.reshape(SHARD, 4, MAIN),
            hid_last.reshape(SHARD, 4, NDP),
            jnp.zeros((SHARD, 4, PAD - D), BF),
        ],
        axis=2,
    )
    shard = [hid.reshape(SHARD, 4 * PAD)]
    shard += [pad_cols(outdown[SHARD * (1 + a) : SHARD * (2 + a)], PAD) for a in range(4)]
    shard += [pad_cols(qkv_w[0][:, i * D : (i + 1) * D], PAD) for i in range(3)]
    shard += [pad_cols(outdown[:SHARD], PAD)]
    shard = jnp.concatenate(shard, axis=1)
    tail = jnp.concatenate([shard[16], vectors[0].reshape(-1), up_b[0]])
    tail = jnp.pad(tail, (0, 16 * TAILW - tail.shape[0])).reshape(16, TAILW)
    sent = jnp.concatenate([shard[:16], tail], axis=1)
    whole = lax.all_gather(sent, ("x", "y", "z"), axis=0, tiled=True)
    tails, vecs, nat = unpack(whole, c)

    ends = jnp.cumsum(lengths[:, 0], axis=1)
    place = jnp.arange(rows, dtype=jnp.int32)
    seg = jnp.sum((place[None, :, None] >= ends[:, None, :]).astype(jnp.int32), axis=2)
    seg = (seg + 8 * jnp.arange(mb, dtype=jnp.int32)[:, None]).reshape(n)
    at = jnp.arange(n, dtype=jnp.int32)
    pairs = ((seg[:, None] == seg[None, :]) & (at[:, None] >= at[None, :])).astype(F32)

    order_d = c["order_d"]
    x0 = matmul(inputs.reshape(n, D), order_d).astype(BF)
    cot = matmul(cotangent.reshape(n, D), order_d).astype(BF)
    place = jnp.stack([lax.axis_index("x"), lax.axis_index("y"), lax.axis_index("z"), section])
    call = functools.partial(
        layer_call,
        whole=whole,
        tails=tails,
        vecs=vecs,
        nat=nat,
        pairs=pairs,
        order=order,
        place=place,
    )

    first = call("fwd", x=x0)
    arrived = lax.ppermute(first["result"], "section", [(0, 1)])
    top = call("both", x=arrived, grad=cot, old=first)
    coming = lax.ppermute(top["dx"], "section", [(1, 0)])
    early = [top["early0"]] + [ring(top[f"early{d}"], "z", d) for d in (1, 3, 2)]
    branch = jnp.where(section == 0, coming, cot)
    branches = [branch] + [ring(branch, "z", d) for d in (1, 3)]
    kept = {k: first[k] for k in KEPT}
    old = {**{k: top[k] for k in (*GRADS, *LATE)}, **kept}
    bwd = call("bwd", x=x0, grad=coming, old=old)
    sends = [bwd[f"late{d}"] for d in (1, 3, 2)]
    early, branches, sends = lax.optimization_barrier((early, branches, sends))
    branches.append(ring(branches[0], "z", 2))
    late = [bwd["late0"]] + [ring(v, "z", d) for v, d in zip(sends, (1, 3, 2))]

    vmem, sem = pltpu.VMEM, pltpu.SemaphoreType.DMA
    down = local_call(
        down_products_kernel,
        "down_products",
        place,
        [],
        [block(PAD)] * 4,
        [vmem((4, 4, CHUNK, PAD), BF), vmem((4,) + WIDEROW, BF), vmem((4,) + ROW, BF), sem((3, 4))],
        far=[*early, *branches],
        far_out=True,
    )
    late, down = lax.optimization_barrier((late, down))
    small, down = lax.optimization_barrier((bwd["small"], down))
    down = [down[0]] + [ring(down[d], "y", d) for d in (2, 1, 3)]
    out = local_call(
        products_kernel,
        "products",
        place,
        [small],
        [block(WIDE[0])] * 4 + [block(PAD - PART)] * 4,
        [vmem((4, 4, CHUNK, width), BF) for width in (WIDE[0], PAD - PART)]
        + [vmem((4, 4) + WIDEROW, BF), sem((7, 4))],
        far=[*early, *late],
        far_out=True,
    )
    xs, ys = out[:4], out[4:]
    down[1], xs = lax.optimization_barrier((down[1], xs))
    down, ys = lax.optimization_barrier((down, ys))
    up = [xs[0]] + [ring(xs[d], "x", d) for d in (2, 1, 3)]
    attn = [ys[0]] + [ring(ys[d], "y", d) for d in (2, 1, 3)]
    out = local_call(
        first_sum_kernel,
        "first_sum",
        place,
        [],
        [((CHUNK, WIDE[h]), BF) for h in (0, 1) for _ in range(4)],
        [vmem((4, 4, CHUNK, width), BF) for width in (WIDE[0], PAD, PAD - PART)]
        + [sem((3, 4, 4))],
        far=[*up, *down, *attn],
    )
    got = []
    for h, axis in ((0, "y"), (1, "x")):
        got += [out[4 * h]] + [ring(out[4 * h + d], axis, d) for d in (1, 3, 2)]
    out = local_call(
        second_sum_kernel,
        "second_sum",
        place,
        got,
        [((24, sum(WIDE)), BF)] * 4,
        [vmem((4, 24, sum(WIDE)), BF)],
    )
    got = [out[0]] + [ring(out[d], "z", d) for d in (1, 2, 3)]
    g_up, g_down, g_out, g_qkv, sums = local_call(
        final_kernel,
        "owners",
        place,
        got,
        [
            ((SHARD, 1, FF), F32),
            ((4 * SHARD, 1, D), F32),
            ((SHARD, 1, D), F32),
            ((SHARD, 1, 3 * D), F32),
            ((SHARD, PAD - D), F32),
        ],
        [
            vmem((4, 24, sum(WIDE)), BF),
            vmem((D, D), BF),
            vmem((PAD, D), BF),
            pltpu.SemaphoreType.DMA((2,)),
        ],
        far=[c["hid_t"], order],
    )
    acts, grads = local_call(
        restore_kernel, "restore", place, [order, top["result"], bwd["dx"]], [(ROW, BF)] * 2
    )
    return (
        acts.reshape(1, mb, rows, D),
        grads.reshape(1, mb, rows, D),
        sums[None, :, :8],
        g_qkv.reshape(1, SHARD, 3 * D),
        g_out.reshape(1, SHARD, D),
        g_up.reshape(1, SHARD, FF),
        sums[:, 8:12].T.reshape(1, 4 * SHARD),
        g_down.reshape(1, 4 * SHARD, D),
    )


def solution(mesh):
    grid = Mesh(mesh.devices.reshape(2, 4, 4, 4), ("section", "x", "y", "z"))
    dp = ("x", "y", "z")
    tokens = P(None, dp, None)
    rows = P("section", dp, None)
    in_specs = (tokens, tokens, tokens, rows, rows, rows, rows, P("section", dp), rows)
    stacks = P("section", None, dp, None)
    out_specs = (stacks, stacks, rows, rows, rows, rows, P("section", dp), rows)
    return jax.shard_map(body, mesh=grid, in_specs=in_specs, out_specs=out_specs, check_vma=False)
```

```python
import functools

import jax
import jax.numpy as jnp
import numpy as np
from jax import lax
from jax.experimental import pallas as pl
from jax.experimental.pallas import tpu as pltpu
from jax.sharding import Mesh, PartitionSpec as P

HEADS = 17
HDIM = 64
D = HEADS * HDIM
FF = 4 * D
SHARD = 17
NDP = 64
MAIN = 16 * NDP
PAD = 1152
ROWS = 128
PAIRS = PAD // 128

UP, DOWN, QKV, OUT, BLOCKS = 0, 4, 8, 11, 12
TAIL0 = BLOCKS * PAD
TAILW = 896
WIDTH = TAIL0 + TAILW
SMALLS = 256

NORM_EPSILON = 1e-05
SCORE_SCALE = 0.125
GELU_C = float(np.sqrt(2 / np.pi))
GELU_A = 0.044715
BF = jnp.bfloat16
F32 = jnp.float32
WINDOW = 3
VMEM_BYTES = 58 * 1024 * 1024


def constants():
    n = np.arange(D)
    shard_of = np.where(n < MAIN, n // 16, n - MAIN)
    row_of = np.where(n < MAIN, n % 16, 16)
    order = np.zeros((PAD, D), np.float32)
    order[shard_of * SHARD + row_of, n] = 1
    f = np.arange(D)
    s, a, r = f // 68, (f % 68) // SHARD, f % SHARD
    hid = np.zeros((D, D), np.float32)
    hid[f, np.where(r < 16, a * 256 + s * 16 + r, 1024 + a * 16 + s)] = 1
    k = np.arange(SMALLS)
    is_vec, is_up = k < 136, (k >= 136) & (k < 204)
    k_row = np.where(is_vec, k // 8, np.where(is_up, (k - 136) % SHARD, -1))
    k_out = np.where(is_vec, k % 8, np.where(is_up, 8 + (k - 136) // SHARD, -1))
    pick = (k_out[None, :] == np.arange(16)[:, None]).astype(np.float32)
    spread = (np.arange(NDP)[:, None] == shard_of[None, :]).astype(np.float32)
    keep = (k_row[:, None] == row_of[None, :]).astype(np.float32)
    nat = np.arange(PAD)
    spread_nat = (np.arange(NDP)[:, None] == nat[None, :] // SHARD).astype(np.float32)
    keep_nat = (k_row[:, None] == nat[None, :] % SHARD).astype(np.float32)
    m = np.arange(MAIN)
    turn = np.zeros((MAIN, MAIN), np.float32)
    turn[(m % 16) * NDP + m // 16, m] = 1
    names = ("order", "hid", "pick", "spread", "keep", "spread_nat", "keep_nat", "turn")
    values = (order, hid, pick, spread, keep, spread_nat, keep_nat, turn)
    found = {name: jnp.asarray(value, BF) for name, value in zip(names, values)}
    found["order_d"] = jnp.asarray(order[:D], BF)
    found["hid_t"] = jnp.asarray(hid.T, BF)
    return found


def matmul(a, b):
    return jnp.dot(a, b, preferred_element_type=F32)


def dot_t(a, b):
    return lax.dot_general(a, b, (((1,), (1,)), ((), ())), preferred_element_type=F32)


def t_dot(a, b):
    return lax.dot_general(a, b, (((0,), (0,)), ((), ())), preferred_element_type=F32)


def norm_parts(features):
    centred = features - jnp.mean(features, axis=-1, keepdims=True)
    inverse = lax.rsqrt(jnp.mean(centred * centred, axis=-1, keepdims=True) + NORM_EPSILON)
    return centred * inverse, inverse


def norm_back(gradient, normed, inverse, gain):
    scaled = gradient * gain
    centred = scaled - jnp.mean(scaled, axis=-1, keepdims=True)
    return inverse * (centred - normed * jnp.mean(scaled * normed, axis=-1, keepdims=True))


def col_sum(v):
    return jnp.sum(v, axis=0, keepdims=True)


def unpack_kernel(whole, *refs):
    given, (tails, vecs, nat), (raw, table, *held), sems = refs[:6], refs[6:9], refs[9:17], refs[17]
    copies = [pltpu.make_async_copy(whole.at[:, pl.ds(TAIL0, TAILW)], raw, sems.at[0])]
    for i, (source, target) in enumerate(zip(given, held)):
        copies.append(pltpu.make_async_copy(source, target, sems.at[1 + i]))
    for copy in copies:
        copy.start()
    turn, pick, spread, keep, spread_nat, keep_nat = held
    copies[0].wait()
    copies[1].wait()
    turned = matmul(turn[...], raw[...]).astype(BF)
    for j in range(16):
        table[:, j * TAILW : (j + 1) * TAILW] = turned[j * NDP : (j + 1) * NDP]
    out = pltpu.make_async_copy(table, tails, sems.at[7])
    out.start()
    for copy in copies[2:]:
        copy.wait()
    small = table[:, TAIL0 : TAIL0 + SMALLS]
    for result, s, k in ((vecs, spread, keep), (nat, spread_nat, keep_nat)):
        wide_rows = t_dot(small, s[...]) * k[...].astype(F32)
        result[...] = matmul(pick[...], wide_rows.astype(BF))
    out.wait()


def unpack(whole, c):
    vm = pl.BlockSpec(memory_space=pltpu.VMEM)
    hbm = pl.BlockSpec(memory_space=pl.ANY)
    consts = [c[k] for k in ("turn", "pick", "spread", "keep", "spread_nat", "keep_nat")]
    table = (NDP, 16 * TAILW)
    return pl.pallas_call(
        unpack_kernel,
        in_specs=[hbm] * 7,
        out_specs=[hbm, vm, vm],
        out_shape=[
            jax.ShapeDtypeStruct(table, BF),
            jax.ShapeDtypeStruct((16, D), F32),
            jax.ShapeDtypeStruct((16, PAD), F32),
        ],
        scratch_shapes=[pltpu.VMEM((MAIN, TAILW), BF), pltpu.VMEM(table, BF)]
        + [pltpu.VMEM(v.shape, BF) for v in consts]
        + [pltpu.SemaphoreType.DMA((8,))],
        compiler_params=pltpu.CompilerParams(vmem_limit_bytes=VMEM_BYTES),
        name="unpack",
    )(whole, *consts)


class Weights:
    def __init__(self, whole, tails, buf, sems, kind):
        self.whole, self.tails, self.buf, self.sems, self.kind = whole, tails, buf, sems, kind

    def block(self, p):
        if self.kind == "bwd":
            pair = (p % 2 == 0) * DOWN + p // 2
            rest = OUT * (p == 8) + (p - 1) * (p > 8)
            return pair * (p < 8) + rest * (p >= 8)
        q = p - 4
        return (p < 4) * (QKV + p) + (p >= 4) * ((q % 2) * DOWN + q // 2)

    def copies(self, p):
        b = self.block(p)
        cols = pl.ds(pl.multiple_of(b * PAD, 128), PAD)
        return (
            pltpu.make_async_copy(
                self.whole.at[:, cols], self.buf.at[b, pl.ds(0, MAIN)], self.sems.at[b, 0]
            ),
            pltpu.make_async_copy(
                self.tails.at[:, cols], self.buf.at[b, pl.ds(MAIN, NDP)], self.sems.at[b, 1]
            ),
        )

    def start(self, p):
        for copy in self.copies(p):
            copy.start()

    def begin(self):
        for p in range(WINDOW):
            self.start(p)

    def wait(self, p):
        for copy in self.copies(p):
            copy.wait()
        if isinstance(p, int):
            if p + WINDOW < BLOCKS:
                self.start(p + WINDOW)
        else:

            @pl.when(p + WINDOW < BLOCKS)
            def _():
                self.start(p + WINDOW)


def pair_masks():
    lane = lax.broadcasted_iota(jnp.int32, (ROWS, 128), 1)
    first = (lane < HDIM).astype(F32)
    return first, 1.0 - first


def stacked(v, masks):
    return jnp.concatenate([(v * m).astype(BF) for m in masks], axis=0)


def soft_pair(q, kk, allowed):
    scores = dot_t(q, kk) * SCORE_SCALE
    halves = []
    for h in range(2):
        s = jnp.where(allowed, scores[:, h * ROWS : (h + 1) * ROWS], -1e30)
        e = jnp.exp(s - jnp.max(s, axis=-1, keepdims=True))
        halves.append(e / jnp.sum(e, axis=-1, keepdims=True))
    return halves


def forward_part(w, send, x_ref, place, pairs_ref, vecs, nat, order, r):
    x = x_ref[...].astype(F32)
    normed, _ = norm_parts(x)
    r["attn_in"][0, :, :D] = (normed * vecs[0:1] + vecs[1:2]).astype(BF)

    def project(i, carry):
        w.wait(i)
        shift = jnp.where(i == 0, nat[2:3], jnp.where(i == 2, nat[3:4], 0.0))
        r["packed"][i] = (matmul(r["attn_in"][0, :, :D], w.buf[QKV + i]) + shift).astype(BF)
        return carry

    lax.fori_loop(0, 3, project, 0)
    send("packed")
    masks = pair_masks()
    allowed = pairs_ref[...] > 0
    for p in range(PAIRS):
        cols = pl.ds(p * 128, 128)
        kk = stacked(r["packed"][1, :, cols].astype(F32), masks)
        vv = stacked(r["packed"][2, :, cols].astype(F32), masks)
        halves = soft_pair(r["packed"][0, :, cols], kk, allowed)
        soft = jnp.concatenate([h.astype(BF) for h in halves], axis=1)
        r["heads"][:, cols] = matmul(soft, vv).astype(BF)
    order.wait()
    mixed = matmul(r["heads"][...], order.ref[...]).astype(BF)
    r["attn_in"][1, :, :D] = mixed
    w.wait(3)
    branch = matmul(mixed, w.buf[OUT])[:, :D]
    middle = x + branch + vecs[4:5]
    r["middle"][...] = middle
    send("middle")
    normed, _ = norm_parts(middle)
    r["second"][:, :D] = (normed * vecs[5:6] + vecs[6:7]).astype(BF)
    r["acc"][...] = jnp.zeros((ROWS, PAD), F32)

    def feed(a, carry):
        w.wait(4 + 2 * a)
        hidden = matmul(r["second"][:, :D], w.buf[UP + a])[:, :D] + vecs[pl.ds(8 + a, 1)]
        r["hidden"][a] = hidden
        bent = jnp.tanh(GELU_C * (hidden + GELU_A * (hidden * hidden * hidden)))
        r["active"][a, :, :D] = (0.5 * hidden * (1.0 + bent)).astype(BF)
        w.wait(5 + 2 * a)
        r["acc"][...] += matmul(r["active"][a, :, :D], w.buf[DOWN + a])
        return carry

    lax.fori_loop(0, 4, feed, 0)
    r["result"][...] = (r["middle"][...] + r["acc"][:, :D] + vecs[7:8]).astype(BF)
    send("hidden")
    send("early")


def backward_part(w, wait, send, grad_ref, x_ref, place, pairs_ref, vecs, order, r):
    grad = grad_ref[...]
    dres = grad.astype(F32)
    r["acc"][...] = jnp.zeros((ROWS, PAD), F32)

    def feed(a, carry):
        if wait:
            w.wait(2 * a)
        dactive = dot_t(grad_ref[...], w.buf[DOWN + a, :, :D])
        h = r["hidden"][a]
        square = h * h
        bent = jnp.tanh(GELU_C * (h + GELU_A * (square * h)))
        slope = 0.5 * (1.0 + bent) + (0.5 * GELU_C) * h * (1.0 - bent * bent) * (
            1.0 + (3 * GELU_A) * square
        )
        dhidden = (dactive * slope).astype(BF)
        r["dhidden"][a, :, :D] = dhidden
        r["small"][pl.ds(8 + a, 1)] = col_sum(dhidden.astype(F32))
        if wait:
            w.wait(2 * a + 1)
        r["acc"][:, :D] += dot_t(dhidden, w.buf[UP + a, :, :D])
        return carry

    lax.fori_loop(0, 4, feed, 0)
    send("late_first")
    dsecond = r["acc"][:, :D]
    normed, inverse = norm_parts(r["middle"][...])
    r["small"][5:6] = col_sum(dsecond * normed)
    r["small"][6:7] = col_sum(dsecond)
    r["small"][7:8] = col_sum(dres)
    dmiddle = dres + norm_back(dsecond, normed, inverse, vecs[5:6])
    r["middle"][...] = dmiddle
    dattn = dmiddle.astype(BF)
    r["dpacked"][3, :, :D] = dattn
    r["small"][4:5] = col_sum(dattn.astype(F32))
    if wait:
        w.wait(8)
    dmixed = dot_t(dattn, w.buf[OUT, :, :D]).astype(BF)
    if wait:
        order.wait()
    r["heads"][...] = dot_t(dmixed, order.ref[...]).astype(BF)
    masks = pair_masks()
    allowed = pairs_ref[...] > 0
    for p in range(PAIRS):
        cols = pl.ds(p * 128, 128)
        width = min(D - p * 128, 128)
        live = pl.ds(p * 128, width)
        q = r["packed"][0, :, cols]
        kk = stacked(r["packed"][1, :, cols].astype(F32), masks)
        vv = stacked(r["packed"][2, :, cols].astype(F32), masks)
        dm = r["heads"][:, cols]
        halves = soft_pair(q, kk, allowed)
        dsoft = dot_t(dm, vv)
        dscores = []
        for h, p_half in enumerate(halves):
            d_half = dsoft[:, h * ROWS : (h + 1) * ROWS]
            centre = jnp.sum(d_half * p_half, axis=-1, keepdims=True)
            dscores.append((p_half * (d_half - centre)).astype(BF))
        ds = jnp.concatenate(dscores, axis=1)
        soft = jnp.concatenate([h.astype(BF) for h in halves], axis=1)
        dq = matmul(ds, kk) * SCORE_SCALE
        dk = t_dot(ds, q) * SCORE_SCALE
        dv = t_dot(soft, dm)
        dk = dk[:ROWS] * masks[0] + dk[ROWS:] * masks[1]
        dv = dv[:ROWS] * masks[0] + dv[ROWS:] * masks[1]
        for i, v in enumerate((dq, dk, dv)):
            r["dpacked"][i, :, live] = v[:, :width].astype(BF)
    send("late_second")
    sums = [col_sum(r["dpacked"][i, :, :D].astype(F32)) for i in (0, 2)]
    sums = jnp.concatenate(sums + [jnp.zeros((14, D), F32)], axis=0).astype(BF)
    r["small"][2:4] = matmul(sums, order.ref[:D])[:2]
    r["acc"][...] = jnp.zeros((ROWS, PAD), F32)

    def project(i, carry):
        if wait:
            w.wait(9 + i)
        r["acc"][:, :D] += dot_t(r["dpacked"][i, :, :D], w.buf[QKV + i, :, :D])
        return carry

    lax.fori_loop(0, 3, project, 0)
    dentry = r["acc"][:, :D]
    normed, inverse = norm_parts(x_ref[...].astype(F32))
    r["small"][0:1] = col_sum(dentry * normed)
    r["small"][1:2] = col_sum(dentry)
    r["small"][12:16] = jnp.zeros((4, D), F32)
    r["dx"][...] = (r["middle"][...] + norm_back(dentry, normed, inverse, vecs[0:1])).astype(BF)


ROW = (ROWS, D)
WIDEROW = (ROWS, PAD)
KEPT = {
    "packed": ((3,) + WIDEROW, BF),
    "middle": (ROW, F32),
    "hidden": ((4,) + ROW, F32),
}
EARLY = {f"early{d}": ((3,) + WIDEROW, BF) for d in range(4)}
LATE = {f"late{d}": ((2,) + WIDEROW, BF) for d in range(4)}
RESULT = {"result": (ROW, BF)}
GRADS = {"dx": (ROW, BF), "small": ((16, D), F32)}
FWD_WORK = {
    "attn_in": ((2,) + WIDEROW, BF),
    "second": (WIDEROW, BF),
    "active": ((4,) + WIDEROW, BF),
}
BWD_WORK = {
    "dhidden": ((4,) + WIDEROW, BF),
    "dpacked": ((4,) + WIDEROW, BF),
}
WORK = {"heads": (WIDEROW, BF), "acc": (WIDEROW, F32)}


class Fetched:
    def __init__(self, source, ref, sem):
        self.ref, self.copy = ref, pltpu.make_async_copy(source, ref, sem)

    def start(self):
        self.copy.start()

    def wait(self):
        self.copy.wait()


def layer_call(kind, whole, tails, vecs, nat, pairs, order, place, x, grad=None, old=None):
    near_out = {"fwd": RESULT, "both": {**RESULT, **GRADS}, "bwd": GRADS}[kind]
    far_out = {"fwd": {**EARLY, **KEPT}, "both": {**EARLY, **LATE}, "bwd": LATE}[kind]
    outs = {**near_out, **far_out}
    work = {**WORK, **KEPT}
    if kind != "bwd":
        work.update(FWD_WORK)
    if kind != "fwd":
        work.update(BWD_WORK)
    passed = {"fwd": {}, "both": {**RESULT, **EARLY}, "bwd": {**GRADS, **LATE}}[kind]
    loaded = KEPT if kind == "bwd" else {}
    far = [whole, tails, order] + [old[k] for k in (*passed, *loaded)]
    near = [vecs, nat, pairs, x] + ([] if grad is None else [grad])
    section = 1 if kind == "both" else 0

    def kernel(place_ref, *refs):
        far_refs, refs = refs[: len(far)], refs[len(far) :]
        near_refs, refs = refs[: len(near)], refs[len(near) :]
        out = dict(zip(outs, refs))
        refs = refs[len(outs) :]
        r = {**dict(zip(work, refs)), **{k: out[k] for k in near_out}}
        buf, order_buf, sems, old_sems, order_sem, out_sems = refs[len(work) :]
        w = Weights(far_refs[0], far_refs[1], buf, sems, kind)
        order_in = Fetched(far_refs[2], order_buf, order_sem)
        vecs_ref, nat_ref, pairs_ref, x_ref = near_refs[:4]
        old_refs = dict(zip((*passed, *loaded), far_refs[3:]))
        sent = []

        def send(name):
            if name in KEPT:
                moves = [(r[name], out[name])] if name in out else []
            else:
                moves = []
                for d in range(4):
                    z = lax.rem(place_ref[2] + d, 4)
                    if name == "early":
                        sources = (r["second"], r["active"].at[z], r["attn_in"].at[z // 3])
                        moves += [(v, out[f"early{d}"].at[i]) for i, v in enumerate(sources)]
                    elif name == "late_first":
                        moves.append((r["dhidden"].at[z], out[f"late{d}"].at[0]))
                    else:
                        moves.append((r["dpacked"].at[z], out[f"late{d}"].at[1]))
            for source, target in moves:
                copy = pltpu.make_async_copy(source, target, out_sems.at[len(sent)])
                copy.start()
                sent.append(copy)

        @pl.when(place_ref[3] == section)
        def _():
            fetched = [
                Fetched(old_refs[k], r[k], old_sems.at[i]) for i, k in enumerate(loaded)
            ]
            for copy in fetched:
                copy.start()
            w.begin()
            order_in.start()
            if kind != "bwd":
                forward_part(
                    w, send, x_ref, place_ref, pairs_ref, vecs_ref, nat_ref, order_in, r
                )
            for copy in fetched:
                copy.wait()
            if kind != "fwd":
                backward_part(
                    w,
                    kind == "bwd",
                    send,
                    near_refs[4],
                    x_ref,
                    place_ref,
                    pairs_ref,
                    vecs_ref,
                    order_in,
                    r,
                )
            for copy in sent:
                copy.wait()

        if passed:

            @pl.when(place_ref[3] != section)
            def _():
                into, back = [], []
                for i, k in enumerate(passed):
                    if k in near_out:
                        into.append(pltpu.make_async_copy(old_refs[k], out[k], old_sems.at[i]))
                        continue
                    for j in range(passed[k][0][0]):
                        held = buf.at[i, pl.ds(j * ROWS, ROWS)]
                        n = len(back)
                        into.append(
                            pltpu.make_async_copy(old_refs[k].at[j], held, out_sems.at[n])
                        )
                        back.append(
                            pltpu.make_async_copy(held, out[k].at[j], out_sems.at[16 + n])
                        )
                for copies in (into, back):
                    for copy in copies:
                        copy.start()
                    for copy in copies:
                        copy.wait()

    vm = pl.BlockSpec(memory_space=pltpu.VMEM)
    hbm = pl.BlockSpec(memory_space=pl.ANY)
    results = pl.pallas_call(
        kernel,
        in_specs=[pl.BlockSpec(memory_space=pltpu.SMEM)] + [hbm] * len(far) + [vm] * len(near),
        out_specs=[vm] * len(near_out) + [hbm] * len(far_out),
        out_shape=[jax.ShapeDtypeStruct(s, t) for s, t in outs.values()],
        scratch_shapes=[pltpu.VMEM(s, t) for s, t in work.values()]
        + [
            pltpu.VMEM((BLOCKS, D, PAD), BF),
            pltpu.VMEM((PAD, D), BF),
            pltpu.SemaphoreType.DMA((BLOCKS, 2)),
            pltpu.SemaphoreType.DMA((8,)),
            pltpu.SemaphoreType.DMA,
            pltpu.SemaphoreType.DMA((32,)),
        ],
        compiler_params=pltpu.CompilerParams(vmem_limit_bytes=VMEM_BYTES),
        cost_estimate=pl.CostEstimate(
            flops={"fwd": 4, "both": 12, "bwd": 8}[kind] * 10**9,
            bytes_accessed=BLOCKS * D * PAD * 2,
            transcendentals=10**6,
        ),
        name="layer_" + kind,
    )(place, *far, *near)
    return dict(zip(outs, results))


CHUNK = 72
PART = 384
WIDE = (PAD + PART, PAD + PAD - PART)


def block(width):
    return ((4, CHUNK, width), BF)


def local_call(kernel, name, place, ins, out_shapes, scratch=(), far=(), far_out=False):
    vm = pl.BlockSpec(memory_space=pltpu.VMEM)
    hbm = pl.BlockSpec(memory_space=pl.ANY)
    return pl.pallas_call(
        kernel,
        in_specs=[pl.BlockSpec(memory_space=pltpu.SMEM)] + [hbm] * len(far) + [vm] * len(ins),
        out_specs=[hbm if far_out else vm] * len(out_shapes),
        out_shape=[jax.ShapeDtypeStruct(s, t) for s, t in out_shapes],
        scratch_shapes=list(scratch),
        compiler_params=pltpu.CompilerParams(vmem_limit_bytes=VMEM_BYTES),
        name=name,
    )(place, *far, *ins)


def product(a, b, store):
    last = t_dot(a[:, MAIN:], b)
    nothing = jnp.zeros((4, PAD), F32)
    for x in range(4):
        main = t_dot(a[:, x * 256 : (x + 1) * 256], b)
        for y in range(4):
            at = (x * 4 + y) * 4
            rows = [main[y * 64 : (y + 1) * 64], last[at : at + 4], nothing]
            store(x, y, jnp.concatenate(rows, axis=0).astype(BF))


def send_blocks(held, first, outs, sems, cols=None):
    copies = []
    for d in range(4):
        source, target = held.at[lax.rem(first + d, 4)], outs[d]
        if cols is not None:
            source, target = source.at[:, :, cols], target.at[:, :, cols]
        copies.append(pltpu.make_async_copy(source, target, sems.at[d]))
        copies[-1].start()
    return copies


def load(sources, held, sems, other=None, use_other=None):
    copies = []
    for d in range(4):
        copies.append(pltpu.make_async_copy(sources[d], held.at[d], sems.at[d]))
        if other is None:
            copies[d].start()
            continue
        pl.when(jnp.logical_not(use_other))(copies[d].start)
        pl.when(use_other)(pltpu.make_async_copy(other[d], held.at[d], sems.at[d]).start)

    def rows():
        for copy in copies:
            copy.wait()
        return jnp.concatenate([held[d, :, :D] for d in range(4)], axis=0)

    return rows


def wide(v):
    return jnp.concatenate([v, jnp.zeros((v.shape[0], PAD - D), v.dtype)], axis=1)


def down_products_kernel(place, *refs):
    early, branch, cots, outs = refs[:4], refs[4:8], refs[8:12], refs[12:16]
    held, a_held, b_held, sems = refs[16:]
    a = load([e.at[1] for e in early], a_held, sems.at[0])
    b = load(branch, b_held, sems.at[1], cots, place[3] == 1)

    def store(x, y, v):
        held[y, x] = v

    product(a(), wide(b()), store)
    for copy in send_blocks(held, place[1], outs, sems.at[2]):
        copy.wait()


def products_kernel(place, *refs):
    early, late, small, outs = refs[:4], refs[4:8], refs[8], refs[9:17]
    first, second, held, sems = refs[17:]
    a_up = load([e.at[0] for e in early], held.at[0], sems.at[0])
    b_up = load([v.at[0] for v in late], held.at[1], sems.at[1])
    a_attn = load([e.at[2] for e in early], held.at[2], sems.at[2])
    b_attn = load([v.at[1] for v in late], held.at[3], sems.at[3])
    slot = lax.broadcasted_iota(jnp.int32, (16, PAD), 1) - D
    unit = (slot == lax.broadcasted_iota(jnp.int32, (16, PAD), 0)).astype(F32).astype(BF)

    def store_up(x, y, v):
        first[x, y, :, :PAD] = v

    def store_attn(x, y, v):
        first[x, y, :, PAD:] = v[:, :PART]
        second[y, x] = v[:, PART:]

    product(a_up(), wide(b_up()), store_up)
    copies = send_blocks(first, place[0], outs[:4], sems.at[4], pl.ds(0, PAD))
    a = jnp.concatenate([a_attn(), small[...].astype(BF)], axis=0)
    b = jnp.concatenate([wide(b_attn()), unit], axis=0)
    product(a, b, store_attn)
    copies += send_blocks(first, place[0], outs[:4], sems.at[5], pl.ds(PAD, PART))
    copies += send_blocks(second, place[1], outs[4:], sems.at[6])
    for copy in copies:
        copy.wait()


def total(parts):
    return sum((p.astype(F32) for p in parts[1:]), parts[0].astype(F32))


def first_sum_kernel(place, *refs):
    given, outs, held, sems = refs[:12], refs[12:20], refs[20:23], refs[23]
    copies = {}
    for d in range(4):
        for g, other in ((1, 0), (0, 1), (2, 0)):
            i = lax.rem(place[other] + d, 4)
            copies[g, d] = [
                pltpu.make_async_copy(given[4 * g + k].at[i], held[g].at[d, k], sems.at[g, d, k])
                for k in range(4)
            ]
            for copy in copies[g, d]:
                copy.start()
    for d in range(4):
        for g, h, start in ((1, 1, 0), (0, 0, 0), (2, 1, PAD)):
            for copy in copies[g, d]:
                copy.wait()
            summed = total([held[g][d, k] for k in range(4)]).astype(BF)
            outs[4 * h + d][:, start : start + summed.shape[1]] = summed


def second_sum_kernel(place, *refs):
    outs, held = refs[8:12], refs[12]
    for h in range(2):
        full = total([p[...] for p in refs[4 * h : 4 * h + 4]])
        start = h * WIDE[0]
        empty = jnp.zeros((7, WIDE[h]), F32)
        for z in range(4):
            rows = [full[z * 16 : (z + 1) * 16], full[64 + z : 65 + z], empty]
            held[z, :, start : start + WIDE[h]] = jnp.concatenate(rows, axis=0).astype(BF)
    for d in range(4):
        outs[d][...] = held[lax.rem(place[2] + d, 4)]


def final_kernel(place, *refs):
    hid_in, order_in, parts, outs = refs[0], refs[1], refs[2:6], refs[6:11]
    held, hid, order, sems = refs[11:]
    g_up, g_down, g_out, g_qkv, sums = outs
    hid_copy = pltpu.make_async_copy(hid_in, hid, sems.at[0])
    order_copy = pltpu.make_async_copy(order_in, order, sems.at[1])
    hid_copy.start()
    order_copy.start()
    for d in range(4):
        held[lax.rem(place[2] + 4 - d, 4)] = parts[d][...]
    up = []
    for j in range(4):
        pieces = [held[a, :, j * 256 : (j + 1) * 256] for a in range(4)]
        pieces += [held[a, :, MAIN + j * 16 : MAIN + (j + 1) * 16] for a in range(4)]
        up.append(jnp.concatenate(pieces, axis=1))
    hid_copy.wait()
    up = matmul(jnp.concatenate(up, axis=0), hid[...])
    up = jnp.concatenate([up[j * 24 : (j + 1) * 24] for j in range(4)], axis=1)
    for i in range(SHARD):
        g_up[i] = up[i : i + 1]
    start = WIDE[0]
    attn = [
        jnp.concatenate([held[a, :, PAD:start], held[a, :, start + PAD :]], axis=1)
        for a in range(4)
    ]
    rows = [held[a, :, start : start + D] for a in range(4)] + [attn[3][:, :D]]
    order_copy.wait()
    rows = dot_t(jnp.concatenate(rows, axis=0), order[:D])
    qkv = jnp.concatenate([v[:, :D].astype(F32) for v in attn[:3]], axis=1)
    for i in range(SHARD):
        for a in range(4):
            g_down[a * SHARD + i] = rows[a * 24 + i : a * 24 + i + 1]
        g_out[i] = rows[96 + i : 97 + i]
        g_qkv[i] = qkv[i : i + 1]
    sums[...] = total([v[:SHARD, D:] for v in attn])


def ring(v, axis, d):
    return lax.ppermute(v, axis, [(i, (i + d) % 4) for i in range(4)])


def ring_of_first(v, d):
    return lax.ppermute(v, ("section", "z"), [(i, (i + d) % 4) for i in range(4)])


def restore_kernel(place, order, result, dx, acts, grads):
    acts[...] = dot_t(result[...], order[:D]).astype(BF)
    grads[...] = dot_t(dx[...], order[:D]).astype(BF)


def pad_cols(v, width):
    return jnp.pad(v, ((0, 0), (0, width - v.shape[1])))


def body(inputs, cotangent, lengths, vectors, qkv_w, out_w, up_w, up_b, down_w):
    section = lax.axis_index("section")
    mb, rows, _ = inputs.shape
    n = mb * rows
    c = constants()
    order = c["order"]

    outdown = matmul(jnp.concatenate([out_w[0], down_w[0]], axis=0), c["order_d"]).astype(BF)
    hid = matmul(up_w[0].reshape(SHARD * 4, D), c["hid"]).astype(BF).reshape(SHARD, 4, D)
    hid_main = hid[:, :, :MAIN].reshape(SHARD, 4, 4, 256).transpose(0, 2, 1, 3)
    hid_last = hid[:, :, MAIN:].reshape(SHARD, 4, 4, 16).transpose(0, 2, 1, 3)
    hid = jnp.concatenate(
        [
            hid_main.reshape(SHARD, 4, MAIN),
            hid_last.reshape(SHARD, 4, NDP),
            jnp.zeros((SHARD, 4, PAD - D), BF),
        ],
        axis=2,
    )
    shard = [hid.reshape(SHARD, 4 * PAD)]
    shard += [pad_cols(outdown[SHARD * (1 + a) : SHARD * (2 + a)], PAD) for a in range(4)]
    shard += [pad_cols(qkv_w[0][:, i * D : (i + 1) * D], PAD) for i in range(3)]
    shard += [pad_cols(outdown[:SHARD], PAD)]
    shard = jnp.concatenate(shard, axis=1)
    tail = jnp.concatenate([shard[16], vectors[0].reshape(-1), up_b[0]])
    tail = jnp.pad(tail, (0, 16 * TAILW - tail.shape[0])).reshape(16, TAILW)
    sent = jnp.concatenate([shard[:16], tail], axis=1)
    whole = lax.all_gather(sent, ("x", "y", "z"), axis=0, tiled=True)
    order_d = c["order_d"]
    cot = matmul(cotangent.reshape(n, D), order_d).astype(BF)
    cots = [cot] + [ring(cot, "z", d) for d in (1, 3, 2)]
    whole, cots = lax.optimization_barrier((whole, cots))
    tails, vecs, nat = unpack(whole, c)

    ends = jnp.cumsum(lengths[:, 0], axis=1)
    place = jnp.arange(rows, dtype=jnp.int32)
    seg = jnp.sum((place[None, :, None] >= ends[:, None, :]).astype(jnp.int32), axis=2)
    seg = (seg + 8 * jnp.arange(mb, dtype=jnp.int32)[:, None]).reshape(n)
    at = jnp.arange(n, dtype=jnp.int32)
    pairs = ((seg[:, None] == seg[None, :]) & (at[:, None] >= at[None, :])).astype(F32)

    x0 = matmul(inputs.reshape(n, D), order_d).astype(BF)
    place = jnp.stack([lax.axis_index("x"), lax.axis_index("y"), lax.axis_index("z"), section])
    call = functools.partial(
        layer_call,
        whole=whole,
        tails=tails,
        vecs=vecs,
        nat=nat,
        pairs=pairs,
        order=order,
        place=place,
    )

    first = call("fwd", x=x0)
    arrived = lax.ppermute(first["result"], "section", [(0, 1)])
    top = call("both", x=arrived, grad=cot, old=first)
    coming = lax.ppermute(top["dx"], "section", [(1, 0)])
    early = [top["early0"]] + [ring(top[f"early{d}"], "z", d) for d in (1, 3, 2)]
    branches = [coming] + [ring_of_first(coming, d) for d in (1, 3)]
    early[1], held = lax.optimization_barrier((early[1], coming))
    branches.append(ring_of_first(held, 2))
    kept = {k: first[k] for k in KEPT}
    old = {**{k: top[k] for k in (*GRADS, *LATE)}, **kept}
    bwd = call("bwd", x=x0, grad=coming, old=old)
    sends = [bwd[f"late{d}"] for d in (1, 3, 2)]
    early, branches, sends = lax.optimization_barrier((early, branches, sends))
    late = [bwd["late0"]] + [ring(v, "z", d) for v, d in zip(sends, (1, 3, 2))]

    vmem, sem = pltpu.VMEM, pltpu.SemaphoreType.DMA
    down = local_call(
        down_products_kernel,
        "down_products",
        place,
        [],
        [block(PAD)] * 4,
        [vmem((4, 4, CHUNK, PAD), BF), vmem((4,) + WIDEROW, BF), vmem((4,) + ROW, BF), sem((3, 4))],
        far=[*early, *branches, *cots],
        far_out=True,
    )
    late, down = lax.optimization_barrier((late, down))
    small, down = lax.optimization_barrier((bwd["small"], down))
    down = [down[0]] + [ring(down[d], "y", d) for d in (2, 1, 3)]
    out = local_call(
        products_kernel,
        "products",
        place,
        [small],
        [block(WIDE[0])] * 4 + [block(PAD - PART)] * 4,
        [vmem((4, 4, CHUNK, width), BF) for width in (WIDE[0], PAD - PART)]
        + [vmem((4, 4) + WIDEROW, BF), sem((7, 4))],
        far=[*early, *late],
        far_out=True,
    )
    xs, ys = out[:4], out[4:]
    down[1], xs = lax.optimization_barrier((down[1], xs))
    down, ys = lax.optimization_barrier((down, ys))
    up = [xs[0]] + [ring(xs[d], "x", d) for d in (2, 1, 3)]
    attn = [ys[0]] + [ring(ys[d], "y", d) for d in (2, 1, 3)]
    out = local_call(
        first_sum_kernel,
        "first_sum",
        place,
        [],
        [((CHUNK, WIDE[h]), BF) for h in (0, 1) for _ in range(4)],
        [vmem((4, 4, CHUNK, width), BF) for width in (WIDE[0], PAD, PAD - PART)]
        + [sem((3, 4, 4))],
        far=[*up, *down, *attn],
    )
    got = []
    for h, axis in ((0, "y"), (1, "x")):
        got += [out[4 * h]] + [ring(out[4 * h + d], axis, d) for d in (1, 3, 2)]
    out = local_call(
        second_sum_kernel,
        "second_sum",
        place,
        got,
        [((24, sum(WIDE)), BF)] * 4,
        [vmem((4, 24, sum(WIDE)), BF)],
    )
    got = [out[0]] + [ring(out[d], "z", d) for d in (1, 2, 3)]
    g_up, g_down, g_out, g_qkv, sums = local_call(
        final_kernel,
        "owners",
        place,
        got,
        [
            ((SHARD, 1, FF), F32),
            ((4 * SHARD, 1, D), F32),
            ((SHARD, 1, D), F32),
            ((SHARD, 1, 3 * D), F32),
            ((SHARD, PAD - D), F32),
        ],
        [
            vmem((4, 24, sum(WIDE)), BF),
            vmem((D, D), BF),
            vmem((PAD, D), BF),
            pltpu.SemaphoreType.DMA((2,)),
        ],
        far=[c["hid_t"], order],
    )
    acts, grads = local_call(
        restore_kernel, "restore", place, [order, top["result"], bwd["dx"]], [(ROW, BF)] * 2
    )
    return (
        acts.reshape(1, mb, rows, D),
        grads.reshape(1, mb, rows, D),
        sums[None, :, :8],
        g_qkv.reshape(1, SHARD, 3 * D),
        g_out.reshape(1, SHARD, D),
        g_up.reshape(1, SHARD, FF),
        sums[:, 8:12].T.reshape(1, 4 * SHARD),
        g_down.reshape(1, 4 * SHARD, D),
    )


def solution(mesh):
    grid = Mesh(mesh.devices.reshape(2, 4, 4, 4), ("section", "x", "y", "z"))
    dp = ("x", "y", "z")
    tokens = P(None, dp, None)
    rows = P("section", dp, None)
    in_specs = (tokens, tokens, tokens, rows, rows, rows, rows, P("section", dp), rows)
    stacks = P("section", None, dp, None)
    out_specs = (stacks, stacks, rows, rows, rows, rows, P("section", dp), rows)
    return jax.shard_map(body, mesh=grid, in_specs=in_specs, out_specs=out_specs, check_vma=False)
```

```python
import functools

import jax
import jax.numpy as jnp
import numpy as np
from jax import lax
from jax.experimental import pallas as pl
from jax.experimental.pallas import tpu as pltpu
from jax.sharding import Mesh, PartitionSpec as P

HEADS = 17
HDIM = 64
D = HEADS * HDIM
FF = 4 * D
SHARD = 17
NDP = 64
MAIN = 16 * NDP
PAD = 1152
ROWS = 128
PAIRS = PAD // 128

UP, DOWN, QKV, OUT, BLOCKS = 0, 4, 8, 11, 12
TAIL0 = BLOCKS * PAD
TAILW = 896
WIDTH = TAIL0 + TAILW
SMALLS = 256

NORM_EPSILON = 1e-05
SCORE_SCALE = 0.125
GELU_C = float(np.sqrt(2 / np.pi))
GELU_A = 0.044715
BF = jnp.bfloat16
F32 = jnp.float32
WINDOW = 3
VMEM_BYTES = 58 * 1024 * 1024


def constants():
    n = np.arange(D)
    shard_of = np.where(n < MAIN, n // 16, n - MAIN)
    row_of = np.where(n < MAIN, n % 16, 16)
    order = np.zeros((PAD, D), np.float32)
    order[shard_of * SHARD + row_of, n] = 1
    f = np.arange(D)
    s, a, r = f // 68, (f % 68) // SHARD, f % SHARD
    hid = np.zeros((D, D), np.float32)
    hid[f, np.where(r < 16, a * 256 + s * 16 + r, 1024 + a * 16 + s)] = 1
    k = np.arange(SMALLS)
    is_vec, is_up = k < 136, (k >= 136) & (k < 204)
    k_row = np.where(is_vec, k // 8, np.where(is_up, (k - 136) % SHARD, -1))
    k_out = np.where(is_vec, k % 8, np.where(is_up, 8 + (k - 136) // SHARD, -1))
    pick = (k_out[None, :] == np.arange(16)[:, None]).astype(np.float32)
    spread = (np.arange(NDP)[:, None] == shard_of[None, :]).astype(np.float32)
    keep = (k_row[:, None] == row_of[None, :]).astype(np.float32)
    nat = np.arange(PAD)
    spread_nat = (np.arange(NDP)[:, None] == nat[None, :] // SHARD).astype(np.float32)
    keep_nat = (k_row[:, None] == nat[None, :] % SHARD).astype(np.float32)
    m = np.arange(MAIN)
    turn = np.zeros((MAIN, MAIN), np.float32)
    turn[(m % 16) * NDP + m // 16, m] = 1
    names = ("order", "hid", "pick", "spread", "keep", "spread_nat", "keep_nat", "turn")
    values = (order, hid, pick, spread, keep, spread_nat, keep_nat, turn)
    found = {name: jnp.asarray(value, BF) for name, value in zip(names, values)}
    found["order_d"] = jnp.asarray(order[:D], BF)
    found["hid_t"] = jnp.asarray(hid.T, BF)
    return found


def matmul(a, b):
    return jnp.dot(a, b, preferred_element_type=F32)


def dot_t(a, b):
    return lax.dot_general(a, b, (((1,), (1,)), ((), ())), preferred_element_type=F32)


def t_dot(a, b):
    return lax.dot_general(a, b, (((0,), (0,)), ((), ())), preferred_element_type=F32)


def norm_parts(features):
    centred = features - jnp.mean(features, axis=-1, keepdims=True)
    inverse = lax.rsqrt(jnp.mean(centred * centred, axis=-1, keepdims=True) + NORM_EPSILON)
    return centred * inverse, inverse


def norm_back(gradient, normed, inverse, gain):
    scaled = gradient * gain
    centred = scaled - jnp.mean(scaled, axis=-1, keepdims=True)
    return inverse * (centred - normed * jnp.mean(scaled * normed, axis=-1, keepdims=True))


def col_sum(v):
    return jnp.sum(v, axis=0, keepdims=True)


def unpack_kernel(whole, *refs):
    given, (tails, vecs, nat), (raw, table, *held), sems = refs[:6], refs[6:9], refs[9:17], refs[17]
    copies = [pltpu.make_async_copy(whole.at[:, pl.ds(TAIL0, TAILW)], raw, sems.at[0])]
    for i, (source, target) in enumerate(zip(given, held)):
        copies.append(pltpu.make_async_copy(source, target, sems.at[1 + i]))
    for copy in copies:
        copy.start()
    turn, pick, spread, keep, spread_nat, keep_nat = held
    copies[0].wait()
    copies[1].wait()
    turned = matmul(turn[...], raw[...]).astype(BF)
    for j in range(16):
        table[:, j * TAILW : (j + 1) * TAILW] = turned[j * NDP : (j + 1) * NDP]
    out = pltpu.make_async_copy(table, tails, sems.at[7])
    out.start()
    for copy in copies[2:]:
        copy.wait()
    small = table[:, TAIL0 : TAIL0 + SMALLS]
    for result, s, k in ((vecs, spread, keep), (nat, spread_nat, keep_nat)):
        wide_rows = t_dot(small, s[...]) * k[...].astype(F32)
        result[...] = matmul(pick[...], wide_rows.astype(BF))
    out.wait()


def unpack(whole, c):
    vm = pl.BlockSpec(memory_space=pltpu.VMEM)
    hbm = pl.BlockSpec(memory_space=pl.ANY)
    consts = [c[k] for k in ("turn", "pick", "spread", "keep", "spread_nat", "keep_nat")]
    table = (NDP, 16 * TAILW)
    return pl.pallas_call(
        unpack_kernel,
        in_specs=[hbm] * 7,
        out_specs=[hbm, vm, vm],
        out_shape=[
            jax.ShapeDtypeStruct(table, BF),
            jax.ShapeDtypeStruct((16, D), F32),
            jax.ShapeDtypeStruct((16, PAD), F32),
        ],
        scratch_shapes=[pltpu.VMEM((MAIN, TAILW), BF), pltpu.VMEM(table, BF)]
        + [pltpu.VMEM(v.shape, BF) for v in consts]
        + [pltpu.SemaphoreType.DMA((8,))],
        compiler_params=pltpu.CompilerParams(vmem_limit_bytes=VMEM_BYTES),
        name="unpack",
    )(whole, *consts)


class Weights:
    def __init__(self, whole, tails, buf, sems, kind):
        self.whole, self.tails, self.buf, self.sems, self.kind = whole, tails, buf, sems, kind

    def block(self, p):
        if self.kind == "bwd":
            pair = (p % 2 == 0) * DOWN + p // 2
            rest = OUT * (p == 8) + (p - 1) * (p > 8)
            return pair * (p < 8) + rest * (p >= 8)
        q = p - 4
        return (p < 4) * (QKV + p) + (p >= 4) * ((q % 2) * DOWN + q // 2)

    def copies(self, p):
        b = self.block(p)
        cols = pl.ds(pl.multiple_of(b * PAD, 128), PAD)
        return (
            pltpu.make_async_copy(
                self.whole.at[:, cols], self.buf.at[b, pl.ds(0, MAIN)], self.sems.at[b, 0]
            ),
            pltpu.make_async_copy(
                self.tails.at[:, cols], self.buf.at[b, pl.ds(MAIN, NDP)], self.sems.at[b, 1]
            ),
        )

    def start(self, p):
        for copy in self.copies(p):
            copy.start()

    def begin(self):
        for p in range(WINDOW):
            self.start(p)

    def wait(self, p):
        for copy in self.copies(p):
            copy.wait()
        if isinstance(p, int):
            if p + WINDOW < BLOCKS:
                self.start(p + WINDOW)
        else:

            @pl.when(p + WINDOW < BLOCKS)
            def _():
                self.start(p + WINDOW)


def pair_masks():
    lane = lax.broadcasted_iota(jnp.int32, (ROWS, 128), 1)
    first = (lane < HDIM).astype(F32)
    return first, 1.0 - first


def stacked(v, masks):
    return jnp.concatenate([(v * m).astype(BF) for m in masks], axis=0)


def soft_pair(q, kk, allowed):
    scores = dot_t(q, kk) * SCORE_SCALE
    halves = []
    for h in range(2):
        s = jnp.where(allowed, scores[:, h * ROWS : (h + 1) * ROWS], -1e30)
        e = jnp.exp(s - jnp.max(s, axis=-1, keepdims=True))
        halves.append(e / jnp.sum(e, axis=-1, keepdims=True))
    return halves


def forward_part(w, send, x_ref, place, pairs_ref, vecs, nat, order, r):
    x = x_ref[...].astype(F32)
    normed, _ = norm_parts(x)
    r["attn_in"][0, :, :D] = (normed * vecs[0:1] + vecs[1:2]).astype(BF)

    def project(i, carry):
        w.wait(i)
        shift = jnp.where(i == 0, nat[2:3], jnp.where(i == 2, nat[3:4], 0.0))
        r["packed"][i] = (matmul(r["attn_in"][0, :, :D], w.buf[QKV + i]) + shift).astype(BF)
        return carry

    lax.fori_loop(0, 3, project, 0)
    send("packed")
    masks = pair_masks()
    allowed = pairs_ref[...] > 0
    for p in range(PAIRS):
        cols = pl.ds(p * 128, 128)
        kk = stacked(r["packed"][1, :, cols].astype(F32), masks)
        vv = stacked(r["packed"][2, :, cols].astype(F32), masks)
        halves = soft_pair(r["packed"][0, :, cols], kk, allowed)
        soft = jnp.concatenate([h.astype(BF) for h in halves], axis=1)
        r["heads"][:, cols] = matmul(soft, vv).astype(BF)
    order.wait()
    mixed = matmul(r["heads"][...], order.ref[...]).astype(BF)
    r["attn_in"][1, :, :D] = mixed
    w.wait(3)
    branch = matmul(mixed, w.buf[OUT])[:, :D]
    middle = x + branch + vecs[4:5]
    r["middle"][...] = middle
    send("middle")
    normed, _ = norm_parts(middle)
    r["second"][:, :D] = (normed * vecs[5:6] + vecs[6:7]).astype(BF)
    r["acc"][...] = jnp.zeros((ROWS, PAD), F32)

    def feed(a, carry):
        w.wait(4 + 2 * a)
        hidden = matmul(r["second"][:, :D], w.buf[UP + a])[:, :D] + vecs[pl.ds(8 + a, 1)]
        r["hidden"][a] = hidden
        bent = jnp.tanh(GELU_C * (hidden + GELU_A * (hidden * hidden * hidden)))
        r["active"][a, :, :D] = (0.5 * hidden * (1.0 + bent)).astype(BF)
        w.wait(5 + 2 * a)
        r["acc"][...] += matmul(r["active"][a, :, :D], w.buf[DOWN + a])
        return carry

    lax.fori_loop(0, 4, feed, 0)
    r["result"][...] = (r["middle"][...] + r["acc"][:, :D] + vecs[7:8]).astype(BF)
    send("hidden")
    send("early")


def backward_part(w, wait, send, grad_ref, x_ref, place, pairs_ref, vecs, order, r):
    grad = grad_ref[...]
    dres = grad.astype(F32)
    r["acc"][...] = jnp.zeros((ROWS, PAD), F32)

    def feed(a, carry):
        if wait:
            w.wait(2 * a)
        dactive = dot_t(grad_ref[...], w.buf[DOWN + a, :, :D])
        h = r["hidden"][a]
        square = h * h
        bent = jnp.tanh(GELU_C * (h + GELU_A * (square * h)))
        slope = 0.5 * (1.0 + bent) + (0.5 * GELU_C) * h * (1.0 - bent * bent) * (
            1.0 + (3 * GELU_A) * square
        )
        dhidden = (dactive * slope).astype(BF)
        r["dhidden"][a, :, :D] = dhidden
        r["small"][pl.ds(8 + a, 1)] = col_sum(dhidden.astype(F32))
        if wait:
            w.wait(2 * a + 1)
        r["acc"][:, :D] += dot_t(dhidden, w.buf[UP + a, :, :D])
        return carry

    lax.fori_loop(0, 4, feed, 0)
    send("late_first")
    dsecond = r["acc"][:, :D]
    normed, inverse = norm_parts(r["middle"][...])
    r["small"][5:6] = col_sum(dsecond * normed)
    r["small"][6:7] = col_sum(dsecond)
    r["small"][7:8] = col_sum(dres)
    dmiddle = dres + norm_back(dsecond, normed, inverse, vecs[5:6])
    r["middle"][...] = dmiddle
    dattn = dmiddle.astype(BF)
    r["dpacked"][3, :, :D] = dattn
    r["small"][4:5] = col_sum(dattn.astype(F32))
    if wait:
        w.wait(8)
    dmixed = dot_t(dattn, w.buf[OUT, :, :D]).astype(BF)
    if wait:
        order.wait()
    r["heads"][...] = dot_t(dmixed, order.ref[...]).astype(BF)
    masks = pair_masks()
    allowed = pairs_ref[...] > 0
    for p in range(PAIRS):
        cols = pl.ds(p * 128, 128)
        width = min(D - p * 128, 128)
        live = pl.ds(p * 128, width)
        q = r["packed"][0, :, cols]
        kk = stacked(r["packed"][1, :, cols].astype(F32), masks)
        vv = stacked(r["packed"][2, :, cols].astype(F32), masks)
        dm = r["heads"][:, cols]
        halves = soft_pair(q, kk, allowed)
        dsoft = dot_t(dm, vv)
        dscores = []
        for h, p_half in enumerate(halves):
            d_half = dsoft[:, h * ROWS : (h + 1) * ROWS]
            centre = jnp.sum(d_half * p_half, axis=-1, keepdims=True)
            dscores.append((p_half * (d_half - centre)).astype(BF))
        ds = jnp.concatenate(dscores, axis=1)
        soft = jnp.concatenate([h.astype(BF) for h in halves], axis=1)
        dq = matmul(ds, kk) * SCORE_SCALE
        dk = t_dot(ds, q) * SCORE_SCALE
        dv = t_dot(soft, dm)
        dk = dk[:ROWS] * masks[0] + dk[ROWS:] * masks[1]
        dv = dv[:ROWS] * masks[0] + dv[ROWS:] * masks[1]
        for i, v in enumerate((dq, dk, dv)):
            r["dpacked"][i, :, live] = v[:, :width].astype(BF)
    send("late_second")
    sums = [col_sum(r["dpacked"][i, :, :D].astype(F32)) for i in (0, 2)]
    sums = jnp.concatenate(sums + [jnp.zeros((14, D), F32)], axis=0).astype(BF)
    r["small"][2:4] = matmul(sums, order.ref[:D])[:2]
    r["acc"][...] = jnp.zeros((ROWS, PAD), F32)

    def project(i, carry):
        if wait:
            w.wait(9 + i)
        r["acc"][:, :D] += dot_t(r["dpacked"][i, :, :D], w.buf[QKV + i, :, :D])
        return carry

    lax.fori_loop(0, 3, project, 0)
    dentry = r["acc"][:, :D]
    normed, inverse = norm_parts(x_ref[...].astype(F32))
    r["small"][0:1] = col_sum(dentry * normed)
    r["small"][1:2] = col_sum(dentry)
    r["small"][12:16] = jnp.zeros((4, D), F32)
    r["dx"][...] = (r["middle"][...] + norm_back(dentry, normed, inverse, vecs[0:1])).astype(BF)


ROW = (ROWS, D)
WIDEROW = (ROWS, PAD)
KEPT = {
    "packed": ((3,) + WIDEROW, BF),
    "middle": (ROW, F32),
    "hidden": ((4,) + ROW, F32),
}
EARLY = {f"early{d}": ((3,) + WIDEROW, BF) for d in range(4)}
LATE = {f"late{d}": ((2,) + WIDEROW, BF) for d in range(4)}
RESULT = {"result": (ROW, BF)}
GRADS = {"dx": (ROW, BF), "small": ((16, D), F32)}
FWD_WORK = {
    "attn_in": ((2,) + WIDEROW, BF),
    "second": (WIDEROW, BF),
    "active": ((4,) + WIDEROW, BF),
}
BWD_WORK = {
    "dhidden": ((4,) + WIDEROW, BF),
    "dpacked": ((4,) + WIDEROW, BF),
}
WORK = {"heads": (WIDEROW, BF), "acc": (WIDEROW, F32)}


class Fetched:
    def __init__(self, source, ref, sem):
        self.ref, self.copy = ref, pltpu.make_async_copy(source, ref, sem)

    def start(self):
        self.copy.start()

    def wait(self):
        self.copy.wait()


def layer_call(kind, whole, tails, vecs, nat, pairs, order, place, x, grad=None, old=None):
    near_out = {"fwd": RESULT, "both": {**RESULT, **GRADS}, "bwd": GRADS}[kind]
    far_out = {"fwd": {**EARLY, **KEPT}, "both": {**EARLY, **LATE}, "bwd": LATE}[kind]
    outs = {**near_out, **far_out}
    work = {**WORK, **KEPT}
    if kind != "bwd":
        work.update(FWD_WORK)
    if kind != "fwd":
        work.update(BWD_WORK)
    passed = {"fwd": {}, "both": {**RESULT, **EARLY}, "bwd": {**GRADS, **LATE}}[kind]
    loaded = KEPT if kind == "bwd" else {}
    far = [whole, tails, order] + [old[k] for k in (*passed, *loaded)]
    near = [vecs, nat, pairs, x] + ([] if grad is None else [grad])
    section = 1 if kind == "both" else 0

    def kernel(place_ref, *refs):
        far_refs, refs = refs[: len(far)], refs[len(far) :]
        near_refs, refs = refs[: len(near)], refs[len(near) :]
        out = dict(zip(outs, refs))
        refs = refs[len(outs) :]
        r = {**dict(zip(work, refs)), **{k: out[k] for k in near_out}}
        buf, order_buf, sems, old_sems, order_sem, out_sems = refs[len(work) :]
        w = Weights(far_refs[0], far_refs[1], buf, sems, kind)
        order_in = Fetched(far_refs[2], order_buf, order_sem)
        vecs_ref, nat_ref, pairs_ref, x_ref = near_refs[:4]
        old_refs = dict(zip((*passed, *loaded), far_refs[3:]))
        sent = []

        def send(name):
            if name in KEPT:
                moves = [(r[name], out[name])] if name in out else []
            else:
                moves = []
                for d in range(4):
                    z = lax.rem(place_ref[2] + d, 4)
                    if name == "early":
                        sources = (r["second"], r["active"].at[z], r["attn_in"].at[z // 3])
                        moves += [(v, out[f"early{d}"].at[i]) for i, v in enumerate(sources)]
                    elif name == "late_first":
                        moves.append((r["dhidden"].at[z], out[f"late{d}"].at[0]))
                    else:
                        moves.append((r["dpacked"].at[z], out[f"late{d}"].at[1]))
            for source, target in moves:
                copy = pltpu.make_async_copy(source, target, out_sems.at[len(sent)])
                copy.start()
                sent.append(copy)

        @pl.when(place_ref[3] == section)
        def _():
            fetched = [
                Fetched(old_refs[k], r[k], old_sems.at[i]) for i, k in enumerate(loaded)
            ]
            for copy in fetched:
                copy.start()
            w.begin()
            order_in.start()
            if kind != "bwd":
                forward_part(
                    w, send, x_ref, place_ref, pairs_ref, vecs_ref, nat_ref, order_in, r
                )
            for copy in fetched:
                copy.wait()
            if kind != "fwd":
                backward_part(
                    w,
                    kind == "bwd",
                    send,
                    near_refs[4],
                    x_ref,
                    place_ref,
                    pairs_ref,
                    vecs_ref,
                    order_in,
                    r,
                )
            for copy in sent:
                copy.wait()

        if passed:

            @pl.when(place_ref[3] != section)
            def _():
                into, back = [], []
                for i, k in enumerate(passed):
                    if k in near_out:
                        into.append(pltpu.make_async_copy(old_refs[k], out[k], old_sems.at[i]))
                        continue
                    for j in range(passed[k][0][0]):
                        held = buf.at[i, pl.ds(j * ROWS, ROWS)]
                        n = len(back)
                        into.append(
                            pltpu.make_async_copy(old_refs[k].at[j], held, out_sems.at[n])
                        )
                        back.append(
                            pltpu.make_async_copy(held, out[k].at[j], out_sems.at[16 + n])
                        )
                for copies in (into, back):
                    for copy in copies:
                        copy.start()
                    for copy in copies:
                        copy.wait()

    vm = pl.BlockSpec(memory_space=pltpu.VMEM)
    hbm = pl.BlockSpec(memory_space=pl.ANY)
    results = pl.pallas_call(
        kernel,
        in_specs=[pl.BlockSpec(memory_space=pltpu.SMEM)] + [hbm] * len(far) + [vm] * len(near),
        out_specs=[vm] * len(near_out) + [hbm] * len(far_out),
        out_shape=[jax.ShapeDtypeStruct(s, t) for s, t in outs.values()],
        scratch_shapes=[pltpu.VMEM(s, t) for s, t in work.values()]
        + [
            pltpu.VMEM((BLOCKS, D, PAD), BF),
            pltpu.VMEM((PAD, D), BF),
            pltpu.SemaphoreType.DMA((BLOCKS, 2)),
            pltpu.SemaphoreType.DMA((8,)),
            pltpu.SemaphoreType.DMA,
            pltpu.SemaphoreType.DMA((32,)),
        ],
        compiler_params=pltpu.CompilerParams(vmem_limit_bytes=VMEM_BYTES),
        cost_estimate=pl.CostEstimate(
            flops={"fwd": 4, "both": 12, "bwd": 8}[kind] * 10**9,
            bytes_accessed=BLOCKS * D * PAD * 2,
            transcendentals=10**6,
        ),
        name="layer_" + kind,
    )(place, *far, *near)
    return dict(zip(outs, results))


CHUNK = 72
PART = 384
WIDE = (PAD + PART, PAD + PAD - PART)


def block(width):
    return ((4, CHUNK, width), BF)


def local_call(kernel, name, place, ins, out_shapes, scratch=(), far=(), far_out=False):
    vm = pl.BlockSpec(memory_space=pltpu.VMEM)
    hbm = pl.BlockSpec(memory_space=pl.ANY)
    return pl.pallas_call(
        kernel,
        in_specs=[pl.BlockSpec(memory_space=pltpu.SMEM)] + [hbm] * len(far) + [vm] * len(ins),
        out_specs=[hbm if far_out else vm] * len(out_shapes),
        out_shape=[jax.ShapeDtypeStruct(s, t) for s, t in out_shapes],
        scratch_shapes=list(scratch),
        compiler_params=pltpu.CompilerParams(vmem_limit_bytes=VMEM_BYTES),
        name=name,
    )(place, *far, *ins)


def product(a, b, store):
    last = t_dot(a[:, MAIN:], b)
    nothing = jnp.zeros((4, PAD), F32)
    for x in range(4):
        main = t_dot(a[:, x * 256 : (x + 1) * 256], b)
        for y in range(4):
            at = (x * 4 + y) * 4
            rows = [main[y * 64 : (y + 1) * 64], last[at : at + 4], nothing]
            store(x, y, jnp.concatenate(rows, axis=0).astype(BF))


def send_blocks(held, first, outs, sems):
    copies = []
    for d in range(4):
        source = held.at[lax.rem(first + d, 4)]
        copies.append(pltpu.make_async_copy(source, outs[d], sems.at[d]))
        copies[-1].start()
    return copies


def load(sources, held, sems, other=None, use_other=None):
    copies = []
    for d in range(4):
        copies.append(pltpu.make_async_copy(sources[d], held.at[d], sems.at[d]))
        if other is None:
            copies[d].start()
            continue
        pl.when(jnp.logical_not(use_other))(copies[d].start)
        pl.when(use_other)(pltpu.make_async_copy(other[d], held.at[d], sems.at[d]).start)

    def rows():
        for copy in copies:
            copy.wait()
        return jnp.concatenate([held[d, :, :D] for d in range(4)], axis=0)

    return rows


def wide(v):
    return jnp.concatenate([v, jnp.zeros((v.shape[0], PAD - D), v.dtype)], axis=1)


def down_products_kernel(place, *refs):
    early, branch, cots, outs = refs[:4], refs[4:8], refs[8:12], refs[12:16]
    held, a_held, b_held, sems = refs[16:]
    a = load([e.at[1] for e in early], a_held, sems.at[0])
    b = load(branch, b_held, sems.at[1], cots, place[3] == 1)

    def store(x, y, v):
        held[y, x] = v

    product(a(), wide(b()), store)
    for copy in send_blocks(held, place[1], outs, sems.at[2]):
        copy.wait()


def up_products_kernel(place, *refs):
    early, late, outs = refs[:4], refs[4:8], refs[8:12]
    held, a_held, b_held, sems = refs[12:]
    a = load([e.at[0] for e in early], a_held, sems.at[0])
    b = load([v.at[0] for v in late], b_held, sems.at[1])

    def store(x, y, v):
        held[x, y] = v

    product(a(), wide(b()), store)
    for copy in send_blocks(held, place[0], outs, sems.at[2]):
        copy.wait()


def attn_products_kernel(place, *refs):
    early, late, small, outs = refs[:4], refs[4:8], refs[8], refs[9:17]
    first, second, a_held, b_held, sems = refs[17:]
    a = load([e.at[2] for e in early], a_held, sems.at[0])
    b = load([v.at[1] for v in late], b_held, sems.at[1])
    slot = lax.broadcasted_iota(jnp.int32, (16, PAD), 1) - D
    unit = (slot == lax.broadcasted_iota(jnp.int32, (16, PAD), 0)).astype(F32).astype(BF)

    def store(x, y, v):
        first[x, y] = v[:, :PART]
        second[y, x] = v[:, PART:]

    a = jnp.concatenate([a(), small[...].astype(BF)], axis=0)
    b = jnp.concatenate([wide(b()), unit], axis=0)
    product(a, b, store)
    copies = send_blocks(first, place[0], outs[:4], sems.at[2])
    copies += send_blocks(second, place[1], outs[4:], sems.at[3])
    for copy in copies:
        copy.wait()


def total(parts):
    return sum((p.astype(F32) for p in parts[1:]), parts[0].astype(F32))


def first_sum_kernel(place, *refs):
    given, outs, held, sems = refs[:16], refs[16:24], refs[24:28], refs[28]
    copies = {}
    for d in range(4):
        for g, other in ((1, 0), (0, 1), (3, 0), (2, 1)):
            i = lax.rem(place[other] + d, 4)
            copies[g, d] = [
                pltpu.make_async_copy(given[4 * g + k].at[i], held[g].at[d, k], sems.at[g, d, k])
                for k in range(4)
            ]
            for copy in copies[g, d]:
                copy.start()
    for d in range(4):
        for g, h, start in ((1, 1, 0), (0, 0, 0), (3, 1, PAD), (2, 0, PAD)):
            for copy in copies[g, d]:
                copy.wait()
            summed = total([held[g][d, k] for k in range(4)]).astype(BF)
            outs[4 * h + d][:, start : start + summed.shape[1]] = summed


def second_sum_kernel(place, *refs):
    outs, held = refs[8:12], refs[12]
    for h in range(2):
        full = total([p[...] for p in refs[4 * h : 4 * h + 4]])
        start = h * WIDE[0]
        empty = jnp.zeros((7, WIDE[h]), F32)
        for z in range(4):
            rows = [full[z * 16 : (z + 1) * 16], full[64 + z : 65 + z], empty]
            held[z, :, start : start + WIDE[h]] = jnp.concatenate(rows, axis=0).astype(BF)
    for d in range(4):
        outs[d][...] = held[lax.rem(place[2] + d, 4)]


def final_kernel(place, *refs):
    hid_in, order_in, parts, outs = refs[0], refs[1], refs[2:6], refs[6:11]
    held, hid, order, sems = refs[11:]
    g_up, g_down, g_out, g_qkv, sums = outs
    hid_copy = pltpu.make_async_copy(hid_in, hid, sems.at[0])
    order_copy = pltpu.make_async_copy(order_in, order, sems.at[1])
    hid_copy.start()
    order_copy.start()
    for d in range(4):
        held[lax.rem(place[2] + 4 - d, 4)] = parts[d][...]
    up = []
    for j in range(4):
        pieces = [held[a, :, j * 256 : (j + 1) * 256] for a in range(4)]
        pieces += [held[a, :, MAIN + j * 16 : MAIN + (j + 1) * 16] for a in range(4)]
        up.append(jnp.concatenate(pieces, axis=1))
    hid_copy.wait()
    up = matmul(jnp.concatenate(up, axis=0), hid[...])
    up = jnp.concatenate([up[j * 24 : (j + 1) * 24] for j in range(4)], axis=1)
    for i in range(SHARD):
        g_up[i] = up[i : i + 1]
    start = WIDE[0]
    attn = [
        jnp.concatenate([held[a, :, PAD:start], held[a, :, start + PAD :]], axis=1)
        for a in range(4)
    ]
    rows = [held[a, :, start : start + D] for a in range(4)] + [attn[3][:, :D]]
    order_copy.wait()
    rows = dot_t(jnp.concatenate(rows, axis=0), order[:D])
    qkv = jnp.concatenate([v[:, :D].astype(F32) for v in attn[:3]], axis=1)
    for i in range(SHARD):
        for a in range(4):
            g_down[a * SHARD + i] = rows[a * 24 + i : a * 24 + i + 1]
        g_out[i] = rows[96 + i : 97 + i]
        g_qkv[i] = qkv[i : i + 1]
    sums[...] = total([v[:SHARD, D:] for v in attn])


def ring(v, axis, d):
    return lax.ppermute(v, axis, [(i, (i + d) % 4) for i in range(4)])


def restore_kernel(place, order, result, dx, acts, grads):
    acts[...] = dot_t(result[...], order[:D]).astype(BF)
    grads[...] = dot_t(dx[...], order[:D]).astype(BF)


def pad_cols(v, width):
    return jnp.pad(v, ((0, 0), (0, width - v.shape[1])))


def body(inputs, cotangent, lengths, vectors, qkv_w, out_w, up_w, up_b, down_w):
    section = lax.axis_index("section")
    mb, rows, _ = inputs.shape
    n = mb * rows
    c = constants()
    order = c["order"]

    outdown = matmul(jnp.concatenate([out_w[0], down_w[0]], axis=0), c["order_d"]).astype(BF)
    hid = matmul(up_w[0].reshape(SHARD * 4, D), c["hid"]).astype(BF).reshape(SHARD, 4, D)
    hid_main = hid[:, :, :MAIN].reshape(SHARD, 4, 4, 256).transpose(0, 2, 1, 3)
    hid_last = hid[:, :, MAIN:].reshape(SHARD, 4, 4, 16).transpose(0, 2, 1, 3)
    hid = jnp.concatenate(
        [
            hid_main.reshape(SHARD, 4, MAIN),
            hid_last.reshape(SHARD, 4, NDP),
            jnp.zeros((SHARD, 4, PAD - D), BF),
        ],
        axis=2,
    )
    shard = [hid.reshape(SHARD, 4 * PAD)]
    shard += [pad_cols(outdown[SHARD * (1 + a) : SHARD * (2 + a)], PAD) for a in range(4)]
    shard += [pad_cols(qkv_w[0][:, i * D : (i + 1) * D], PAD) for i in range(3)]
    shard += [pad_cols(outdown[:SHARD], PAD)]
    shard = jnp.concatenate(shard, axis=1)
    tail = jnp.concatenate([shard[16], vectors[0].reshape(-1), up_b[0]])
    tail = jnp.pad(tail, (0, 16 * TAILW - tail.shape[0])).reshape(16, TAILW)
    sent = jnp.concatenate([shard[:16], tail], axis=1)
    whole = lax.all_gather(sent, ("x", "y", "z"), axis=0, tiled=True)
    order_d = c["order_d"]
    cot = matmul(cotangent.reshape(n, D), order_d).astype(BF)
    cots = [cot] + [ring(cot, "z", d) for d in (1, 3, 2)]
    whole, cots = lax.optimization_barrier((whole, cots))
    tails, vecs, nat = unpack(whole, c)

    ends = jnp.cumsum(lengths[:, 0], axis=1)
    place = jnp.arange(rows, dtype=jnp.int32)
    seg = jnp.sum((place[None, :, None] >= ends[:, None, :]).astype(jnp.int32), axis=2)
    seg = (seg + 8 * jnp.arange(mb, dtype=jnp.int32)[:, None]).reshape(n)
    at = jnp.arange(n, dtype=jnp.int32)
    pairs = ((seg[:, None] == seg[None, :]) & (at[:, None] >= at[None, :])).astype(F32)

    x0 = matmul(inputs.reshape(n, D), order_d).astype(BF)
    place = jnp.stack([lax.axis_index("x"), lax.axis_index("y"), lax.axis_index("z"), section])
    call = functools.partial(
        layer_call,
        whole=whole,
        tails=tails,
        vecs=vecs,
        nat=nat,
        pairs=pairs,
        order=order,
        place=place,
    )

    first = call("fwd", x=x0)
    arrived = lax.ppermute(first["result"], "section", [(0, 1)])
    top = call("both", x=arrived, grad=cot, old=first)
    coming = lax.ppermute(top["dx"], "section", [(1, 0)])
    early = [top["early0"]] + [ring(top[f"early{d}"], "z", d) for d in (1, 3, 2)]
    branches = [coming] + [ring(coming, "z", d) for d in (1, 3)]
    early[1], held = lax.optimization_barrier((early[1], coming))
    branches.append(ring(held, "z", 2))
    kept = {k: first[k] for k in KEPT}
    old = {**{k: top[k] for k in (*GRADS, *LATE)}, **kept}
    bwd = call("bwd", x=x0, grad=coming, old=old)
    sends = [bwd[f"late{d}"] for d in (1, 3, 2)]
    early, branches, sends = lax.optimization_barrier((early, branches, sends))
    late = [bwd["late0"]] + [ring(v, "z", d) for v, d in zip(sends, (1, 3, 2))]

    vmem, sem = pltpu.VMEM, pltpu.SemaphoreType.DMA
    down = local_call(
        down_products_kernel,
        "down_products",
        place,
        [],
        [block(PAD)] * 4,
        [vmem((4, 4, CHUNK, PAD), BF), vmem((4,) + WIDEROW, BF), vmem((4,) + ROW, BF), sem((3, 4))],
        far=[*early, *branches, *cots],
        far_out=True,
    )
    late, down = lax.optimization_barrier((late, down))
    down = [down[0]] + [ring(down[d], "y", d) for d in (2, 1, 3)]
    up = local_call(
        up_products_kernel,
        "up_products",
        place,
        [],
        [block(PAD)] * 4,
        [vmem((4, 4, CHUNK, PAD), BF)] + [vmem((4,) + WIDEROW, BF)] * 2 + [sem((3, 4))],
        far=[*early, *late],
        far_out=True,
    )
    up = [up[0]] + [ring(up[d], "x", d) for d in (2, 1, 3)]
    out = local_call(
        attn_products_kernel,
        "attn_products",
        place,
        [bwd["small"]],
        [block(PART)] * 4 + [block(PAD - PART)] * 4,
        [vmem((4, 4, CHUNK, width), BF) for width in (PART, PAD - PART)]
        + [vmem((4,) + WIDEROW, BF)] * 2
        + [sem((4, 4))],
        far=[*early, *late],
        far_out=True,
    )
    xs, ys = out[:4], out[4:]
    up[1], xs = lax.optimization_barrier((up[1], xs))
    down[1], ys = lax.optimization_barrier((down[1], ys))
    attn_x = [xs[0]] + [ring(xs[d], "x", d) for d in (2, 1, 3)]
    attn_y = [ys[0]] + [ring(ys[d], "y", d) for d in (2, 1, 3)]
    out = local_call(
        first_sum_kernel,
        "first_sum",
        place,
        [],
        [((CHUNK, WIDE[h]), BF) for h in (0, 1) for _ in range(4)],
        [vmem((4, 4, CHUNK, width), BF) for width in (PAD, PAD, PART, PAD - PART)]
        + [sem((4, 4, 4))],
        far=[*up, *down, *attn_x, *attn_y],
    )
    got = []
    for h, axis in ((0, "y"), (1, "x")):
        got += [out[4 * h]] + [ring(out[4 * h + d], axis, d) for d in (1, 3, 2)]
    out = local_call(
        second_sum_kernel,
        "second_sum",
        place,
        got,
        [((24, sum(WIDE)), BF)] * 4,
        [vmem((4, 24, sum(WIDE)), BF)],
    )
    got = [out[0]] + [ring(out[d], "z", d) for d in (1, 2, 3)]
    g_up, g_down, g_out, g_qkv, sums = local_call(
        final_kernel,
        "owners",
        place,
        got,
        [
            ((SHARD, 1, FF), F32),
            ((4 * SHARD, 1, D), F32),
            ((SHARD, 1, D), F32),
            ((SHARD, 1, 3 * D), F32),
            ((SHARD, PAD - D), F32),
        ],
        [
            vmem((4, 24, sum(WIDE)), BF),
            vmem((D, D), BF),
            vmem((PAD, D), BF),
            pltpu.SemaphoreType.DMA((2,)),
        ],
        far=[c["hid_t"], order],
    )
    acts, grads = local_call(
        restore_kernel, "restore", place, [order, top["result"], bwd["dx"]], [(ROW, BF)] * 2
    )
    return (
        acts.reshape(1, mb, rows, D),
        grads.reshape(1, mb, rows, D),
        sums[None, :, :8],
        g_qkv.reshape(1, SHARD, 3 * D),
        g_out.reshape(1, SHARD, D),
        g_up.reshape(1, SHARD, FF),
        sums[:, 8:12].T.reshape(1, 4 * SHARD),
        g_down.reshape(1, 4 * SHARD, D),
    )


def solution(mesh):
    grid = Mesh(mesh.devices.reshape(2, 4, 4, 4), ("section", "x", "y", "z"))
    dp = ("x", "y", "z")
    tokens = P(None, dp, None)
    rows = P("section", dp, None)
    in_specs = (tokens, tokens, tokens, rows, rows, rows, rows, P("section", dp), rows)
    stacks = P("section", None, dp, None)
    out_specs = (stacks, stacks, rows, rows, rows, rows, P("section", dp), rows)
    return jax.shard_map(body, mesh=grid, in_specs=in_specs, out_specs=out_specs, check_vma=False)
```

```python
import functools

import jax
import jax.numpy as jnp
import numpy as np
from jax import lax
from jax.experimental import pallas as pl
from jax.experimental.pallas import tpu as pltpu
from jax.sharding import Mesh, PartitionSpec as P

HEADS = 17
HDIM = 64
D = HEADS * HDIM
FF = 4 * D
SHARD = 17
NDP = 64
MAIN = 16 * NDP
PAD = 1152
ROWS = 128
PAIRS = PAD // 128

UP, DOWN, QKV, OUT, BLOCKS = 0, 4, 8, 11, 12
TAIL0 = BLOCKS * PAD
TAILW = 896
WIDTH = TAIL0 + TAILW
SMALLS = 256

NORM_EPSILON = 1e-05
SCORE_SCALE = 0.125
GELU_C = float(np.sqrt(2 / np.pi))
GELU_A = 0.044715
BF = jnp.bfloat16
F32 = jnp.float32
WINDOW = {"fwd": 4, "both": 4, "bwd": 2}
VMEM_BYTES = 58 * 1024 * 1024


def constants():
    n = np.arange(D)
    shard_of = np.where(n < MAIN, n // 16, n - MAIN)
    row_of = np.where(n < MAIN, n % 16, 16)
    order = np.zeros((PAD, D), np.float32)
    order[shard_of * SHARD + row_of, n] = 1
    f = np.arange(D)
    s, a, r = f // 68, (f % 68) // SHARD, f % SHARD
    hid = np.zeros((D, D), np.float32)
    hid[f, np.where(r < 16, a * 256 + s * 16 + r, 1024 + a * 16 + s)] = 1
    k = np.arange(SMALLS)
    is_vec, is_up = k < 136, (k >= 136) & (k < 204)
    k_row = np.where(is_vec, k // 8, np.where(is_up, (k - 136) % SHARD, -1))
    k_out = np.where(is_vec, k % 8, np.where(is_up, 8 + (k - 136) // SHARD, -1))
    pick = (k_out[None, :] == np.arange(16)[:, None]).astype(np.float32)
    spread = (np.arange(NDP)[:, None] == shard_of[None, :]).astype(np.float32)
    keep = (k_row[:, None] == row_of[None, :]).astype(np.float32)
    nat = np.arange(PAD)
    spread_nat = (np.arange(NDP)[:, None] == nat[None, :] // SHARD).astype(np.float32)
    keep_nat = (k_row[:, None] == nat[None, :] % SHARD).astype(np.float32)
    m = np.arange(MAIN)
    turn = np.zeros((MAIN, MAIN), np.float32)
    turn[(m % 16) * NDP + m // 16, m] = 1
    names = ("order", "hid", "pick", "spread", "keep", "spread_nat", "keep_nat", "turn")
    values = (order, hid, pick, spread, keep, spread_nat, keep_nat, turn)
    found = {name: jnp.asarray(value, BF) for name, value in zip(names, values)}
    found["order_d"] = jnp.asarray(order[:D], BF)
    found["hid_t"] = jnp.asarray(hid.T, BF)
    return found


def matmul(a, b):
    return jnp.dot(a, b, preferred_element_type=F32)


def dot_t(a, b):
    return lax.dot_general(a, b, (((1,), (1,)), ((), ())), preferred_element_type=F32)


def t_dot(a, b):
    return lax.dot_general(a, b, (((0,), (0,)), ((), ())), preferred_element_type=F32)


def norm_parts(features):
    centred = features - jnp.mean(features, axis=-1, keepdims=True)
    inverse = lax.rsqrt(jnp.mean(centred * centred, axis=-1, keepdims=True) + NORM_EPSILON)
    return centred * inverse, inverse


def norm_back(gradient, normed, inverse, gain):
    scaled = gradient * gain
    centred = scaled - jnp.mean(scaled, axis=-1, keepdims=True)
    return inverse * (centred - normed * jnp.mean(scaled * normed, axis=-1, keepdims=True))


def col_sum(v):
    return jnp.sum(v, axis=0, keepdims=True)


def unpack_kernel(whole, *refs):
    given, (tails, vecs, nat), (raw, table, *held), sems = refs[:6], refs[6:9], refs[9:17], refs[17]
    copies = [pltpu.make_async_copy(whole.at[:, pl.ds(TAIL0, TAILW)], raw, sems.at[0])]
    for i, (source, target) in enumerate(zip(given, held)):
        copies.append(pltpu.make_async_copy(source, target, sems.at[1 + i]))
    for copy in copies:
        copy.start()
    turn, pick, spread, keep, spread_nat, keep_nat = held
    copies[0].wait()
    copies[1].wait()
    turned = matmul(turn[...], raw[...]).astype(BF)
    for j in range(16):
        table[:, j * TAILW : (j + 1) * TAILW] = turned[j * NDP : (j + 1) * NDP]
    out = pltpu.make_async_copy(table, tails, sems.at[7])
    out.start()
    for copy in copies[2:]:
        copy.wait()
    small = table[:, TAIL0 : TAIL0 + SMALLS]
    for result, s, k in ((vecs, spread, keep), (nat, spread_nat, keep_nat)):
        wide_rows = t_dot(small, s[...]) * k[...].astype(F32)
        result[...] = matmul(pick[...], wide_rows.astype(BF))
    out.wait()


def unpack(whole, c):
    vm = pl.BlockSpec(memory_space=pltpu.VMEM)
    hbm = pl.BlockSpec(memory_space=pl.ANY)
    consts = [c[k] for k in ("turn", "pick", "spread", "keep", "spread_nat", "keep_nat")]
    table = (NDP, 16 * TAILW)
    return pl.pallas_call(
        unpack_kernel,
        in_specs=[hbm] * 7,
        out_specs=[hbm, vm, vm],
        out_shape=[
            jax.ShapeDtypeStruct(table, BF),
            jax.ShapeDtypeStruct((16, D), F32),
            jax.ShapeDtypeStruct((16, PAD), F32),
        ],
        scratch_shapes=[pltpu.VMEM((MAIN, TAILW), BF), pltpu.VMEM(table, BF)]
        + [pltpu.VMEM(v.shape, BF) for v in consts]
        + [pltpu.SemaphoreType.DMA((8,))],
        compiler_params=pltpu.CompilerParams(vmem_limit_bytes=VMEM_BYTES),
        name="unpack",
    )(whole, *consts)


class Weights:
    def __init__(self, whole, tails, buf, sems, kind):
        self.whole, self.tails, self.buf, self.sems, self.kind = whole, tails, buf, sems, kind
        self.window = WINDOW[kind]

    def block(self, p):
        if self.kind == "bwd":
            pair = (p % 2 == 0) * DOWN + p // 2
            rest = OUT * (p == 8) + (p - 1) * (p > 8)
            return pair * (p < 8) + rest * (p >= 8)
        q = p - 4
        return (p < 4) * (QKV + p) + (p >= 4) * ((q % 2) * DOWN + q // 2)

    def copies(self, p):
        b = self.block(p)
        cols = pl.ds(pl.multiple_of(b * PAD, 128), PAD)
        return (
            pltpu.make_async_copy(
                self.whole.at[:, cols], self.buf.at[b, pl.ds(0, MAIN)], self.sems.at[b, 0]
            ),
            pltpu.make_async_copy(
                self.tails.at[:, cols], self.buf.at[b, pl.ds(MAIN, NDP)], self.sems.at[b, 1]
            ),
        )

    def start(self, p):
        for copy in self.copies(p):
            copy.start()

    def begin(self):
        for p in range(self.window):
            self.start(p)

    def wait(self, p):
        for copy in self.copies(p):
            copy.wait()
        if isinstance(p, int):
            if p + self.window < BLOCKS:
                self.start(p + self.window)
        else:

            @pl.when(p + self.window < BLOCKS)
            def _():
                self.start(p + self.window)


def pair_masks():
    lane = lax.broadcasted_iota(jnp.int32, (ROWS, 128), 1)
    first = (lane < HDIM).astype(F32)
    return first, 1.0 - first


def stacked(v, masks):
    return jnp.concatenate([(v * m).astype(BF) for m in masks], axis=0)


def soft_pair(q, kk, allowed):
    scores = dot_t(q, kk) * SCORE_SCALE
    halves = []
    for h in range(2):
        s = jnp.where(allowed, scores[:, h * ROWS : (h + 1) * ROWS], -1e30)
        e = jnp.exp(s - jnp.max(s, axis=-1, keepdims=True))
        halves.append(e / jnp.sum(e, axis=-1, keepdims=True))
    return halves


def forward_part(w, send, x_ref, place, pairs_ref, vecs, nat, order, r):
    x = x_ref[...].astype(F32)
    normed, _ = norm_parts(x)
    r["attn_in"][0, :, :D] = (normed * vecs[0:1] + vecs[1:2]).astype(BF)

    def project(i, carry):
        w.wait(i)
        shift = jnp.where(i == 0, nat[2:3], jnp.where(i == 2, nat[3:4], 0.0))
        r["packed"][i] = (matmul(r["attn_in"][0, :, :D], w.buf[QKV + i]) + shift).astype(BF)
        return carry

    lax.fori_loop(0, 3, project, 0)
    send("packed")
    masks = pair_masks()
    allowed = pairs_ref[...] > 0
    for p in range(PAIRS):
        cols = pl.ds(p * 128, 128)
        kk = stacked(r["packed"][1, :, cols].astype(F32), masks)
        vv = stacked(r["packed"][2, :, cols].astype(F32), masks)
        halves = soft_pair(r["packed"][0, :, cols], kk, allowed)
        soft = jnp.concatenate([h.astype(BF) for h in halves], axis=1)
        r["heads"][:, cols] = matmul(soft, vv).astype(BF)
    order.wait()
    mixed = matmul(r["heads"][...], order.ref[...]).astype(BF)
    r["attn_in"][1, :, :D] = mixed
    w.wait(3)
    branch = matmul(mixed, w.buf[OUT])[:, :D]
    middle = x + branch + vecs[4:5]
    r["middle"][...] = middle
    send("middle")
    normed, _ = norm_parts(middle)
    r["second"][:, :D] = (normed * vecs[5:6] + vecs[6:7]).astype(BF)
    r["acc"][...] = jnp.zeros((ROWS, PAD), F32)

    def feed(a, carry):
        w.wait(4 + 2 * a)
        hidden = matmul(r["second"][:, :D], w.buf[UP + a])[:, :D] + vecs[pl.ds(8 + a, 1)]
        r["hidden"][a] = hidden
        bent = jnp.tanh(GELU_C * (hidden + GELU_A * (hidden * hidden * hidden)))
        r["active"][a, :, :D] = (0.5 * hidden * (1.0 + bent)).astype(BF)
        w.wait(5 + 2 * a)
        r["acc"][...] += matmul(r["active"][a, :, :D], w.buf[DOWN + a])
        return carry

    lax.fori_loop(0, 4, feed, 0)
    r["result"][...] = (r["middle"][...] + r["acc"][:, :D] + vecs[7:8]).astype(BF)
    send("hidden")
    send("early")


def backward_part(w, wait, send, grad_ref, x_ref, place, pairs_ref, vecs, order, r):
    grad = grad_ref[...]
    dres = grad.astype(F32)
    r["acc"][...] = jnp.zeros((ROWS, PAD), F32)

    def feed(a, carry):
        if wait:
            w.wait(2 * a)
        dactive = dot_t(grad_ref[...], w.buf[DOWN + a, :, :D])
        h = r["hidden"][a]
        square = h * h
        bent = jnp.tanh(GELU_C * (h + GELU_A * (square * h)))
        slope = 0.5 * (1.0 + bent) + (0.5 * GELU_C) * h * (1.0 - bent * bent) * (
            1.0 + (3 * GELU_A) * square
        )
        dhidden = (dactive * slope).astype(BF)
        r["dhidden"][a, :, :D] = dhidden
        r["small"][pl.ds(8 + a, 1)] = col_sum(dhidden.astype(F32))
        if wait:
            w.wait(2 * a + 1)
        r["acc"][:, :D] += dot_t(dhidden, w.buf[UP + a, :, :D])
        return carry

    lax.fori_loop(0, 4, feed, 0)
    send("late_first")
    dsecond = r["acc"][:, :D]
    normed, inverse = norm_parts(r["middle"][...])
    r["small"][5:6] = col_sum(dsecond * normed)
    r["small"][6:7] = col_sum(dsecond)
    r["small"][7:8] = col_sum(dres)
    dmiddle = dres + norm_back(dsecond, normed, inverse, vecs[5:6])
    r["middle"][...] = dmiddle
    dattn = dmiddle.astype(BF)
    r["dpacked"][3, :, :D] = dattn
    r["small"][4:5] = col_sum(dattn.astype(F32))
    if wait:
        w.wait(8)
    dmixed = dot_t(dattn, w.buf[OUT, :, :D]).astype(BF)
    if wait:
        order.wait()
    r["heads"][...] = dot_t(dmixed, order.ref[...]).astype(BF)
    masks = pair_masks()
    allowed = pairs_ref[...] > 0
    for p in range(PAIRS):
        cols = pl.ds(p * 128, 128)
        width = min(D - p * 128, 128)
        live = pl.ds(p * 128, width)
        q = r["packed"][0, :, cols]
        kk = stacked(r["packed"][1, :, cols].astype(F32), masks)
        vv = stacked(r["packed"][2, :, cols].astype(F32), masks)
        dm = r["heads"][:, cols]
        halves = soft_pair(q, kk, allowed)
        dsoft = dot_t(dm, vv)
        dscores = []
        for h, p_half in enumerate(halves):
            d_half = dsoft[:, h * ROWS : (h + 1) * ROWS]
            centre = jnp.sum(d_half * p_half, axis=-1, keepdims=True)
            dscores.append((p_half * (d_half - centre)).astype(BF))
        ds = jnp.concatenate(dscores, axis=1)
        soft = jnp.concatenate([h.astype(BF) for h in halves], axis=1)
        dq = matmul(ds, kk) * SCORE_SCALE
        dk = t_dot(ds, q) * SCORE_SCALE
        dv = t_dot(soft, dm)
        dk = dk[:ROWS] * masks[0] + dk[ROWS:] * masks[1]
        dv = dv[:ROWS] * masks[0] + dv[ROWS:] * masks[1]
        for i, v in enumerate((dq, dk, dv)):
            r["dpacked"][i, :, live] = v[:, :width].astype(BF)
    send("late_second")
    sums = [col_sum(r["dpacked"][i, :, :D].astype(F32)) for i in (0, 2)]
    sums = jnp.concatenate(sums + [jnp.zeros((14, D), F32)], axis=0).astype(BF)
    r["small"][2:4] = matmul(sums, order.ref[:D])[:2]
    r["acc"][...] = jnp.zeros((ROWS, PAD), F32)

    def project(i, carry):
        if wait:
            w.wait(9 + i)
        r["acc"][:, :D] += dot_t(r["dpacked"][i, :, :D], w.buf[QKV + i, :, :D])
        return carry

    lax.fori_loop(0, 3, project, 0)
    dentry = r["acc"][:, :D]
    normed, inverse = norm_parts(x_ref[...].astype(F32))
    r["small"][0:1] = col_sum(dentry * normed)
    r["small"][1:2] = col_sum(dentry)
    r["small"][12:16] = jnp.zeros((4, D), F32)
    r["dx"][...] = (r["middle"][...] + norm_back(dentry, normed, inverse, vecs[0:1])).astype(BF)


ROW = (ROWS, D)
WIDEROW = (ROWS, PAD)
KEPT = {
    "packed": ((3,) + WIDEROW, BF),
    "middle": (ROW, F32),
    "hidden": ((4,) + ROW, F32),
}
EARLY = {f"early{d}": ((3,) + WIDEROW, BF) for d in range(4)}
LATE = {f"late{d}": ((2,) + WIDEROW, BF) for d in range(4)}
RESULT = {"result": (ROW, BF)}
GRADS = {"dx": (ROW, BF), "small": ((16, D), F32)}
FWD_WORK = {
    "attn_in": ((2,) + WIDEROW, BF),
    "second": (WIDEROW, BF),
    "active": ((4,) + WIDEROW, BF),
}
BWD_WORK = {
    "dhidden": ((4,) + WIDEROW, BF),
    "dpacked": ((4,) + WIDEROW, BF),
}
WORK = {"heads": (WIDEROW, BF), "acc": (WIDEROW, F32)}


class Fetched:
    def __init__(self, source, ref, sem):
        self.ref, self.copy = ref, pltpu.make_async_copy(source, ref, sem)

    def start(self):
        self.copy.start()

    def wait(self):
        self.copy.wait()


def layer_call(kind, whole, tails, vecs, nat, pairs, order, place, x, grad=None, old=None):
    near_out = {"fwd": RESULT, "both": {**RESULT, **GRADS}, "bwd": GRADS}[kind]
    far_out = {"fwd": {**EARLY, **KEPT}, "both": {**EARLY, **LATE}, "bwd": LATE}[kind]
    outs = {**near_out, **far_out}
    work = {**WORK, **KEPT}
    if kind != "bwd":
        work.update(FWD_WORK)
    if kind != "fwd":
        work.update(BWD_WORK)
    passed = {"fwd": {}, "both": {**RESULT, **EARLY}, "bwd": {**GRADS, **LATE}}[kind]
    loaded = KEPT if kind == "bwd" else {}
    far = [whole, tails, order] + [old[k] for k in (*passed, *loaded)]
    near = [vecs, nat, pairs, x] + ([] if grad is None else [grad])
    section = 1 if kind == "both" else 0

    def kernel(place_ref, *refs):
        far_refs, refs = refs[: len(far)], refs[len(far) :]
        near_refs, refs = refs[: len(near)], refs[len(near) :]
        out = dict(zip(outs, refs))
        refs = refs[len(outs) :]
        r = {**dict(zip(work, refs)), **{k: out[k] for k in near_out}}
        buf, order_buf, sems, old_sems, order_sem, out_sems = refs[len(work) :]
        w = Weights(far_refs[0], far_refs[1], buf, sems, kind)
        order_in = Fetched(far_refs[2], order_buf, order_sem)
        vecs_ref, nat_ref, pairs_ref, x_ref = near_refs[:4]
        old_refs = dict(zip((*passed, *loaded), far_refs[3:]))
        sent = []

        def send(name):
            if name in KEPT:
                moves = [(r[name], out[name])] if name in out else []
            else:
                moves = []
                for d in range(4):
                    z = lax.rem(place_ref[2] + d, 4)
                    if name == "early":
                        sources = (r["second"], r["active"].at[z], r["attn_in"].at[z // 3])
                        moves += [(v, out[f"early{d}"].at[i]) for i, v in enumerate(sources)]
                    elif name == "late_first":
                        moves.append((r["dhidden"].at[z], out[f"late{d}"].at[0]))
                    else:
                        moves.append((r["dpacked"].at[z], out[f"late{d}"].at[1]))
            for source, target in moves:
                copy = pltpu.make_async_copy(source, target, out_sems.at[len(sent)])
                copy.start()
                sent.append(copy)

        @pl.when(place_ref[3] == section)
        def _():
            fetched = [
                Fetched(old_refs[k], r[k], old_sems.at[i]) for i, k in enumerate(loaded)
            ]
            for copy in fetched:
                copy.start()
            w.begin()
            order_in.start()
            if kind != "bwd":
                forward_part(
                    w, send, x_ref, place_ref, pairs_ref, vecs_ref, nat_ref, order_in, r
                )
            for copy in fetched:
                copy.wait()
            if kind != "fwd":
                backward_part(
                    w,
                    kind == "bwd",
                    send,
                    near_refs[4],
                    x_ref,
                    place_ref,
                    pairs_ref,
                    vecs_ref,
                    order_in,
                    r,
                )
            for copy in sent:
                copy.wait()

        if passed:

            @pl.when(place_ref[3] != section)
            def _():
                into, back = [], []
                for i, k in enumerate(passed):
                    if k in near_out:
                        into.append(pltpu.make_async_copy(old_refs[k], out[k], old_sems.at[i]))
                        continue
                    for j in range(passed[k][0][0]):
                        held = buf.at[i, pl.ds(j * ROWS, ROWS)]
                        n = len(back)
                        into.append(
                            pltpu.make_async_copy(old_refs[k].at[j], held, out_sems.at[n])
                        )
                        back.append(
                            pltpu.make_async_copy(held, out[k].at[j], out_sems.at[16 + n])
                        )
                for copies in (into, back):
                    for copy in copies:
                        copy.start()
                    for copy in copies:
                        copy.wait()

    vm = pl.BlockSpec(memory_space=pltpu.VMEM)
    hbm = pl.BlockSpec(memory_space=pl.ANY)
    results = pl.pallas_call(
        kernel,
        in_specs=[pl.BlockSpec(memory_space=pltpu.SMEM)] + [hbm] * len(far) + [vm] * len(near),
        out_specs=[vm] * len(near_out) + [hbm] * len(far_out),
        out_shape=[jax.ShapeDtypeStruct(s, t) for s, t in outs.values()],
        scratch_shapes=[pltpu.VMEM(s, t) for s, t in work.values()]
        + [
            pltpu.VMEM((BLOCKS, D, PAD), BF),
            pltpu.VMEM((PAD, D), BF),
            pltpu.SemaphoreType.DMA((BLOCKS, 2)),
            pltpu.SemaphoreType.DMA((8,)),
            pltpu.SemaphoreType.DMA,
            pltpu.SemaphoreType.DMA((32,)),
        ],
        compiler_params=pltpu.CompilerParams(vmem_limit_bytes=VMEM_BYTES),
        cost_estimate=pl.CostEstimate(
            flops={"fwd": 4, "both": 12, "bwd": 8}[kind] * 10**9,
            bytes_accessed=BLOCKS * D * PAD * 2,
            transcendentals=10**6,
        ),
        name="layer_" + kind,
    )(place, *far, *near)
    return dict(zip(outs, results))


CHUNK = 72
PART = 384
WIDE = (PAD + PART, PAD + PAD - PART)


def block(width):
    return ((4, CHUNK, width), BF)


def local_call(kernel, name, place, ins, out_shapes, scratch=(), far=(), far_out=False):
    vm = pl.BlockSpec(memory_space=pltpu.VMEM)
    hbm = pl.BlockSpec(memory_space=pl.ANY)
    return pl.pallas_call(
        kernel,
        in_specs=[pl.BlockSpec(memory_space=pltpu.SMEM)] + [hbm] * len(far) + [vm] * len(ins),
        out_specs=[hbm if far_out else vm] * len(out_shapes),
        out_shape=[jax.ShapeDtypeStruct(s, t) for s, t in out_shapes],
        scratch_shapes=list(scratch),
        compiler_params=pltpu.CompilerParams(vmem_limit_bytes=VMEM_BYTES),
        name=name,
    )(place, *far, *ins)


def product(a, b, store):
    last = t_dot(a[:, MAIN:], b)
    nothing = jnp.zeros((4, PAD), F32)
    for x in range(4):
        main = t_dot(a[:, x * 256 : (x + 1) * 256], b)
        for y in range(4):
            at = (x * 4 + y) * 4
            rows = [main[y * 64 : (y + 1) * 64], last[at : at + 4], nothing]
            store(x, y, jnp.concatenate(rows, axis=0).astype(BF))


def send_blocks(held, first, outs, sems):
    copies = []
    for d in range(4):
        source = held.at[lax.rem(first + d, 4)]
        copies.append(pltpu.make_async_copy(source, outs[d], sems.at[d]))
        copies[-1].start()
    return copies


def load(sources, held, sems, other=None, use_other=None):
    copies = []
    for d in range(4):
        copies.append(pltpu.make_async_copy(sources[d], held.at[d], sems.at[d]))
        if other is None:
            copies[d].start()
            continue
        pl.when(jnp.logical_not(use_other))(copies[d].start)
        pl.when(use_other)(pltpu.make_async_copy(other[d], held.at[d], sems.at[d]).start)

    def rows():
        for copy in copies:
            copy.wait()
        return jnp.concatenate([held[d, :, :D] for d in range(4)], axis=0)

    return rows


def wide(v):
    return jnp.concatenate([v, jnp.zeros((v.shape[0], PAD - D), v.dtype)], axis=1)


def down_products_kernel(place, *refs):
    early, branch, cots, outs = refs[:4], refs[4:8], refs[8:12], refs[12:16]
    held, a_held, b_held, sems = refs[16:]
    a = load([e.at[1] for e in early], a_held, sems.at[0])
    b = load(branch, b_held, sems.at[1], cots, place[3] == 1)

    def store(x, y, v):
        held[y, x] = v

    product(a(), wide(b()), store)
    for copy in send_blocks(held, place[1], outs, sems.at[2]):
        copy.wait()


def up_products_kernel(place, *refs):
    early, late, outs = refs[:4], refs[4:8], refs[8:12]
    held, a_held, b_held, sems = refs[12:]
    a = load([e.at[0] for e in early], a_held, sems.at[0])
    b = load([v.at[0] for v in late], b_held, sems.at[1])

    def store(x, y, v):
        held[x, y] = v

    product(a(), wide(b()), store)
    for copy in send_blocks(held, place[0], outs, sems.at[2]):
        copy.wait()


def attn_products_kernel(place, *refs):
    early, late, small, outs = refs[:4], refs[4:8], refs[8], refs[9:17]
    first, second, a_held, b_held, sems = refs[17:]
    a = load([e.at[2] for e in early], a_held, sems.at[0])
    b = load([v.at[1] for v in late], b_held, sems.at[1])
    slot = lax.broadcasted_iota(jnp.int32, (16, PAD), 1) - D
    unit = (slot == lax.broadcasted_iota(jnp.int32, (16, PAD), 0)).astype(F32).astype(BF)

    def store(x, y, v):
        first[x, y] = v[:, :PART]
        second[y, x] = v[:, PART:]

    a = jnp.concatenate([a(), small[...].astype(BF)], axis=0)
    b = jnp.concatenate([wide(b()), unit], axis=0)
    product(a, b, store)
    copies = send_blocks(first, place[0], outs[:4], sems.at[2])
    copies += send_blocks(second, place[1], outs[4:], sems.at[3])
    for copy in copies:
        copy.wait()


def total(parts):
    return sum((p.astype(F32) for p in parts[1:]), parts[0].astype(F32))


def first_sum_kernel(place, *refs):
    given, outs, held, sems = refs[:16], refs[16:24], refs[24:28], refs[28]
    copies = {}
    for d in range(4):
        for g, other in ((1, 0), (0, 1), (3, 0), (2, 1)):
            i = lax.rem(place[other] + d, 4)
            copies[g, d] = [
                pltpu.make_async_copy(given[4 * g + k].at[i], held[g].at[d, k], sems.at[g, d, k])
                for k in range(4)
            ]
            for copy in copies[g, d]:
                copy.start()
    for d in range(4):
        for g, h, start in ((1, 1, 0), (0, 0, 0), (3, 1, PAD), (2, 0, PAD)):
            for copy in copies[g, d]:
                copy.wait()
            summed = total([held[g][d, k] for k in range(4)]).astype(BF)
            outs[4 * h + d][:, start : start + summed.shape[1]] = summed


def second_sum_kernel(place, *refs):
    outs, held = refs[8:12], refs[12]
    for h in range(2):
        full = total([p[...] for p in refs[4 * h : 4 * h + 4]])
        start = h * WIDE[0]
        empty = jnp.zeros((7, WIDE[h]), F32)
        for z in range(4):
            rows = [full[z * 16 : (z + 1) * 16], full[64 + z : 65 + z], empty]
            held[z, :, start : start + WIDE[h]] = jnp.concatenate(rows, axis=0).astype(BF)
    for d in range(4):
        outs[d][...] = held[lax.rem(place[2] + d, 4)]


def final_kernel(place, *refs):
    hid_in, order_in, parts, outs = refs[0], refs[1], refs[2:6], refs[6:11]
    held, hid, order, sems = refs[11:]
    g_up, g_down, g_out, g_qkv, sums = outs
    hid_copy = pltpu.make_async_copy(hid_in, hid, sems.at[0])
    order_copy = pltpu.make_async_copy(order_in, order, sems.at[1])
    hid_copy.start()
    order_copy.start()
    for d in range(4):
        held[lax.rem(place[2] + 4 - d, 4)] = parts[d][...]
    up = []
    for j in range(4):
        pieces = [held[a, :, j * 256 : (j + 1) * 256] for a in range(4)]
        pieces += [held[a, :, MAIN + j * 16 : MAIN + (j + 1) * 16] for a in range(4)]
        up.append(jnp.concatenate(pieces, axis=1))
    hid_copy.wait()
    up = matmul(jnp.concatenate(up, axis=0), hid[...])
    up = jnp.concatenate([up[j * 24 : (j + 1) * 24] for j in range(4)], axis=1)
    for i in range(SHARD):
        g_up[i] = up[i : i + 1]
    start = WIDE[0]
    attn = [
        jnp.concatenate([held[a, :, PAD:start], held[a, :, start + PAD :]], axis=1)
        for a in range(4)
    ]
    rows = [held[a, :, start : start + D] for a in range(4)] + [attn[3][:, :D]]
    order_copy.wait()
    rows = dot_t(jnp.concatenate(rows, axis=0), order[:D])
    qkv = jnp.concatenate([v[:, :D].astype(F32) for v in attn[:3]], axis=1)
    for i in range(SHARD):
        for a in range(4):
            g_down[a * SHARD + i] = rows[a * 24 + i : a * 24 + i + 1]
        g_out[i] = rows[96 + i : 97 + i]
        g_qkv[i] = qkv[i : i + 1]
    sums[...] = total([v[:SHARD, D:] for v in attn])


def ring(v, axis, d):
    return lax.ppermute(v, axis, [(i, (i + d) % 4) for i in range(4)])


def restore_kernel(place, order, result, dx, acts, grads):
    acts[...] = dot_t(result[...], order[:D]).astype(BF)
    grads[...] = dot_t(dx[...], order[:D]).astype(BF)


def pad_cols(v, width):
    return jnp.pad(v, ((0, 0), (0, width - v.shape[1])))


def body(inputs, cotangent, lengths, vectors, qkv_w, out_w, up_w, up_b, down_w):
    section = lax.axis_index("section")
    mb, rows, _ = inputs.shape
    n = mb * rows
    c = constants()
    order = c["order"]

    outdown = matmul(jnp.concatenate([out_w[0], down_w[0]], axis=0), c["order_d"]).astype(BF)
    hid = matmul(up_w[0].reshape(SHARD * 4, D), c["hid"]).astype(BF).reshape(SHARD, 4, D)
    hid_main = hid[:, :, :MAIN].reshape(SHARD, 4, 4, 256).transpose(0, 2, 1, 3)
    hid_last = hid[:, :, MAIN:].reshape(SHARD, 4, 4, 16).transpose(0, 2, 1, 3)
    hid = jnp.concatenate(
        [
            hid_main.reshape(SHARD, 4, MAIN),
            hid_last.reshape(SHARD, 4, NDP),
            jnp.zeros((SHARD, 4, PAD - D), BF),
        ],
        axis=2,
    )
    shard = [hid.reshape(SHARD, 4 * PAD)]
    shard += [pad_cols(outdown[SHARD * (1 + a) : SHARD * (2 + a)], PAD) for a in range(4)]
    shard += [pad_cols(qkv_w[0][:, i * D : (i + 1) * D], PAD) for i in range(3)]
    shard += [pad_cols(outdown[:SHARD], PAD)]
    shard = jnp.concatenate(shard, axis=1)
    tail = jnp.concatenate([shard[16], vectors[0].reshape(-1), up_b[0]])
    tail = jnp.pad(tail, (0, 16 * TAILW - tail.shape[0])).reshape(16, TAILW)
    sent = jnp.concatenate([shard[:16], tail], axis=1)
    whole = lax.all_gather(sent, ("x", "y", "z"), axis=0, tiled=True)
    order_d = c["order_d"]
    cot = matmul(cotangent.reshape(n, D), order_d).astype(BF)
    cots = [cot] + [ring(cot, "z", d) for d in (1, 3, 2)]
    whole, cots = lax.optimization_barrier((whole, cots))
    tails, vecs, nat = unpack(whole, c)

    ends = jnp.cumsum(lengths[:, 0], axis=1)
    place = jnp.arange(rows, dtype=jnp.int32)
    seg = jnp.sum((place[None, :, None] >= ends[:, None, :]).astype(jnp.int32), axis=2)
    seg = (seg + 8 * jnp.arange(mb, dtype=jnp.int32)[:, None]).reshape(n)
    at = jnp.arange(n, dtype=jnp.int32)
    pairs = ((seg[:, None] == seg[None, :]) & (at[:, None] >= at[None, :])).astype(F32)

    x0 = matmul(inputs.reshape(n, D), order_d).astype(BF)
    place = jnp.stack([lax.axis_index("x"), lax.axis_index("y"), lax.axis_index("z"), section])
    call = functools.partial(
        layer_call,
        whole=whole,
        tails=tails,
        vecs=vecs,
        nat=nat,
        pairs=pairs,
        order=order,
        place=place,
    )

    first = call("fwd", x=x0)
    arrived = lax.ppermute(first["result"], "section", [(0, 1)])
    top = call("both", x=arrived, grad=cot, old=first)
    coming = lax.ppermute(top["dx"], "section", [(1, 0)])
    early = [top["early0"]] + [ring(top[f"early{d}"], "z", d) for d in (1, 3, 2)]
    branches = [coming] + [ring(coming, "z", d) for d in (1, 3)]
    early[1], held = lax.optimization_barrier((early[1], coming))
    branches.append(ring(held, "z", 2))
    kept = {k: first[k] for k in KEPT}
    old = {**{k: top[k] for k in (*GRADS, *LATE)}, **kept}
    bwd = call("bwd", x=x0, grad=coming, old=old)
    sends = [bwd[f"late{d}"] for d in (1, 3, 2)]
    early, branches, sends = lax.optimization_barrier((early, branches, sends))
    late = [bwd["late0"]] + [ring(v, "z", d) for v, d in zip(sends, (1, 3, 2))]

    vmem, sem = pltpu.VMEM, pltpu.SemaphoreType.DMA
    down = local_call(
        down_products_kernel,
        "down_products",
        place,
        [],
        [block(PAD)] * 4,
        [vmem((4, 4, CHUNK, PAD), BF), vmem((4,) + WIDEROW, BF), vmem((4,) + ROW, BF), sem((3, 4))],
        far=[*early, *branches, *cots],
        far_out=True,
    )
    late[1], late[2], down = lax.optimization_barrier((late[1], late[2], down))
    down = [down[0]] + [ring(down[d], "y", d) for d in (2, 1, 3)]
    up = local_call(
        up_products_kernel,
        "up_products",
        place,
        [],
        [block(PAD)] * 4,
        [vmem((4, 4, CHUNK, PAD), BF)] + [vmem((4,) + WIDEROW, BF)] * 2 + [sem((3, 4))],
        far=[*early, *late],
        far_out=True,
    )
    up = [up[0]] + [ring(up[d], "x", d) for d in (2, 1, 3)]
    out = local_call(
        attn_products_kernel,
        "attn_products",
        place,
        [bwd["small"]],
        [block(PART)] * 4 + [block(PAD - PART)] * 4,
        [vmem((4, 4, CHUNK, width), BF) for width in (PART, PAD - PART)]
        + [vmem((4,) + WIDEROW, BF)] * 2
        + [sem((4, 4))],
        far=[*early, *late],
        far_out=True,
    )
    xs, ys = list(out[:4]), list(out[4:])
    up[1], *xs = lax.optimization_barrier((up[1], *xs))
    down[1], ys = lax.optimization_barrier((down[1], ys))
    acts, grads = local_call(
        restore_kernel, "restore", place, [order, top["result"], bwd["dx"]], [(ROW, BF)] * 2
    )
    attn_x = [xs[0]] + [ring(xs[d], "x", d) for d in (2, 1, 3)]
    attn_y = [ys[0]] + [ring(ys[d], "y", d) for d in (2, 1, 3)]
    acts, grads, attn_y[3] = lax.optimization_barrier((acts, grads, attn_y[3]))
    out = local_call(
        first_sum_kernel,
        "first_sum",
        place,
        [],
        [((CHUNK, WIDE[h]), BF) for h in (0, 1) for _ in range(4)],
        [vmem((4, 4, CHUNK, width), BF) for width in (PAD, PAD, PART, PAD - PART)]
        + [sem((4, 4, 4))],
        far=[*up, *down, *attn_x, *attn_y],
    )
    got = []
    for h, axis in ((0, "y"), (1, "x")):
        got += [out[4 * h]] + [ring(out[4 * h + d], axis, d) for d in (1, 3, 2)]
    out = local_call(
        second_sum_kernel,
        "second_sum",
        place,
        got,
        [((24, sum(WIDE)), BF)] * 4,
        [vmem((4, 24, sum(WIDE)), BF)],
    )
    got = [out[0]] + [ring(out[d], "z", d) for d in (1, 2, 3)]
    g_up, g_down, g_out, g_qkv, sums = local_call(
        final_kernel,
        "owners",
        place,
        got,
        [
            ((SHARD, 1, FF), F32),
            ((4 * SHARD, 1, D), F32),
            ((SHARD, 1, D), F32),
            ((SHARD, 1, 3 * D), F32),
            ((SHARD, PAD - D), F32),
        ],
        [
            vmem((4, 24, sum(WIDE)), BF),
            vmem((D, D), BF),
            vmem((PAD, D), BF),
            pltpu.SemaphoreType.DMA((2,)),
        ],
        far=[c["hid_t"], order],
    )
    return (
        acts.reshape(1, mb, rows, D),
        grads.reshape(1, mb, rows, D),
        sums[None, :, :8],
        g_qkv.reshape(1, SHARD, 3 * D),
        g_out.reshape(1, SHARD, D),
        g_up.reshape(1, SHARD, FF),
        sums[:, 8:12].T.reshape(1, 4 * SHARD),
        g_down.reshape(1, 4 * SHARD, D),
    )


def solution(mesh):
    grid = Mesh(mesh.devices.reshape(2, 4, 4, 4), ("section", "x", "y", "z"))
    dp = ("x", "y", "z")
    tokens = P(None, dp, None)
    rows = P("section", dp, None)
    in_specs = (tokens, tokens, tokens, rows, rows, rows, rows, P("section", dp), rows)
    stacks = P("section", None, dp, None)
    out_specs = (stacks, stacks, rows, rows, rows, rows, P("section", dp), rows)
    return jax.shard_map(body, mesh=grid, in_specs=in_specs, out_specs=out_specs, check_vma=False)
```
